32 devices in a mesh: seed: 4 (over z), dp: 8 (over y, x, core).
Axes of the slice: x: 2, y: 2, z: 4, core: 2. Of those that a mesh axis runs over, the one named last changes fastest.
Arguments:
- states: float32 [4, 17, 32768], P('seed', None, 'dp'), may hold values from -6 to 6
- actions: float32 [4, 6, 32768], P('seed', None, 'dp'), may hold values from -0.95 to 0.95
- rewards: float32 [4, 32768], P('seed', 'dp'), may hold values from -24 to 24
- next_states: float32 [4, 17, 32768], P('seed', None, 'dp'), may hold values from -6 to 6
- dones: int32 [4, 32768], P('seed', 'dp'), may hold values 0 or 1
- noise_now: float32 [4, 6, 32768], P('seed', None, 'dp'), may hold values from -4 to 4
- noise_next: float32 [4, 6, 32768], P('seed', None, 'dp'), may hold values from -4 to 4
- probs: float32 [4, 32768], P('seed', 'dp'), may hold values from 1e-06 to 4.8e-05
- valid_counts: int32 [4, 8], P('seed', 'dp'), may hold values from 1 to 4096, as said below
- owners: int32 [4, 32768], P('seed', 'dp'), may hold values from 0 to 7, as said below
- slots: int32 [4, 32768], P('seed', 'dp'), may hold values from 0 to 4095, as said below
- old_priorities: float32 [4, 32768], P('seed', 'dp'), may hold values from 0.01 to 2
- actor_w1: float32 [4, 256, 17], P('seed'), may hold values from -1.5 to 1.5
- actor_b1: float32 [4, 256], P('seed'), may hold values from -1.5 to 1.5
- actor_w2: float32 [4, 256, 256], P('seed'), may hold values from -0.375 to 0.375
- actor_b2: float32 [4, 256], P('seed'), may hold values from -1.5 to 1.5
- actor_w3: float32 [4, 12, 256], P('seed'), may hold values from -0.375 to 0.375
- actor_b3: float32 [4, 12], P('seed'), may hold values from -1.5 to 1.5
- critic_w1: float32 [4, 2, 256, 23], P('seed'), may hold values from -1.25 to 1.25
- critic_b1: float32 [4, 2, 256], P('seed'), may hold values from -1.5 to 1.5
- critic_w2: float32 [4, 2, 256, 256], P('seed'), may hold values from -0.375 to 0.375
- critic_b2: float32 [4, 2, 256], P('seed'), may hold values from -1.5 to 1.5
- critic_w3: float32 [4, 2, 256], P('seed'), may hold values from -0.375 to 0.375
- critic_b3: float32 [4, 2], P('seed'), may hold values from -2 to 2
- target_w1: float32 [4, 2, 256, 23], P('seed'), may hold values from -1.25 to 1.25
- target_b1: float32 [4, 2, 256], P('seed'), may hold values from -1.5 to 1.5
- target_w2: float32 [4, 2, 256, 256], P('seed'), may hold values from -0.375 to 0.375
- target_b2: float32 [4, 2, 256], P('seed'), may hold values from -1.5 to 1.5
- target_w3: float32 [4, 2, 256], P('seed'), may hold values from -0.375 to 0.375
- target_b3: float32 [4, 2], P('seed'), may hold values from -2 to 2
- log_alpha: float32 [4], P('seed'), may hold values from -2.5 to -0.5
Outputs:
- grad_actor_w1: float32 [4, 256, 17], P('seed', 'dp')
- grad_actor_b1: float32 [4, 256], P('seed', 'dp')
- grad_actor_w2: float32 [4, 256, 256], P('seed', 'dp')
- grad_actor_b2: float32 [4, 256], P('seed', 'dp')
- grad_actor_w3: float32 [4, 12, 256], P('seed', None, 'dp')
- grad_actor_b3: float32 [4, 12], P('seed')
- grad_critic_w1: float32 [4, 2, 256, 23], P('seed', None, 'dp')
- grad_critic_b1: float32 [4, 2, 256], P('seed', None, 'dp')
- grad_critic_w2: float32 [4, 2, 256, 256], P('seed', None, 'dp')
- grad_critic_b2: float32 [4, 2, 256], P('seed', None, 'dp')
- grad_critic_w3: float32 [4, 2, 256], P('seed', None, 'dp')
- grad_critic_b3: float32 [4, 2], P('seed')
- grad_log_alpha: float32 [4], P('seed')
- new_priorities: float32 [4, 32768], P('seed', 'dp')
- max_priority: float32 [], replicated
The draws below stay inside these ranges and needn't reach their ends.
Inputs may be any that keep to these rules, and one draw needn't show every extreme that they name: `valid_counts`: some device of each agent has all 4096 rows valid. `owners`: the 4096 rows of each device name every owner exactly 512 times. Within one agent, rows that name the same owner hold distinct slots, and every slot of every owner is named.
All inputs are finite; a program needn't handle non-finite values. No bound on the sum of `dones` on one device may be relied on, other than what follows from the above.
Results may differ from the reference program's by a relative error of at most 0.0001.
Values sent between devices are 32-bit elements; how exact they have to be, the bound alone decides.
No kernel may reach another device: no remote copies, remote signals or barrier semaphores. Data moves between devices by JAX's collectives and lax.ppermute only.
A program may use at most 128 MiB of HBM per device.

```python
import math
import jax
import jax.numpy as jnp
from jax import lax

OBS = 17
ACT = 6
HID = 256
TOK_DEV = 4096
SEEDS = 4
TOKENS = 32768
REPLAY_DEV = 4096
REPLAY = 32768


def routing(key):
    peers = TOKENS // TOK_DEV
    share = TOK_DEV // peers

    def one_agent(agent_key):
        own_key, slot_key = jax.random.split(agent_key)
        base = jnp.arange(TOK_DEV, dtype=jnp.int32) // share
        picked = jax.vmap(lambda k: jax.random.permutation(k, base))(jax.random.split(own_key, peers))
        hits = (picked[:, :, None] == jnp.arange(peers, dtype=jnp.int32)[None, None, :]).astype(jnp.int32)
        rank = jnp.sum(hits * (jnp.cumsum(hits, axis=1) - 1), axis=2)
        orders = jax.vmap(lambda k: jax.random.permutation(k, TOK_DEV))(jax.random.split(slot_key, peers))
        position = jnp.arange(peers, dtype=jnp.int32)[:, None] * share + rank
        chosen = orders[picked, position]
        return (picked.reshape(-1), chosen.reshape(-1))
    return jax.vmap(one_agent)(jax.random.split(key, SEEDS))


def draw_owners(key, part):
    return routing(key)[0].astype(jnp.int32)


def draw_slots(key, part):
    return routing(key)[1].astype(jnp.int32)


def draw_valid_counts(key, part):
    key = jax.random.fold_in(key, 11)
    peers = TOKENS // TOK_DEV
    steps = jnp.arange(peers, dtype=jnp.int32)
    upper = TOK_DEV // 3 + 2 * TOK_DEV // 3 * steps // max(peers - 1, 1)
    lower = upper * 3 // 4
    first_key, second_key = jax.random.split(key)
    counts = jax.random.randint(first_key, (SEEDS, peers), lower[None, :], upper[None, :] + 1)
    full = jax.random.randint(second_key, (SEEDS, 1), 0, peers)
    counts = jnp.where(steps[None, :] == full, TOK_DEV, counts)
    return counts.astype(jnp.int32)


def draw_rewards(key, part):
    key = jax.random.fold_in(key, 7)
    peers = TOKENS // TOK_DEV
    device = (jnp.arange(TOKENS) // TOK_DEV).astype(jnp.float32)
    agent = jnp.arange(SEEDS).astype(jnp.float32)[:, None]
    scale = (1.0 + 2.0 * device / max(peers - 1, 1))[None, :] * (1.0 + agent / max(SEEDS - 1, 1))
    base = jnp.clip(jax.random.normal(key, (SEEDS, TOKENS)), -4.0, 4.0)
    return (base * scale).astype(jnp.float32)


def draw_probs(key, part):
    key = jax.random.fold_in(key, 5)
    peers = TOKENS // TOK_DEV
    device = (jnp.arange(TOKENS) // TOK_DEV).astype(jnp.float32)
    base = 3.0 - 2.0 * device / max(peers - 1, 1)
    spread = jax.random.uniform(key, (SEEDS, TOKENS), minval=0.0, maxval=math.log(10.0))
    return (1e-06 * base[None, :] * jnp.exp(spread)).astype(jnp.float32)


def touch_ends(entries, rng, smallest, top_value):
    dims = entries.shape
    spot = [jax.random.randint(jax.random.fold_in(rng, axis), (), 0, dims[axis]) for axis in range(len(dims))]
    entries = entries.at[tuple(spot)].set(smallest)
    longest = dims.index(max(dims))
    spot[longest] = (spot[longest] + 1) % dims[longest]
    return entries.at[tuple(spot)].set(top_value)


def levels(key, extent, cuts, smallest, largest):
    factor_of = 1.0
    for dim, parts in cuts:
        draws = jax.random.uniform(jax.random.fold_in(jax.random.fold_in(key, 6), dim), (parts,), jnp.float32, smallest / len(cuts), largest / len(cuts))
        factor_of = factor_of * jnp.repeat(jnp.exp(draws), extent[dim] // parts).reshape((-1,) + (1,) * (len(extent) - 1 - dim))
    return factor_of


def normal_values(key, shape, width, reach, pieces=(), kind=jnp.bfloat16):
    values = jax.random.normal(key, shape, jnp.float32) * width
    if len(pieces) > 0:
        values = levels(key, shape, pieces, -0.22, 0.18) * values
    return jnp.clip(values, min=-reach, max=reach).astype(kind)


def setup_inputs(seed: int = 0) -> dict:
    key_of = jax.random.split(jax.random.key(seed), 32)
    states = normal_values(key_of[0], (SEEDS, OBS, TOKENS), 1.0, 6.0, ((0, 4), (2, 8)), jnp.float32)
    actions = jnp.clip(jax.random.uniform(key_of[1], (SEEDS, ACT, TOKENS), jnp.float32, -0.95, 0.95) * levels(key_of[1], (SEEDS, ACT, TOKENS), ((0, 4), (2, 8)), -0.4, 0.0), -0.95, 0.95)
    rewards = draw_rewards(jax.random.fold_in(key_of[31], 71), 0)
    next_states = normal_values(key_of[3], (SEEDS, OBS, TOKENS), 1.0, 6.0, ((0, 4), (2, 8)), jnp.float32)
    dones = touch_ends((jax.random.randint(key_of[4], (SEEDS, TOKENS), 0, 10) < 1).astype(jnp.int32), jax.random.fold_in(key_of[4], 1), 0, 1)
    noise_now = normal_values(key_of[5], (SEEDS, ACT, TOKENS), 1.0, 4.0, ((0, 4), (2, 8)), jnp.float32)
    noise_next = normal_values(key_of[6], (SEEDS, ACT, TOKENS), 1.0, 4.0, ((0, 4), (2, 8)), jnp.float32)
    probs = draw_probs(jax.random.fold_in(key_of[31], 71), 0)
    valid_counts = draw_valid_counts(jax.random.fold_in(key_of[31], 71), 0)
    owners = draw_owners(jax.random.fold_in(key_of[31], 71), 0)
    slots = draw_slots(jax.random.fold_in(key_of[31], 71), 0)
    old_priorities = jnp.clip(jnp.exp(math.log(2.0) - 5.2983174 * jax.random.uniform(key_of[11], (SEEDS, REPLAY), jnp.float32) ** levels(key_of[11], (SEEDS, REPLAY), ((0, 4), (1, 8)), -0.2, 0.2)), 0.01, 2.0)
    actor_w1 = normal_values(key_of[12], (SEEDS, HID, OBS), OBS ** -0.5, 1.5, ((0, 4),), jnp.float32)
    actor_b1 = normal_values(key_of[13], (SEEDS, HID), 0.3, 1.5, ((0, 4),), jnp.float32)
    actor_w2 = normal_values(key_of[14], (SEEDS, HID, HID), HID ** -0.5, 0.375, ((0, 4),), jnp.float32)
    actor_b2 = normal_values(key_of[15], (SEEDS, HID), 0.3, 1.5, ((0, 4),), jnp.float32)
    actor_w3 = normal_values(key_of[16], (SEEDS, 2 * ACT, HID), HID ** -0.5, 0.375, ((0, 4),), jnp.float32)
    actor_b3 = normal_values(key_of[17], (SEEDS, 2 * ACT), 0.3, 1.5, ((0, 4),), jnp.float32)
    critic_w1 = normal_values(key_of[18], (SEEDS, 2, HID, OBS + ACT), (OBS + ACT) ** -0.5, 1.25, ((0, 4),), jnp.float32)
    critic_b1 = normal_values(key_of[19], (SEEDS, 2, HID), 0.3, 1.5, ((0, 4),), jnp.float32)
    critic_w2 = normal_values(key_of[20], (SEEDS, 2, HID, HID), HID ** -0.5, 0.375, ((0, 4),), jnp.float32)
    critic_b2 = normal_values(key_of[21], (SEEDS, 2, HID), 0.3, 1.5, ((0, 4),), jnp.float32)
    critic_w3 = normal_values(key_of[22], (SEEDS, 2, HID), HID ** -0.5, 0.375, ((0, 4),), jnp.float32)
    critic_b3 = normal_values(key_of[23], (SEEDS, 2), 0.5, 2.0, ((0, 4),), jnp.float32)
    target_w1 = normal_values(key_of[24], (SEEDS, 2, HID, OBS + ACT), (OBS + ACT) ** -0.5, 1.25, ((0, 4),), jnp.float32)
    target_b1 = normal_values(key_of[25], (SEEDS, 2, HID), 0.3, 1.5, ((0, 4),), jnp.float32)
    target_w2 = normal_values(key_of[26], (SEEDS, 2, HID, HID), HID ** -0.5, 0.375, ((0, 4),), jnp.float32)
    target_b2 = normal_values(key_of[27], (SEEDS, 2, HID), 0.3, 1.5, ((0, 4),), jnp.float32)
    target_w3 = normal_values(key_of[28], (SEEDS, 2, HID), HID ** -0.5, 0.375, ((0, 4),), jnp.float32)
    target_b3 = normal_values(key_of[29], (SEEDS, 2), 0.5, 2.0, ((0, 4),), jnp.float32)
    log_alpha = jnp.clip(-2.5 + 2.0 * jax.random.uniform(key_of[30], (SEEDS,), jnp.float32) ** levels(key_of[30], (SEEDS,), ((0, 4),), -0.2, 0.2), -2.5, -0.5)
    return dict(states=states, actions=actions, rewards=rewards, next_states=next_states, dones=dones, noise_now=noise_now, noise_next=noise_next, probs=probs, valid_counts=valid_counts, owners=owners, slots=slots, old_priorities=old_priorities, actor_w1=actor_w1, actor_b1=actor_b1, actor_w2=actor_w2, actor_b2=actor_b2, actor_w3=actor_w3, actor_b3=actor_b3, critic_w1=critic_w1, critic_b1=critic_b1, critic_w2=critic_w2, critic_b2=critic_b2, critic_w3=critic_w3, critic_b3=critic_b3, target_w1=target_w1, target_b1=target_b1, target_w2=target_w2, target_b2=target_b2, target_w3=target_w3, target_b3=target_b3, log_alpha=log_alpha)


HIGH = lax.Precision.HIGHEST
GAMMA = 0.99
STD_LO = -5.0
STD_HI = 2.0
ENTROPY_AIM = -6.0
SOFT_TEMP = 0.1
BETA = 0.4
PRIO_EXP = 0.6
PRIO_EPS = 0.001
HALF_LOG_TAU = 0.5 * math.log(2.0 * math.pi)
LOG_TWO = math.log(2.0)

def dense(weight, inputs, bias):
    return jnp.dot(weight, inputs, precision=HIGH) + bias[:, None]

def actor_head(params, observe):
    w_one, b_one, w_two, b_two, w_out, b_out = params
    hidden = jax.nn.silu(dense(w_one, observe, b_one))
    hidden = jax.nn.silu(dense(w_two, hidden, b_two))
    result = dense(w_out, hidden, b_out)
    half = result.shape[0] // 2
    log_std = STD_LO + 0.5 * (STD_HI - STD_LO) * (jnp.tanh(result[half:]) + 1.0)
    return (result[:half], log_std)

def squash(means, log_std, noise):
    pre = means + jnp.exp(log_std) * noise
    action = jnp.tanh(pre)
    log_jac = 2.0 * (LOG_TWO - pre - jax.nn.softplus(-2.0 * pre))
    logp = lax.optimization_barrier(jnp.sum(-0.5 * noise * noise - log_std - HALF_LOG_TAU - log_jac, axis=0))
    return (action, logp)

def critic_value(params, index, observe, action):
    w_one, b_one, w_two, b_two, w_out, b_out = params
    joined = jnp.concatenate([observe, action], axis=0)
    hidden = jax.nn.silu(dense(w_one[index], joined, b_one[index]))
    hidden = jax.nn.silu(dense(w_two[index], hidden, b_two[index]))
    return jnp.dot(w_out[index], hidden, precision=HIGH) + b_out[index]

def soft_min(first, second):
    return -SOFT_TEMP * jnp.logaddexp(-first / SOFT_TEMP, -second / SOFT_TEMP)

def one_agent(actor_p, critic_p, target_p, temper, observe, action, reward, observe_next, ended, noise_now, noise_next, chance, counts, owner, slot, old_table):
    rows = observe.shape[1]
    place = jnp.arange(rows, dtype=jnp.int32)
    limit = jnp.repeat(counts, TOK_DEV, total_repeat_length=rows)
    valid = place % TOK_DEV < limit
    mask = valid.astype(jnp.float32)
    total = jnp.sum(mask)
    least = jnp.min(jnp.where(valid, chance, 1.0))
    importance = (least / chance) ** BETA
    alpha = jnp.exp(temper)
    next_mean, next_std = actor_head(actor_p, observe_next)
    next_action, next_logp = squash(next_mean, next_std, noise_next)
    target_q = soft_min(critic_value(target_p, 0, observe_next, next_action), critic_value(target_p, 1, observe_next, next_action))
    target = reward + GAMMA * (1.0 - ended.astype(jnp.float32)) * (target_q - alpha * next_logp)
    critic_coef = mask * importance / total
    actor_coef = mask / total

    def critic_loss(params):
        first = critic_value(params, 0, observe, action)
        second = critic_value(params, 1, observe, action)
        loss = jnp.sum(critic_coef * 0.5 * ((first - target) ** 2 + (second - target) ** 2))
        return (loss, 0.5 * (first + second) - target)
    loss_q, critic_back, delta = jax.vjp(critic_loss, critic_p, has_aux=True)
    critic_grad = critic_back(jnp.ones_like(loss_q))[0]

    def actor_loss(params):
        means, log_std = actor_head(params, observe)
        fresh, logp = squash(means, log_std, noise_now)
        value = soft_min(critic_value(critic_p, 0, observe, fresh), critic_value(critic_p, 1, observe, fresh))
        return (jnp.sum(actor_coef * (alpha * logp - value)), logp)
    loss_pi, actor_back, logp_now = jax.vjp(actor_loss, actor_p, has_aux=True)
    actor_grad = actor_back(jnp.ones_like(loss_pi))[0]

    def alpha_loss(value):
        return -jnp.sum(actor_coef * value * (logp_now + ENTROPY_AIM))
    loss_a, alpha_back = jax.vjp(alpha_loss, temper)
    alpha_grad = alpha_back(jnp.ones_like(loss_a))[0]
    priority = (jnp.abs(delta) + PRIO_EPS) ** PRIO_EXP
    where_to = jnp.where(valid, owner * REPLAY_DEV + slot, REPLAY)
    new_table = old_table.at[where_to].set(priority, mode='drop')
    top = jnp.max(jnp.where(valid, priority, 0.0))
    return (actor_grad, critic_grad, alpha_grad, new_table, top)

def reference(states, actions, rewards, next_states, dones, noise_now, noise_next, probs, valid_counts, owners, slots, old_priorities, actor_w1, actor_b1, actor_w2, actor_b2, actor_w3, actor_b3, critic_w1, critic_b1, critic_w2, critic_b2, critic_w3, critic_b3, target_w1, target_b1, target_w2, target_b2, target_w3, target_b3, log_alpha):
    actor_all = (actor_w1, actor_b1, actor_w2, actor_b2, actor_w3, actor_b3)
    critic_all = (critic_w1, critic_b1, critic_w2, critic_b2, critic_w3, critic_b3)
    target_all = (target_w1, target_b1, target_w2, target_b2, target_w3, target_b3)
    actor_list = []
    critic_list = []
    alpha_list = []
    table_list = []
    top_list = []
    for agent in range(SEEDS):
        result = one_agent(tuple((p[agent] for p in actor_all)), tuple((p[agent] for p in critic_all)), tuple((p[agent] for p in target_all)), log_alpha[agent], states[agent], actions[agent], rewards[agent], next_states[agent], dones[agent], noise_now[agent], noise_next[agent], probs[agent], valid_counts[agent], owners[agent], slots[agent], old_priorities[agent])
        actor_list.append(result[0])
        critic_list.append(result[1])
        alpha_list.append(result[2])
        table_list.append(result[3])
        top_list.append(result[4])
    actor_out = [jnp.stack([g[k] for g in actor_list]) for k in range(6)]
    critic_out = [jnp.stack([g[k] for g in critic_list]) for k in range(6)]
    return (actor_out[0], actor_out[1], actor_out[2], actor_out[3], actor_out[4], actor_out[5], critic_out[0], critic_out[1], critic_out[2], critic_out[3], critic_out[4], critic_out[5], jnp.stack(alpha_list), jnp.stack(table_list), jnp.max(jnp.stack(top_list)))
```

```python
import functools
import math

import jax
import jax.numpy as jnp
from jax import lax
from jax.experimental import pallas as pl
from jax.experimental.pallas import tpu as pltpu
from jax.sharding import PartitionSpec as P

F32 = jnp.float32
BF16 = jnp.bfloat16
GAMMA = 0.99
STD_LO = -5.0
STD_HI = 2.0
ENTROPY_AIM = -6.0
SOFT_TEMP = 0.1
BETA = 0.4
PRIO_EXP = 0.6
PRIO_EPS = 0.001
HALF_LOG_TAU = 0.5 * math.log(2.0 * math.pi)
LOG_TWO = math.log(2.0)

LANES = 128
OBS = 17
ACT = 6
HID = 256
JOIN = 24
HEAD = 16
CHUNK = 512
GROUP = CHUNK // LANES
VMEM_LIMIT = 56 * 1024 * 1024


def dot(left, right):
    return jnp.dot(left, right, preferred_element_type=F32)


def dot_t(left, right):
    return lax.dot_general(left, right, (((1,), (1,)), ((), ())), preferred_element_type=F32)


def split(value):
    high = value.astype(BF16)
    low = (value - high.astype(F32)).astype(BF16)
    return high, low


def split_wide(value):
    high = value.astype(BF16).astype(F32)
    return high, value - high


def dot3(weight, value):
    high, low = value
    return dot(weight[0], high) + dot(weight[0], low) + dot(weight[1], high)


def dot3_t(left, right):
    return dot_t(left[0], right[0]) + dot_t(left[0], right[1]) + dot_t(left[1], right[0])


def wide(column):
    return jnp.concatenate([column] * GROUP, axis=1)


def stack_join(value):
    high, low = split_wide(value)
    return jnp.concatenate([high, low, high], axis=0).astype(BF16)


def stack_weight(value):
    high, low = split_wide(value)
    return jnp.transpose(jnp.concatenate([high, high, low], axis=0)).astype(BF16)


def activate(half):
    bent = jnp.tanh(half)
    return bent, half + half * bent


def slope(bent, hidden):
    return (1.0 + hidden) + bent * (1.0 - hidden)


def soft_min(first, second):
    return jnp.minimum(first, second) - SOFT_TEMP * jnp.log(
        1.0 + jnp.exp(-jnp.abs(first - second) / SOFT_TEMP)
    )


def squash(head, noise):
    means, bend = head[:8], jnp.tanh(head[8:])
    log_std = STD_LO + 0.5 * (STD_HI - STD_LO) * (bend + 1.0)
    spread = jnp.exp(log_std) * noise
    pre = means + spread
    action = jnp.tanh(pre)
    size = jnp.abs(pre)
    log_jac = 2.0 * (LOG_TWO - size - jnp.log(1.0 + jnp.exp(-2.0 * size)))
    row = lax.broadcasted_iota(jnp.int32, pre.shape, 0)
    inside = (row >= 1) & (row <= ACT)
    terms = jnp.where(inside, -0.5 * noise * noise - log_std - HALF_LOG_TAU - log_jac, 0.0)
    return action, jnp.sum(terms, axis=0, keepdims=True), spread, bend


def load_rows(ref, count, block):
    blocks = ref.shape[0] // count
    return ref[pl.ds(block, count, stride=blocks), :]


def load_chunk(ref, count, first):
    return jnp.concatenate([load_rows(ref, count, first + g) for g in range(GROUP)], axis=1)


def load_row(ref, first):
    return jnp.concatenate([ref[pl.ds(first + g, 1), :] for g in range(GROUP)], axis=1)


def fill_join(join, obs_ref, act_ref, first):
    join[0:OBS, :] = load_chunk(obs_ref, OBS, first)
    if act_ref is not None:
        join[OBS : OBS + ACT, :] = load_chunk(act_ref, ACT, first)
    join[JOIN - 1 : JOIN, :] = jnp.ones((1, CHUNK), F32)


def with_action(join, action):
    row = lax.broadcasted_iota(jnp.int32, action.shape, 0)
    inside = (row >= 1) & (row <= ACT)
    return jnp.concatenate([join[:16], jnp.where(inside, action, join[16:])], axis=0)


def first_weights(weight_ref, bias_row, index, scratch):
    rows = weight_ref.shape[0]
    scratch[...] = jnp.zeros_like(scratch)
    scratch[0:rows, :] = weight_ref[:, index, :]
    scratch[JOIN - 1 : JOIN, :] = bias_row
    return stack_weight(0.5 * scratch[...])


def store_split(ref, index, value):
    high, low = split(value)
    ref[index, 0] = high
    ref[index, 1] = low


def pair(ref, index):
    return ref[index, 0], ref[index, 1]


def column(row):
    return jnp.transpose(jnp.broadcast_to(row, (LANES, row.shape[1])))


def head_weights(weight_ref, scratch):
    scratch[...] = jnp.zeros_like(scratch)
    scratch[1 : 1 + ACT, :] = weight_ref[0:ACT, 0, :]
    scratch[9 : 9 + ACT, :] = weight_ref[ACT : 2 * ACT, 0, :]
    return scratch[...]


def head_bias(bias_ref):
    row = lax.broadcasted_iota(jnp.int32, (HEAD, LANES), 0)
    out = jnp.zeros((HEAD, LANES), F32)
    for k in range(ACT):
        out = jnp.where(row == 1 + k, bias_ref[0, k], out)
        out = jnp.where(row == 9 + k, bias_ref[0, ACT + k], out)
    return out


def fold(value):
    total = value[:, :LANES]
    for g in range(1, GROUP):
        total = total + value[:, g * LANES : (g + 1) * LANES]
    return total


def valid_lanes(first, count):
    lane = lax.broadcasted_iota(jnp.int32, (1, CHUNK), 1)
    return lane + first * LANES < count


def spread_row(value):
    return jnp.broadcast_to(value, (1, LANES))


def critic_kernel(
    peers,
    count_ref,
    temper_ref,
    actor_b3,
    critic_b3,
    target_b3,
    states,
    actions,
    rewards,
    next_states,
    dones,
    noise_next,
    probs,
    owners,
    slots,
    actor_w1,
    actor_b1,
    actor_w2,
    actor_b2,
    actor_w3,
    critic_w1,
    critic_b1,
    critic_w2,
    critic_b2,
    critic_w3,
    target_w1,
    target_b1,
    target_w2,
    target_b2,
    target_w3,
    send,
    top,
    one,
    two,
    back,
    head,
    bias_two,
    last,
    wide_bias,
    join,
    turn,
    acc_two,
    acc_one,
    acc_side,
    acc_table,
    acc_row,
):
    count = count_ref[0, 0]
    alpha = jnp.exp(temper_ref[0])
    share = HID // peers
    depth = acc_table.shape[0] // peers
    one[0] = first_weights(actor_w1, actor_b1[...], 0, turn)
    for k in range(2):
        one[1 + k] = first_weights(target_w1, target_b1[k : k + 1, :], k, turn)
        one[3 + k] = first_weights(critic_w1, critic_b1[k : k + 1, :], k, turn)
    store_split(two, 0, 0.5 * actor_w2[...])
    bias_two[0] = column(0.5 * actor_b2[...])
    for k in range(2):
        store_split(two, 1 + k, 0.5 * target_w2[k])
        store_split(two, 3 + k, 0.5 * critic_w2[k])
        store_split(back, k, jnp.transpose(0.5 * critic_w2[k]))
        bias_two[1 + k] = column(0.5 * target_b2[k : k + 1, :])
        bias_two[3 + k] = column(0.5 * critic_b2[k : k + 1, :])
        last[k] = column(target_w3[k : k + 1, :])
        last[2 + k] = column(critic_w3[k : k + 1, :])
    store_split(head, 0, head_weights(actor_w3, turn.at[0:HEAD]))
    wide_bias[...] = head_bias(actor_b3)
    acc_two[...] = jnp.zeros_like(acc_two)
    acc_one[...] = jnp.zeros_like(acc_one)
    acc_side[...] = jnp.zeros_like(acc_side)
    acc_table[...] = jnp.zeros_like(acc_table)
    acc_row[...] = jnp.zeros_like(acc_row)

    def step(index, carry):
        first = index * GROUP
        fill_join(join, next_states, None, first)
        join[OBS : OBS + ACT, :] = jnp.zeros((ACT, CHUNK), F32)
        nexts = join[...]
        _, hidden = activate(dot(one[0], stack_join(nexts)))
        half = dot3(pair(two, 0), split(hidden)) + wide(bias_two[0])
        _, hidden = activate(half)
        out = dot3(pair(head, 0), split(hidden)) + wide(wide_bias[...])
        join[OBS : OBS + ACT, :] = load_chunk(noise_next, ACT, first)
        action, logp, _, _ = squash(out, join[16:24, :])
        given = stack_join(with_action(nexts, action))
        values = []
        for k in range(2):
            _, hidden = activate(dot(one[1 + k], given))
            _, hidden = activate(dot3(pair(two, 1 + k), split(hidden)) + wide(bias_two[1 + k]))
            values.append(
                jnp.sum(hidden * wide(last[k]), axis=0, keepdims=True) + target_b3[0, k]
            )
        keep = GAMMA * (1.0 - load_row(dones, first).astype(F32))
        target = load_row(rewards, first) + keep * (soft_min(values[0], values[1]) - alpha * logp)
        valid = valid_lanes(first, count)
        chance = load_row(probs, first)
        coef = jnp.where(valid, jnp.exp(-BETA * jnp.log(chance)), 0.0)
        fill_join(join, states, actions, first)
        given = stack_join(join[...])
        errors = []
        for k in range(2):
            bent, hidden = activate(dot(one[3 + k], given))
            slope_one = slope(bent, hidden)
            hidden_one = split(hidden)
            half = dot3(pair(two, 3 + k), hidden_one) + wide(bias_two[3 + k])
            bent, hidden = activate(half)
            weight = wide(last[2 + k])
            error = jnp.sum(hidden * weight, axis=0, keepdims=True) + critic_b3[0, k] - target
            errors.append(error)
            scaled = coef * error
            grad = (0.5 * scaled) * weight * slope(bent, hidden)
            acc_side[k] += fold(grad)
            acc_side[2 + k] += fold(scaled * hidden)
            acc_row[k : k + 1, :] += scaled
            grad_two = split(grad)
            acc_two[k] += dot3_t(grad_two, hidden_one)
            grad_one = split(dot3(pair(back, k), grad_two) * slope_one)
            acc_one[k] += dot_t(grad_one[0], given[:48]) + dot_t(grad_one[1], given[:48])
        delta = 0.5 * (errors[0] + errors[1])
        priority = jnp.exp(PRIO_EXP * jnp.log(jnp.abs(delta) + PRIO_EPS))
        priority = jnp.where(valid, priority, 0.0)
        acc_row[2:3, :] = jnp.maximum(acc_row[2:3, :], priority)
        slot = load_row(slots, first)
        place = load_row(owners, first) * depth + lax.shift_right_logical(slot, 7)
        lane = slot & (LANES - 1)
        rows = acc_table.shape[0]
        row_hit = lax.broadcasted_iota(jnp.int32, (rows, CHUNK), 0) == place
        lane_hit = lax.broadcasted_iota(jnp.int32, (LANES, CHUNK), 0) == lane
        high, low = split_wide(priority)
        picked = jnp.concatenate(
            [jnp.where(lane_hit, high, 0.0), jnp.where(lane_hit, low, 0.0)], axis=0
        ).astype(BF16)
        acc_table[...] += dot_t(jnp.where(row_hit, 1.0, 0.0).astype(BF16), picked)
        return carry

    lax.fori_loop(0, (count + CHUNK - 1) // CHUNK, step, 0)

    side = [jnp.sum(acc_side[k], axis=1, keepdims=True) for k in range(4)]
    small = [acc_one[k][:, :JOIN] + acc_one[k][:, JOIN:] for k in range(2)]
    joined = jnp.concatenate(small + side + [jnp.zeros((HID, LANES - 52), F32)], axis=1)
    acc_side[0] = joined
    lane = lax.broadcasted_iota(jnp.int32, probs.shape, 1)
    row = lax.broadcasted_iota(jnp.int32, probs.shape, 0)
    least = jnp.min(jnp.where(row * LANES + lane < count, probs[...], 1.0), keepdims=True)
    best = jnp.max(acc_row[2:3, :], keepdims=True)
    top[...] = jnp.broadcast_to(best, top.shape)
    sums = jnp.concatenate(
        [
            jnp.full((1, LANES), count.astype(F32)),
            spread_row(least),
            spread_row(jnp.sum(acc_row[0:1, :], keepdims=True)),
            spread_row(jnp.sum(acc_row[1:2, :], keepdims=True)),
            jnp.zeros((4, LANES), F32),
        ],
        axis=0,
    )
    table = acc_table[:, :LANES] + acc_table[:, LANES:]
    for p in range(peers):
        mine = slice(p * share, (p + 1) * share)
        at = 0
        for k in range(2):
            for t in range(2):
                send[p, at : at + share, :] = acc_two[k, mine, t * LANES : (t + 1) * LANES]
                at += share
        send[p, at : at + share, :] = acc_side[0, mine, :]
        at += share
        send[p, at : at + depth, :] = table[p * depth : (p + 1) * depth]
        at += depth
        send[p, at : at + 8, :] = sums


def actor_kernel(
    peers,
    count_ref,
    temper_ref,
    actor_b3,
    critic_b3,
    states,
    noise_now,
    actor_w1,
    actor_b1,
    actor_w2,
    actor_b2,
    actor_w3,
    critic_w1,
    critic_b1,
    critic_w2,
    critic_b2,
    critic_w3,
    send,
    one,
    two,
    back,
    head,
    head_back,
    entry,
    bias_two,
    last,
    wide_bias,
    join,
    turn,
    acc_two,
    acc_one,
    acc_head,
    acc_side,
    acc_out,
    acc_row,
):
    count = count_ref[0, 0]
    alpha = jnp.exp(temper_ref[0])
    share = HID // peers
    one[0] = first_weights(actor_w1, actor_b1[...], 0, turn)
    for k in range(2):
        one[1 + k] = first_weights(critic_w1, critic_b1[k : k + 1, :], k, turn)
        store_split(entry, k, turn[16:24, :])
    store_split(two, 0, 0.5 * actor_w2[...])
    store_split(back, 0, jnp.transpose(0.5 * actor_w2[...]))
    bias_two[0] = column(0.5 * actor_b2[...])
    for k in range(2):
        store_split(two, 1 + k, 0.5 * critic_w2[k])
        store_split(back, 1 + k, jnp.transpose(0.5 * critic_w2[k]))
        bias_two[1 + k] = column(0.5 * critic_b2[k : k + 1, :])
        last[k] = column(critic_w3[k : k + 1, :])
    final = head_weights(actor_w3, turn.at[0:HEAD])
    store_split(head, 0, final)
    head_back[...] = stack_weight(0.5 * final)
    wide_bias[...] = head_bias(actor_b3)
    acc_two[...] = jnp.zeros_like(acc_two)
    acc_one[...] = jnp.zeros_like(acc_one)
    acc_head[...] = jnp.zeros_like(acc_head)
    acc_side[...] = jnp.zeros_like(acc_side)
    acc_out[...] = jnp.zeros_like(acc_out)
    acc_row[...] = jnp.zeros_like(acc_row)

    def step(index, carry):
        first = index * GROUP
        valid = valid_lanes(first, count)
        mask = jnp.where(valid, 1.0, 0.0)
        fill_join(join, states, noise_now, first)
        noise = join[16:24, :]
        row = lax.broadcasted_iota(jnp.int32, noise.shape, 0)
        inside = (row >= 1) & (row <= ACT)
        tail = jnp.where(inside, 0.0, noise)
        given = stack_join(jnp.concatenate([join[0:16, :], tail], axis=0))
        bent, hidden = activate(dot(one[0], given))
        slope_one = slope(bent, hidden)
        hidden_one = split(hidden)
        bent, hidden = activate(dot3(pair(two, 0), hidden_one) + wide(bias_two[0]))
        slope_two = slope(bent, hidden)
        hidden_two = split(hidden)
        out = dot3(pair(head, 0), hidden_two) + wide(wide_bias[...])
        action, logp, spread, bend = squash(out, noise)
        acc_row[0:1, :] += mask * (logp + ENTROPY_AIM)
        fresh = stack_join(with_action(join[...], action))
        values, slopes = [], []
        for k in range(2):
            bent, hidden = activate(dot(one[1 + k], fresh))
            inner = slope(bent, hidden)
            bent, hidden = activate(dot3(pair(two, 1 + k), split(hidden)) + wide(bias_two[1 + k]))
            weight = wide(last[k])
            values.append(jnp.sum(hidden * weight, axis=0, keepdims=True) + critic_b3[0, k])
            slopes.append((inner, weight * slope(bent, hidden)))
        gap = (values[1] - values[0]) / SOFT_TEMP
        first_part = 0.5 + 0.5 * jnp.tanh(0.5 * gap)
        parts = (first_part, 0.5 - 0.5 * jnp.tanh(0.5 * gap))
        push = jnp.zeros((8, CHUNK), F32)
        for k in range(2):
            inner, outer = slopes[k]
            grad_two = split((-0.5 * mask * parts[k]) * outer)
            grad_one = split(dot3(pair(back, 1 + k), grad_two) * inner)
            push = push + dot3(pair(entry, k), grad_one)
        pull = alpha * mask
        grad_pre = jnp.where(inside, 2.0 * pull * action + push * (1.0 - action * action), 0.0)
        grad_std = jnp.where(inside, grad_pre * spread - pull, 0.0)
        grad_bend = 0.5 * (STD_HI - STD_LO) * grad_std * (1.0 - bend * bend)
        grad_out = jnp.concatenate([grad_pre, grad_bend], axis=0)
        acc_out[...] += fold(grad_out)
        outs = stack_join(grad_out)
        acc_head[...] += dot_t(hidden_two[0], outs[:32]) + dot_t(hidden_two[1], outs[:32])
        grad = dot(head_back[...], outs) * slope_two
        acc_side[...] += fold(grad)
        grad_two = split(grad)
        acc_two[...] += dot3_t(grad_two, hidden_one)
        grad_one = split(dot3(pair(back, 0), grad_two) * slope_one)
        acc_one[...] += dot_t(grad_one[0], given[:48]) + dot_t(grad_one[1], given[:48])
        return carry

    lax.fori_loop(0, (count + CHUNK - 1) // CHUNK, step, 0)

    joined = jnp.concatenate(
        [
            acc_one[:, :JOIN] + acc_one[:, JOIN:],
            acc_head[:, :HEAD] + acc_head[:, HEAD:],
            jnp.sum(acc_side[...], axis=1, keepdims=True),
            jnp.zeros((HID, LANES - JOIN - HEAD - 1), F32),
        ],
        axis=1,
    )
    acc_side[...] = joined
    gone = -jnp.sum(acc_row[0:1, :], keepdims=True)
    out_sum = jnp.broadcast_to(jnp.sum(acc_out[...], axis=1, keepdims=True), (HEAD, LANES))
    for p in range(peers):
        mine = slice(p * share, (p + 1) * share)
        send[p, 0:share, :] = acc_two[mine, 0:LANES]
        send[p, share : 2 * share, :] = acc_two[mine, LANES : 2 * LANES]
        send[p, 2 * share : 3 * share, :] = acc_side[mine, :]
        at = 3 * share
        send[p, at : at + 8, :] = jnp.broadcast_to(gone, (8, LANES))
        send[p, at + 8 : at + 8 + HEAD, :] = out_sum


def finish_kernel(
    critic_in,
    actor_in,
    old,
    a_one,
    a_bias_one,
    a_two,
    a_bias_two,
    a_three,
    a_bias_three,
    c_one,
    c_bias_one,
    c_two,
    c_bias_two,
    c_three,
    c_bias_three,
    g_alpha,
    new,
):
    peers = critic_in.shape[0]
    share = HID // peers
    depth = old.shape[0]

    def total(ref, start, size):
        value = ref[0, start : start + size, :]
        for p in range(1, peers):
            value = value + ref[p, start : start + size, :]
        return value

    at = 5 * share
    table = total(critic_in, at, depth)
    new[...] = jnp.where(table > 0.0, table, old[...])
    at += depth
    sums = total(critic_in, at, 8)
    least = critic_in[0, at + 1 : at + 2, :]
    for p in range(1, peers):
        least = jnp.minimum(least, critic_in[p, at + 1 : at + 2, :])
    actor_scale = 1.0 / sums[0:1, :]
    critic_scale = actor_scale * jnp.exp(BETA * jnp.log(least))
    for k in range(2):
        for t in range(2):
            c_two[k, :, t * LANES : (t + 1) * LANES] = critic_scale * total(
                critic_in, (2 * k + t) * share, share
            )
    small = jnp.transpose(critic_scale * total(critic_in, 4 * share, share))
    for k in range(2):
        for j in range(JOIN - 1):
            c_one[j, k : k + 1, :] = small[k * JOIN + j : k * JOIN + j + 1, :]
        c_bias_one[k : k + 1, :] = small[k * JOIN + JOIN - 1 : k * JOIN + JOIN, :]
        c_bias_two[k : k + 1, :] = small[48 + k : 49 + k, :]
        c_three[k : k + 1, :] = small[50 + k : 51 + k, :]
    lane = lax.broadcasted_iota(jnp.int32, (1, LANES), 1)
    both = jnp.where(lane == 0, sums[2:3, :], sums[3:4, :])
    c_bias_three[...] = (critic_scale * both)[:, 0:2]
    for t in range(2):
        a_two[:, t * LANES : (t + 1) * LANES] = actor_scale * total(actor_in, t * share, share)
    small = jnp.transpose(actor_scale * total(actor_in, 2 * share, share))
    for j in range(OBS):
        a_one[j] = small[j : j + 1, :]
    a_bias_one[...] = small[JOIN - 1 : JOIN, :]
    for j in range(ACT):
        a_three[j] = small[JOIN + 1 + j : JOIN + 2 + j, :]
        a_three[ACT + j] = small[JOIN + 9 + j : JOIN + 10 + j, :]
    a_bias_two[...] = small[JOIN + HEAD : JOIN + HEAD + 1, :]
    sums = total(actor_in, 3 * share, 8 + HEAD)
    g_alpha[...] = (actor_scale * sums[0:1, :])[:, 0:1]
    biases = jnp.zeros((1, LANES), F32)
    for j in range(ACT):
        biases = jnp.where(lane == j, sums[8 + 1 + j : 8 + 2 + j, :], biases)
        biases = jnp.where(lane == ACT + j, sums[8 + 9 + j : 8 + 10 + j, :], biases)
    a_bias_three[...] = (actor_scale * biases)[:, 0 : 2 * ACT]


SMEM = pl.BlockSpec(memory_space=pltpu.SMEM)
VMEM = pl.BlockSpec(memory_space=pltpu.VMEM)


def shards(
    states,
    actions,
    rewards,
    next_states,
    dones,
    noise_now,
    noise_next,
    probs,
    valid_counts,
    owners,
    slots,
    old_priorities,
    actor_w1,
    actor_b1,
    actor_w2,
    actor_b2,
    actor_w3,
    actor_b3,
    critic_w1,
    critic_b1,
    critic_w2,
    critic_b2,
    critic_w3,
    critic_b3,
    target_w1,
    target_b1,
    target_w2,
    target_b2,
    target_w3,
    target_b3,
    log_alpha,
):
    peers = lax.axis_size("dp")
    share = HID // peers

    def rows(value):
        return value.reshape(-1, LANES)

    states, actions, next_states = rows(states), rows(actions), rows(next_states)
    noise_now, noise_next = rows(noise_now), rows(noise_next)
    rewards, dones, probs = rows(rewards), rows(dones), rows(probs)
    owners, slots, old = rows(owners), rows(slots), rows(old_priorities)
    depth = old.shape[0]
    actor_one = jnp.transpose(actor_w1, (2, 0, 1))
    actor_three = jnp.transpose(actor_w3, (1, 0, 2))
    critic_one = jnp.transpose(critic_w1[0], (2, 0, 1))
    target_one = jnp.transpose(target_w1[0], (2, 0, 1))
    critic_rows = 5 * share + depth + 8
    actor_rows = 3 * share + 8 + HEAD
    params = pltpu.CompilerParams(vmem_limit_bytes=VMEM_LIMIT)
    critic_send, top = pl.pallas_call(
        functools.partial(critic_kernel, peers),
        out_shape=(
            jax.ShapeDtypeStruct((peers, critic_rows, LANES), F32),
            jax.ShapeDtypeStruct((8, LANES), F32),
        ),
        in_specs=[SMEM] * 5 + [VMEM] * 24,
        out_specs=(VMEM, VMEM),
        scratch_shapes=[
            pltpu.VMEM((5, HID, 3 * JOIN), BF16),
            pltpu.VMEM((5, 2, HID, HID), BF16),
            pltpu.VMEM((2, 2, HID, HID), BF16),
            pltpu.VMEM((1, 2, HEAD, HID), BF16),
            pltpu.VMEM((5, HID, LANES), F32),
            pltpu.VMEM((4, HID, LANES), F32),
            pltpu.VMEM((HEAD, LANES), F32),
            pltpu.VMEM((JOIN, CHUNK), F32),
            pltpu.VMEM((JOIN, HID), F32),
            pltpu.VMEM((2, HID, HID), F32),
            pltpu.VMEM((2, HID, 2 * JOIN), F32),
            pltpu.VMEM((4, HID, LANES), F32),
            pltpu.VMEM((peers * depth, 2 * LANES), F32),
            pltpu.VMEM((8, CHUNK), F32),
        ],
        compiler_params=params,
        cost_estimate=pl.CostEstimate(flops=20 * 10**9, bytes_accessed=4 * 10**6, transcendentals=10**7),
        name="critic",
    )(
        valid_counts,
        log_alpha,
        actor_b3,
        critic_b3,
        target_b3,
        states,
        actions,
        rewards,
        next_states,
        dones,
        noise_next,
        probs,
        owners,
        slots,
        actor_one,
        actor_b1,
        actor_w2[0],
        actor_b2,
        actor_three,
        critic_one,
        critic_b1[0],
        critic_w2[0],
        critic_b2[0],
        critic_w3[0],
        target_one,
        target_b1[0],
        target_w2[0],
        target_b2[0],
        target_w3[0],
    )
    critic_in = lax.all_to_all(critic_send, "dp", split_axis=0, concat_axis=0, tiled=True)
    actor_send = pl.pallas_call(
        functools.partial(actor_kernel, peers),
        out_shape=jax.ShapeDtypeStruct((peers, actor_rows, LANES), F32),
        in_specs=[SMEM] * 4 + [VMEM] * 12,
        out_specs=VMEM,
        scratch_shapes=[
            pltpu.VMEM((3, HID, 3 * JOIN), BF16),
            pltpu.VMEM((3, 2, HID, HID), BF16),
            pltpu.VMEM((3, 2, HID, HID), BF16),
            pltpu.VMEM((1, 2, HEAD, HID), BF16),
            pltpu.VMEM((HID, 3 * HEAD), BF16),
            pltpu.VMEM((2, 2, 8, HID), BF16),
            pltpu.VMEM((3, HID, LANES), F32),
            pltpu.VMEM((2, HID, LANES), F32),
            pltpu.VMEM((HEAD, LANES), F32),
            pltpu.VMEM((JOIN, CHUNK), F32),
            pltpu.VMEM((JOIN, HID), F32),
            pltpu.VMEM((HID, HID), F32),
            pltpu.VMEM((HID, 2 * JOIN), F32),
            pltpu.VMEM((HID, 2 * HEAD), F32),
            pltpu.VMEM((HID, LANES), F32),
            pltpu.VMEM((HEAD, LANES), F32),
            pltpu.VMEM((8, CHUNK), F32),
        ],
        compiler_params=params,
        cost_estimate=pl.CostEstimate(flops=20 * 10**9, bytes_accessed=4 * 10**6, transcendentals=10**7),
        name="actor",
    )(
        valid_counts,
        log_alpha,
        actor_b3,
        critic_b3,
        states,
        noise_now,
        actor_one,
        actor_b1,
        actor_w2[0],
        actor_b2,
        actor_three,
        critic_one,
        critic_b1[0],
        critic_w2[0],
        critic_b2[0],
        critic_w3[0],
    )
    actor_in = lax.all_to_all(actor_send, "dp", split_axis=0, concat_axis=0, tiled=True)
    tops = lax.all_to_all(jnp.broadcast_to(top[0:1], (lax.axis_size("seed"), LANES)), "seed", split_axis=0, concat_axis=0, tiled=True)
    best = lax.pmax(jnp.max(tops), "dp")
    shape = jax.ShapeDtypeStruct
    outs = pl.pallas_call(
        finish_kernel,
        out_shape=(
            shape((OBS, 1, share), F32),
            shape((1, share), F32),
            shape((share, HID), F32),
            shape((1, share), F32),
            shape((2 * ACT, 1, share), F32),
            shape((1, 2 * ACT), F32),
            shape((JOIN - 1, 2, share), F32),
            shape((2, share), F32),
            shape((2, share, HID), F32),
            shape((2, share), F32),
            shape((2, share), F32),
            shape((1, 2), F32),
            shape((1, 1), F32),
            shape((depth, LANES), F32),
        ),
        in_specs=[VMEM] * 3,
        out_specs=(VMEM,) * 14,
        compiler_params=params,
        name="finish",
    )(critic_in, actor_in, old)
    return (
        jnp.transpose(outs[0], (1, 2, 0)),
        outs[1],
        outs[2][None],
        outs[3],
        jnp.transpose(outs[4], (1, 0, 2)),
        outs[5],
        jnp.transpose(outs[6], (1, 2, 0))[None],
        outs[7][None],
        outs[8][None],
        outs[9][None],
        outs[10][None],
        outs[11],
        outs[12].reshape(1),
        outs[13].reshape(1, -1),
        best,
    )


def solution(mesh):
    token = P("seed", None, "dp")
    line = P("seed", "dp")
    agent = P("seed")
    placed = (
        (token, token, line, token, line, token, token, line, line, line, line, line)
        + (agent,) * 19
    )
    return jax.shard_map(
        shards,
        mesh=mesh,
        in_specs=placed,
        out_specs=(
            P("seed", "dp", None),
            P("seed", "dp"),
            P("seed", "dp", None),
            P("seed", "dp"),
            P("seed", None, "dp"),
            P("seed", None),
            P("seed", None, "dp", None),
            P("seed", None, "dp"),
            P("seed", None, "dp", None),
            P("seed", None, "dp"),
            P("seed", None, "dp"),
            P("seed", None),
            P("seed"),
            P("seed", "dp"),
            P(),
        ),
        check_vma=False,
    )
```

```python
import functools
import math

import jax
import jax.numpy as jnp
from jax import lax
from jax.experimental import pallas as pl
from jax.experimental.pallas import tpu as pltpu
from jax.sharding import PartitionSpec as P

F32 = jnp.float32
BF16 = jnp.bfloat16
GAMMA = 0.99
STD_LO = -5.0
STD_HI = 2.0
ENTROPY_AIM = -6.0
SOFT_TEMP = 0.1
BETA = 0.4
PRIO_EXP = 0.6
PRIO_EPS = 0.001
HALF_LOG_TAU = 0.5 * math.log(2.0 * math.pi)
LOG_TWO = math.log(2.0)

LANES = 128
OBS = 17
ACT = 6
HID = 256
JOIN = 24
HEAD = 16
CHUNK = 256
GROUP = CHUNK // LANES
STREAMS = 4
STRIDE = STREAMS * GROUP
CRITIC_LIMIT = 56 * 1024 * 1024
ACTOR_LIMIT = 24 * 1024 * 1024
FINISH_LIMIT = 8 * 1024 * 1024


def dot(left, right):
    return jnp.dot(left, right, preferred_element_type=F32)


def dot_t(left, right):
    return lax.dot_general(left, right, (((1,), (1,)), ((), ())), preferred_element_type=F32)


def split(value):
    high = value.astype(BF16)
    low = (value - high.astype(F32)).astype(BF16)
    return high, low


def split_wide(value):
    high = value.astype(BF16).astype(F32)
    return high, value - high


def dot3(weight, value):
    high, low = value
    return dot(weight[0], high) + dot(weight[0], low) + dot(weight[1], high)


def dot3_t(left, right):
    return dot_t(left[0], right[0]) + dot_t(left[0], right[1]) + dot_t(left[1], right[0])


def wide(column):
    return jnp.concatenate([column] * GROUP, axis=1)


def stack_join(value):
    high, low = split_wide(value)
    return jnp.concatenate([high, low, high], axis=0).astype(BF16)


def stack_weight(value):
    high, low = split_wide(value)
    return jnp.transpose(jnp.concatenate([high, high, low], axis=0)).astype(BF16)


def activate(half):
    return half * (1.0 + jnp.tanh(half))


def activate_slope(half):
    bent = jnp.tanh(half)
    rise = 1.0 + bent
    hidden = half * rise
    return hidden, rise + hidden * (1.0 - bent)


def interleave(tasks):
    free = {"mxu": 0, "vpu": 0}
    times = {}
    queue = []

    def advance(task, now):
        generator, known = task
        seen = set(known)
        asked = next(generator, None)
        for name in known:
            if name not in seen:
                times[(id(known), name)] = now
        if asked is not None:
            queue.append((now, task, asked))

    for task in tasks:
        advance(task, 0)
    while queue:
        best = None
        for place, (ready, task, (unit, cost)) in enumerate(queue):
            if unit is None:
                if cost not in task[1]:
                    continue
                start = max(ready, times[(id(task[1]), cost)])
            else:
                start = max(ready, free[unit])
            if best is None or start < best[0]:
                best = (start, place)
        start, place = best
        ready, task, (unit, cost) = queue.pop(place)
        if unit is None:
            advance(task, start)
        else:
            free[unit] = start + cost
            advance(task, start + cost)


def soft_min(first, second):
    return jnp.minimum(first, second) - SOFT_TEMP * jnp.log(
        1.0 + jnp.exp(-jnp.abs(first - second) / SOFT_TEMP)
    )


def squash(head, noise):
    means, bend = head[:8], jnp.tanh(head[8:])
    log_std = STD_LO + 0.5 * (STD_HI - STD_LO) * (bend + 1.0)
    spread = jnp.exp(log_std) * noise
    pre = means + spread
    action = jnp.tanh(pre)
    size = jnp.abs(pre)
    log_jac = 2.0 * (LOG_TWO - size - jnp.log(1.0 + jnp.exp(-2.0 * size)))
    row = lax.broadcasted_iota(jnp.int32, pre.shape, 0)
    inside = (row >= 1) & (row <= ACT)
    terms = jnp.where(inside, -0.5 * noise * noise - log_std - HALF_LOG_TAU - log_jac, 0.0)
    return action, jnp.sum(terms, axis=0, keepdims=True), spread, bend


def load_rows(ref, count, block):
    blocks = ref.shape[0] // count
    return ref[pl.ds(block, count, stride=blocks), :]


def load_chunk(ref, count, first):
    return jnp.concatenate([load_rows(ref, count, first + g) for g in range(GROUP)], axis=1)


def load_row(ref, first):
    return jnp.concatenate([ref[pl.ds(first + g, 1), :] for g in range(GROUP)], axis=1)


def fill_join(join, obs_ref, act_ref, first):
    join[0:OBS, :] = load_chunk(obs_ref, OBS, first)
    if act_ref is not None:
        join[OBS : OBS + ACT, :] = load_chunk(act_ref, ACT, first)
    join[JOIN - 1 : JOIN, :] = jnp.ones((1, CHUNK), F32)


def with_action(join, action):
    row = lax.broadcasted_iota(jnp.int32, action.shape, 0)
    inside = (row >= 1) & (row <= ACT)
    return jnp.concatenate([join[:16], jnp.where(inside, action, join[16:])], axis=0)


def first_weights(weight_ref, bias_row, index, scratch):
    rows = weight_ref.shape[0]
    scratch[...] = jnp.zeros_like(scratch)
    scratch[0:rows, :] = weight_ref[:, index, :]
    scratch[JOIN - 1 : JOIN, :] = bias_row
    return stack_weight(0.5 * scratch[...])


def store_split(ref, index, value):
    high, low = split(value)
    ref[index, 0] = high
    ref[index, 1] = low


def pair(ref, index):
    return ref[index, 0], ref[index, 1]


def column(row):
    return jnp.transpose(jnp.broadcast_to(row, (LANES, row.shape[1])))


def back_weights(weight, scale):
    both = jnp.concatenate([scale, scale], axis=1)
    return jnp.transpose(0.25 * both * weight)


def head_weights(weight_ref, scratch):
    scratch[...] = jnp.zeros_like(scratch)
    scratch[1 : 1 + ACT, :] = weight_ref[0:ACT, 0, :]
    scratch[9 : 9 + ACT, :] = weight_ref[ACT : 2 * ACT, 0, :]
    return scratch[...]


def head_bias(bias_ref):
    row = lax.broadcasted_iota(jnp.int32, (HEAD, LANES), 0)
    out = jnp.zeros((HEAD, LANES), F32)
    for k in range(ACT):
        out = jnp.where(row == 1 + k, bias_ref[0, k], out)
        out = jnp.where(row == 9 + k, bias_ref[0, ACT + k], out)
    return out


def fold(value):
    total = value[:, :LANES]
    for g in range(1, GROUP):
        total = total + value[:, g * LANES : (g + 1) * LANES]
    return total


def valid_lanes(first, count):
    lane = lax.broadcasted_iota(jnp.int32, (1, CHUNK), 1)
    return lane + first * LANES < count


def spread_row(value):
    return jnp.broadcast_to(value, (1, LANES))


def critic_kernel(
    peers,
    count_ref,
    temper_ref,
    actor_b3,
    critic_b3,
    target_b3,
    states,
    actions,
    rewards,
    next_states,
    dones,
    noise_next,
    probs,
    owners,
    slots,
    actor_w1,
    actor_b1,
    actor_w2,
    actor_b2,
    actor_w3,
    critic_w1,
    critic_b1,
    critic_w2,
    critic_b2,
    critic_w3,
    target_w1,
    target_b1,
    target_w2,
    target_b2,
    target_w3,
    send,
    one,
    two,
    back,
    head,
    bias_two,
    last,
    wide_bias,
    join,
    turn,
    acc_two,
    acc_one,
    acc_side,
    acc_table,
    acc_row,
):
    count = jnp.max(count_ref[...].astype(F32)).astype(jnp.int32)
    alpha = jnp.exp(temper_ref[...])
    share = HID // peers
    depth = acc_table.shape[0] // peers
    one[0] = first_weights(actor_w1, actor_b1[...], 0, turn)
    for k in range(2):
        one[1 + k] = first_weights(target_w1, target_b1[k : k + 1, :], k, turn)
        one[3 + k] = first_weights(critic_w1, critic_b1[k : k + 1, :], k, turn)
    store_split(two, 0, 0.5 * actor_w2[...])
    bias_two[0] = column(0.5 * actor_b2[...])
    for k in range(2):
        store_split(two, 1 + k, 0.5 * target_w2[k])
        store_split(two, 3 + k, 0.5 * critic_w2[k])
        bias_two[1 + k] = column(0.5 * target_b2[k : k + 1, :])
        bias_two[3 + k] = column(0.5 * critic_b2[k : k + 1, :])
        last[k] = column(target_w3[k : k + 1, :])
        last[2 + k] = column(critic_w3[k : k + 1, :])
        store_split(back, k, back_weights(critic_w2[k], last[2 + k]))
    store_split(head, 0, head_weights(actor_w3, turn.at[0:HEAD]))
    wide_bias[...] = head_bias(actor_b3)
    acc_two[...] = jnp.zeros_like(acc_two)
    acc_one[...] = jnp.zeros_like(acc_one)
    acc_side[...] = jnp.zeros_like(acc_side)
    acc_table[...] = jnp.zeros_like(acc_table)
    acc_row[...] = jnp.zeros_like(acc_row)

    def next_action(first, known, lane):
        yield "mxu", 64
        fill_join(join.at[lane], next_states, None, first)
        join[lane, OBS : OBS + ACT, :] = jnp.zeros((ACT, CHUNK), F32)
        nexts = join[lane]
        half = dot(one[0], stack_join(nexts))
        yield "vpu", 110
        hidden = split(activate(half))
        yield "mxu", 192
        half = dot3(pair(two, 0), hidden)
        yield "vpu", 130
        hidden = split(activate(half + wide(bias_two[0])))
        yield "mxu", 128
        out = dot3(pair(head, 0), hidden)
        yield "vpu", 100
        join[lane, OBS : OBS + ACT, :] = load_chunk(noise_next, ACT, first)
        action, known["logp"], _, _ = squash(out + wide(wide_bias[...]), join[lane, 16:24, :])
        known["given_next"] = stack_join(with_action(nexts, action))

    def target_value(first, known, k):
        yield None, "given_next"
        yield "mxu", 64
        half = dot(one[1 + k], known["given_next"])
        yield "vpu", 110
        hidden = split(activate(half))
        yield "mxu", 192
        half = dot3(pair(two, 1 + k), hidden)
        yield "vpu", 120
        hidden = activate(half + wide(bias_two[1 + k]))
        total = jnp.sum(hidden * wide(last[k]), axis=0, keepdims=True)
        known["next", k] = total + target_b3[0, k]

    def target_row(first, known):
        yield None, "logp"
        yield None, ("next", 0)
        yield None, ("next", 1)
        yield "vpu", 40
        keep = GAMMA * (1.0 - load_row(dones, first).astype(F32))
        worth = soft_min(known["next", 0], known["next", 1]) - alpha * known["logp"]
        known["target"] = load_row(rewards, first) + keep * worth
        known["valid"] = valid_lanes(first, count)
        coef = jnp.exp(-BETA * jnp.log(load_row(probs, first)))
        known["coef"] = jnp.where(known["valid"], coef, 0.0)

    def given_now(first, known, lane):
        yield "vpu", 20
        fill_join(join.at[lane], states, actions, first)
        known["given"] = stack_join(join[lane])

    def critic(first, known, k):
        yield None, "given"
        given = known["given"]
        yield "mxu", 64
        half = dot(one[3 + k], given)
        yield "vpu", 160
        hidden, slope_one = activate_slope(half)
        hidden_one = split(hidden)
        yield "mxu", 192
        half = dot3(pair(two, 3 + k), hidden_one)
        yield "vpu", 170
        hidden, slope_two = activate_slope(half + wide(bias_two[3 + k]))
        value = jnp.sum(hidden * wide(last[2 + k]), axis=0, keepdims=True) + critic_b3[0, k]
        yield None, "target"
        yield "vpu", 160
        error = value - known["target"]
        known["error", k] = error
        scaled = known["coef"] * error
        grad = scaled * slope_two
        acc_side[k] += fold(grad)
        acc_side[2 + k] += fold(scaled * hidden)
        acc_row[k : k + 1, :] += scaled
        grad_two = split(grad)
        yield "mxu", 192
        half = dot3(pair(back, k), grad_two)
        yield "vpu", 90
        grad_one = split(half * slope_one)
        yield "mxu", 192
        acc_two[k] += dot3_t(grad_two, hidden_one)
        yield "mxu", 128
        acc_one[k] += dot_t(grad_one[0], given[:48]) + dot_t(grad_one[1], given[:48])

    def priorities(first, known):
        yield None, ("error", 0)
        yield None, ("error", 1)
        yield "vpu", 120
        delta = 0.5 * (known["error", 0] + known["error", 1])
        priority = jnp.exp(PRIO_EXP * jnp.log(jnp.abs(delta) + PRIO_EPS))
        priority = jnp.where(known["valid"], priority, 0.0)
        acc_row[2:3, :] = jnp.maximum(acc_row[2:3, :], priority)
        slot = load_row(slots, first)
        place = load_row(owners, first) * depth + lax.shift_right_logical(slot, 7)
        lane = slot & (LANES - 1)
        rows = acc_table.shape[0]
        row_hit = lax.broadcasted_iota(jnp.int32, (rows, CHUNK), 0) == place
        lane_hit = lax.broadcasted_iota(jnp.int32, (LANES, CHUNK), 0) == lane
        high, low = split_wide(priority)
        picked = jnp.concatenate(
            [jnp.where(lane_hit, high, 0.0), jnp.where(lane_hit, low, 0.0)], axis=0
        ).astype(BF16)
        hits = jnp.where(row_hit, 1.0, 0.0).astype(BF16)
        yield "mxu", 64
        acc_table[...] += dot_t(hits, picked)

    def step(index, carry):
        tasks = []
        for lane in range(STREAMS):
            first = index * STRIDE + lane * GROUP
            known = {}
            tasks.append((next_action(first, known, 2 * lane), known))
            tasks.append((given_now(first, known, 2 * lane + 1), known))
            for k in range(2):
                tasks.append((critic(first, known, k), known))
            for k in range(2):
                tasks.append((target_value(first, known, k), known))
            tasks.append((target_row(first, known), known))
            tasks.append((priorities(first, known), known))
        interleave(tasks)
        return carry

    span = STREAMS * CHUNK
    lax.fori_loop(0, (count + span - 1) // span, step, 0)

    for k in range(2):
        acc_side[k] = 0.5 * last[2 + k] * acc_side[k]
    side = [jnp.sum(acc_side[k], axis=1, keepdims=True) for k in range(4)]
    small = [acc_one[k][:, :JOIN] + acc_one[k][:, JOIN:] for k in range(2)]
    joined = jnp.concatenate(small + side + [jnp.zeros((HID, LANES - 52), F32)], axis=1)
    acc_side[0] = joined
    lane = lax.broadcasted_iota(jnp.int32, probs.shape, 1)
    row = lax.broadcasted_iota(jnp.int32, probs.shape, 0)
    least = jnp.min(jnp.where(row * LANES + lane < count, probs[...], 1.0), keepdims=True)
    best = jnp.max(acc_row[2:3, :], keepdims=True)
    sums = jnp.concatenate(
        [
            jnp.full((1, LANES), count.astype(F32)),
            spread_row(least),
            spread_row(jnp.sum(acc_row[0:1, :], keepdims=True)),
            spread_row(jnp.sum(acc_row[1:2, :], keepdims=True)),
            spread_row(best),
            jnp.zeros((3, LANES), F32),
        ],
        axis=0,
    )
    table = acc_table[:, :LANES] + acc_table[:, LANES:]
    for p in range(peers):
        mine = slice(p * share, (p + 1) * share)
        at = 0
        for k in range(2):
            for t in range(2):
                block = acc_two[k, mine, t * LANES : (t + 1) * LANES]
                send[p, at : at + share, :] = 0.5 * last[2 + k, mine, :] * block
                at += share
        send[p, at : at + share, :] = acc_side[0, mine, :]
        at += share
        send[p, at : at + depth, :] = table[p * depth : (p + 1) * depth]
        at += depth
        send[p, at : at + 8, :] = sums


def actor_kernel(
    peers,
    core_ref,
    count_ref,
    temper_ref,
    actor_b3,
    critic_b3,
    states,
    noise_now,
    actor_w1,
    actor_b1,
    actor_w2,
    actor_b2,
    actor_w3,
    critic_w1,
    critic_b1,
    critic_w2,
    critic_b2,
    critic_w3,
    keep,
    give,
    one,
    two,
    back,
    head,
    head_back,
    entry,
    bias_two,
    last,
    wide_bias,
    join,
    turn,
    acc_two,
    acc_one,
    acc_head,
    acc_side,
    acc_out,
    acc_row,
):
    count = jnp.max(count_ref[...].astype(F32)).astype(jnp.int32)
    alpha = jnp.exp(temper_ref[...])
    share = HID // peers
    one[0] = first_weights(actor_w1, actor_b1[...], 0, turn)
    for k in range(2):
        one[1 + k] = first_weights(critic_w1, critic_b1[k : k + 1, :], k, turn)
        store_split(entry, k, turn[16:24, :])
    store_split(two, 0, 0.5 * actor_w2[...])
    store_split(back, 0, jnp.transpose(0.5 * actor_w2[...]))
    bias_two[0] = column(0.5 * actor_b2[...])
    for k in range(2):
        store_split(two, 1 + k, 0.5 * critic_w2[k])
        bias_two[1 + k] = column(0.5 * critic_b2[k : k + 1, :])
        last[k] = column(critic_w3[k : k + 1, :])
        store_split(back, 1 + k, back_weights(critic_w2[k], last[k]))
    final = head_weights(actor_w3, turn.at[0:HEAD])
    store_split(head, 0, final)
    head_back[...] = stack_weight(0.5 * final)
    wide_bias[...] = head_bias(actor_b3)
    acc_two[...] = jnp.zeros_like(acc_two)
    acc_one[...] = jnp.zeros_like(acc_one)
    acc_head[...] = jnp.zeros_like(acc_head)
    acc_side[...] = jnp.zeros_like(acc_side)
    acc_out[...] = jnp.zeros_like(acc_out)
    acc_row[...] = jnp.zeros_like(acc_row)

    row = lax.broadcasted_iota(jnp.int32, (8, CHUNK), 0)
    inside = (row >= 1) & (row <= ACT)

    def forward(first, known, lane):
        yield "mxu", 64
        valid = valid_lanes(first, count)
        known["mask"] = jnp.where(valid, 1.0, 0.0)
        fill_join(join.at[lane], states, noise_now, first)
        noise = join[lane, 16:24, :]
        tail = jnp.where(inside, 0.0, noise)
        given = stack_join(jnp.concatenate([join[lane, 0:16, :], tail], axis=0))
        half = dot(one[0], given)
        yield "vpu", 160
        hidden, slope_one = activate_slope(half)
        hidden_one = split(hidden)
        yield "mxu", 192
        half = dot3(pair(two, 0), hidden_one)
        yield "vpu", 170
        hidden, slope_two = activate_slope(half + wide(bias_two[0]))
        hidden_two = split(hidden)
        yield "mxu", 128
        out = dot3(pair(head, 0), hidden_two)
        yield "vpu", 100
        action, logp, spread, bend = squash(out + wide(wide_bias[...]), noise)
        acc_row[0:1, :] += known["mask"] * (logp + ENTROPY_AIM)
        known["fresh"] = stack_join(with_action(join[lane], action))
        yield None, "push"
        yield "vpu", 60
        push = known["push"]
        pull = alpha * known["mask"]
        grad_pre = jnp.where(inside, 2.0 * pull * action + push * (1.0 - action * action), 0.0)
        grad_std = jnp.where(inside, grad_pre * spread - pull, 0.0)
        grad_bend = 0.5 * (STD_HI - STD_LO) * grad_std * (1.0 - bend * bend)
        grad_out = jnp.concatenate([grad_pre, grad_bend], axis=0)
        acc_out[...] += fold(grad_out)
        outs = stack_join(grad_out)
        yield "mxu", 64
        half = dot(head_back[...], outs)
        yield "vpu", 100
        grad = half * slope_two
        acc_side[...] += fold(grad)
        grad_two = split(grad)
        yield "mxu", 192
        half = dot3(pair(back, 0), grad_two)
        yield "vpu", 90
        grad_one = split(half * slope_one)
        yield "mxu", 128
        acc_head[...] += dot_t(hidden_two[0], outs[:32]) + dot_t(hidden_two[1], outs[:32])
        yield "mxu", 192
        acc_two[...] += dot3_t(grad_two, hidden_one)
        yield "mxu", 128
        acc_one[...] += dot_t(grad_one[0], given[:48]) + dot_t(grad_one[1], given[:48])

    def critic(first, known, k):
        yield None, "fresh"
        yield "mxu", 64
        half = dot(one[1 + k], known["fresh"])
        yield "vpu", 160
        hidden, slope_one = activate_slope(half)
        hidden_one = split(hidden)
        yield "mxu", 192
        half = dot3(pair(two, 1 + k), hidden_one)
        yield "vpu", 220
        hidden, slope_two = activate_slope(half + wide(bias_two[1 + k]))
        value = jnp.sum(hidden * wide(last[k]), axis=0, keepdims=True) + critic_b3[0, k]
        known["value", k] = value
        grad_two = split(slope_two)
        yield "mxu", 192
        half = dot3(pair(back, 1 + k), grad_two)
        yield "vpu", 90
        grad_one = split(half * slope_one)
        yield "mxu", 128
        known["pull", k] = dot3(pair(entry, k), grad_one)

    def mix(first, known):
        for k in range(2):
            yield None, ("value", k)
            yield None, ("pull", k)
        yield "vpu", 10
        gap = (known["value", 1] - known["value", 0]) / SOFT_TEMP
        lean = 0.5 * jnp.tanh(0.5 * gap)
        parts = (0.5 + lean) * known["pull", 0] + (0.5 - lean) * known["pull", 1]
        known["push"] = -known["mask"] * parts

    def step(index, carry):
        tasks = []
        for lane in range(STREAMS):
            first = index * STRIDE + lane * GROUP
            known = {}
            tasks.append((forward(first, known, lane), known))
            for k in range(2):
                tasks.append((critic(first, known, k), known))
            tasks.append((mix(first, known), known))
        interleave(tasks)
        return carry

    span = STREAMS * CHUNK
    lax.fori_loop(0, (count + span - 1) // span, step, 0)

    joined = jnp.concatenate(
        [
            acc_one[:, :JOIN] + acc_one[:, JOIN:],
            acc_head[:, :HEAD] + acc_head[:, HEAD:],
            jnp.sum(acc_side[...], axis=1, keepdims=True),
            jnp.zeros((HID, LANES - JOIN - HEAD - 1), F32),
        ],
        axis=1,
    )
    acc_side[...] = joined
    gone = -jnp.sum(acc_row[0:1, :], keepdims=True)
    out_sum = jnp.broadcast_to(jnp.sum(acc_out[...], axis=1, keepdims=True), (HEAD, LANES))
    core = core_ref[0]
    for side, part in ((keep, core), (give, 1 - core)):
        for q in range(peers // 2):
            mine = pl.ds(pl.multiple_of((2 * q + part) * share, 8), share)
            side[q, 0:share, :] = acc_two[mine, 0:LANES]
            side[q, share : 2 * share, :] = acc_two[mine, LANES : 2 * LANES]
            side[q, 2 * share : 3 * share, :] = acc_side[mine, :]
            at = 3 * share
            side[q, at : at + 8, :] = jnp.broadcast_to(gone, (8, LANES))
            side[q, at + 8 : at + 8 + HEAD, :] = out_sum


def finish_kernel(
    critic_in,
    actor_kept,
    actor_in,
    best_kept,
    best_in,
    old,
    a_one,
    a_bias_one,
    a_two,
    a_bias_two,
    a_three,
    a_bias_three,
    c_one,
    c_bias_one,
    c_two,
    c_bias_two,
    c_three,
    c_bias_three,
    g_alpha,
    new,
    best,
):
    peers = critic_in.shape[0]
    share = HID // peers
    depth = old.shape[0]

    def actor_total(start, size):
        return actor_kept[start : start + size, :] + actor_in[start : start + size, :]

    def total(ref, start, size):
        value = ref[0, start : start + size, :]
        for p in range(1, peers):
            value = value + ref[p, start : start + size, :]
        return value

    at = 5 * share
    table = total(critic_in, at, depth)
    new[...] = jnp.where(table > 0.0, table, old[...])
    at += depth
    sums = total(critic_in, at, 8)
    least = critic_in[0, at + 1 : at + 2, :]
    for p in range(1, peers):
        least = jnp.minimum(least, critic_in[p, at + 1 : at + 2, :])
    actor_scale = 1.0 / sums[0:1, :]
    critic_scale = actor_scale * jnp.exp(BETA * jnp.log(least))
    for k in range(2):
        for t in range(2):
            c_two[k, :, t * LANES : (t + 1) * LANES] = critic_scale * total(
                critic_in, (2 * k + t) * share, share
            )
    small = jnp.transpose(critic_scale * total(critic_in, 4 * share, share))
    for k in range(2):
        for j in range(JOIN - 1):
            c_one[j, k : k + 1, :] = small[k * JOIN + j : k * JOIN + j + 1, :]
        c_bias_one[k : k + 1, :] = small[k * JOIN + JOIN - 1 : k * JOIN + JOIN, :]
        c_bias_two[k : k + 1, :] = small[48 + k : 49 + k, :]
        c_three[k : k + 1, :] = small[50 + k : 51 + k, :]
    lane = lax.broadcasted_iota(jnp.int32, (1, LANES), 1)
    both = jnp.where(lane == 0, sums[2:3, :], sums[3:4, :])
    c_bias_three[...] = (critic_scale * both)[:, 0:2]
    for t in range(2):
        a_two[:, t * LANES : (t + 1) * LANES] = actor_scale * actor_total(t * share, share)
    small = jnp.transpose(actor_scale * actor_total(2 * share, share))
    for j in range(OBS):
        a_one[j] = small[j : j + 1, :]
    a_bias_one[...] = small[JOIN - 1 : JOIN, :]
    for j in range(ACT):
        a_three[j] = small[JOIN + 1 + j : JOIN + 2 + j, :]
        a_three[ACT + j] = small[JOIN + 9 + j : JOIN + 10 + j, :]
    a_bias_two[...] = small[JOIN + HEAD : JOIN + HEAD + 1, :]
    sums = actor_total(3 * share, 8 + HEAD)
    g_alpha[...] = (actor_scale * sums[0:1, :])[:, 0:1]
    biases = jnp.zeros((1, LANES), F32)
    for j in range(ACT):
        biases = jnp.where(lane == j, sums[8 + 1 + j : 8 + 2 + j, :], biases)
        biases = jnp.where(lane == ACT + j, sums[8 + 9 + j : 8 + 10 + j, :], biases)
    a_bias_three[...] = (actor_scale * biases)[:, 0 : 2 * ACT]
    best[...] = jnp.maximum(best_kept[...], best_in[...])[:, 0:1]


SMEM = pl.BlockSpec(memory_space=pltpu.SMEM)
VMEM = pl.BlockSpec(memory_space=pltpu.VMEM)


def shards(
    states,
    actions,
    rewards,
    next_states,
    dones,
    noise_now,
    noise_next,
    probs,
    valid_counts,
    owners,
    slots,
    old_priorities,
    actor_w1,
    actor_b1,
    actor_w2,
    actor_b2,
    actor_w3,
    actor_b3,
    critic_w1,
    critic_b1,
    critic_w2,
    critic_b2,
    critic_w3,
    critic_b3,
    target_w1,
    target_b1,
    target_w2,
    target_b2,
    target_w3,
    target_b3,
    log_alpha,
):
    peers = lax.axis_size("dp")
    me = lax.axis_index("dp")
    share = HID // peers

    def rows(value):
        return value.reshape(-1, LANES)

    states, actions, next_states = rows(states), rows(actions), rows(next_states)
    noise_now, noise_next = rows(noise_now), rows(noise_next)
    rewards, dones, probs = rows(rewards), rows(dones), rows(probs)
    owners, slots, old = rows(owners), rows(slots), rows(old_priorities)
    depth = old.shape[0]
    actor_one = jnp.transpose(actor_w1, (2, 0, 1))
    actor_three = jnp.transpose(actor_w3, (1, 0, 2))
    critic_one = jnp.transpose(critic_w1[0], (2, 0, 1))
    target_one = jnp.transpose(target_w1[0], (2, 0, 1))
    critic_rows = 5 * share + depth + 8
    actor_rows = 3 * share + 8 + HEAD
    critic_send = pl.pallas_call(
        functools.partial(critic_kernel, peers),
        out_shape=jax.ShapeDtypeStruct((peers, critic_rows, LANES), F32),
        in_specs=[VMEM] * 2 + [SMEM] * 3 + [VMEM] * 24,
        out_specs=VMEM,
        scratch_shapes=[
            pltpu.VMEM((5, HID, 3 * JOIN), BF16),
            pltpu.VMEM((5, 2, HID, HID), BF16),
            pltpu.VMEM((2, 2, HID, HID), BF16),
            pltpu.VMEM((1, 2, HEAD, HID), BF16),
            pltpu.VMEM((5, HID, LANES), F32),
            pltpu.VMEM((4, HID, LANES), F32),
            pltpu.VMEM((HEAD, LANES), F32),
            pltpu.VMEM((2 * STREAMS, JOIN, CHUNK), F32),
            pltpu.VMEM((JOIN, HID), F32),
            pltpu.VMEM((2, HID, HID), F32),
            pltpu.VMEM((2, HID, 2 * JOIN), F32),
            pltpu.VMEM((4, HID, LANES), F32),
            pltpu.VMEM((peers * depth, 2 * LANES), F32),
            pltpu.VMEM((8, CHUNK), F32),
        ],
        compiler_params=pltpu.CompilerParams(vmem_limit_bytes=CRITIC_LIMIT),
        cost_estimate=pl.CostEstimate(flops=20 * 10**9, bytes_accessed=4 * 10**6, transcendentals=10**7),
        name="critic",
    )(
        valid_counts,
        log_alpha.reshape(1, 1),
        actor_b3,
        critic_b3,
        target_b3,
        states,
        actions,
        rewards,
        next_states,
        dones,
        noise_next,
        probs,
        owners,
        slots,
        actor_one,
        actor_b1,
        actor_w2[0],
        actor_b2,
        actor_three,
        critic_one,
        critic_b1[0],
        critic_w2[0],
        critic_b2[0],
        critic_w3[0],
        target_one,
        target_b1[0],
        target_w2[0],
        target_b2[0],
        target_w3[0],
    )
    critic_in = lax.all_to_all(critic_send, "dp", split_axis=0, concat_axis=0, tiled=True)
    kept, given = pl.pallas_call(
        functools.partial(actor_kernel, peers),
        out_shape=(jax.ShapeDtypeStruct((peers // 2, actor_rows, LANES), F32),) * 2,
        in_specs=[SMEM] + [VMEM] * 2 + [SMEM] * 2 + [VMEM] * 12,
        out_specs=(VMEM, VMEM),
        scratch_shapes=[
            pltpu.VMEM((3, HID, 3 * JOIN), BF16),
            pltpu.VMEM((3, 2, HID, HID), BF16),
            pltpu.VMEM((3, 2, HID, HID), BF16),
            pltpu.VMEM((1, 2, HEAD, HID), BF16),
            pltpu.VMEM((HID, 3 * HEAD), BF16),
            pltpu.VMEM((2, 2, 8, HID), BF16),
            pltpu.VMEM((3, HID, LANES), F32),
            pltpu.VMEM((2, HID, LANES), F32),
            pltpu.VMEM((HEAD, LANES), F32),
            pltpu.VMEM((STREAMS, JOIN, CHUNK), F32),
            pltpu.VMEM((JOIN, HID), F32),
            pltpu.VMEM((HID, HID), F32),
            pltpu.VMEM((HID, 2 * JOIN), F32),
            pltpu.VMEM((HID, 2 * HEAD), F32),
            pltpu.VMEM((HID, LANES), F32),
            pltpu.VMEM((HEAD, LANES), F32),
            pltpu.VMEM((8, CHUNK), F32),
        ],
        compiler_params=pltpu.CompilerParams(vmem_limit_bytes=ACTOR_LIMIT),
        cost_estimate=pl.CostEstimate(flops=20 * 10**9, bytes_accessed=4 * 10**6, transcendentals=10**7),
        name="actor",
    )(
        (me % 2).reshape(1),
        valid_counts,
        log_alpha.reshape(1, 1),
        actor_b3,
        critic_b3,
        states,
        noise_now,
        actor_one,
        actor_b1,
        actor_w2[0],
        actor_b2,
        actor_three,
        critic_one,
        critic_b1[0],
        critic_w2[0],
        critic_b2[0],
        critic_w3[0],
    )
    at = 5 * share + depth + 4
    best = jnp.max(critic_in[:, at : at + 1, :], axis=0)
    best_in = best
    agents = lax.axis_size("seed")
    spans = (agents - 1).bit_length()
    bits = (peers - 1).bit_length()
    actor_in = lax.ppermute(given, "dp", [(k, k ^ 1) for k in range(peers)])
    for bit in range(1, max(bits, 1 + spans)):
        if bit < bits:
            both = (kept + actor_in).reshape(-1, 2, actor_rows, LANES)
            mine = (me >> bit) & 1
            kept = lax.dynamic_index_in_dim(both, mine, 1, False)
            given = lax.dynamic_index_in_dim(both, 1 - mine, 1, False)
            actor_in = lax.ppermute(given, "dp", [(k, k ^ (1 << bit)) for k in range(peers)])
        if bit <= spans:
            best = jnp.maximum(best, best_in)
            best_in = lax.ppermute(best, "seed", [(k, k ^ (1 << (bit - 1))) for k in range(agents)])
        actor_in, best_in = lax.optimization_barrier((actor_in, best_in))
    shape = jax.ShapeDtypeStruct
    outs = pl.pallas_call(
        finish_kernel,
        out_shape=(
            shape((OBS, 1, share), F32),
            shape((1, share), F32),
            shape((share, HID), F32),
            shape((1, share), F32),
            shape((2 * ACT, 1, share), F32),
            shape((1, 2 * ACT), F32),
            shape((JOIN - 1, 2, share), F32),
            shape((2, share), F32),
            shape((2, share, HID), F32),
            shape((2, share), F32),
            shape((2, share), F32),
            shape((1, 2), F32),
            shape((1, 1), F32),
            shape((depth, LANES), F32),
            shape((1, 1), F32),
        ),
        in_specs=[VMEM] * 6,
        out_specs=(VMEM,) * 15,
        compiler_params=pltpu.CompilerParams(vmem_limit_bytes=FINISH_LIMIT),
        name="finish",
    )(critic_in, kept[0], actor_in[0], best, best_in, old)
    return (
        jnp.transpose(outs[0], (1, 2, 0)),
        outs[1],
        outs[2][None],
        outs[3],
        jnp.transpose(outs[4], (1, 0, 2)),
        outs[5],
        jnp.transpose(outs[6], (1, 2, 0))[None],
        outs[7][None],
        outs[8][None],
        outs[9][None],
        outs[10][None],
        outs[11],
        outs[12].reshape(1),
        outs[13].reshape(1, -1),
        outs[14].reshape(()),
    )


def solution(mesh):
    token = P("seed", None, "dp")
    line = P("seed", "dp")
    agent = P("seed")
    placed = (
        (token, token, line, token, line, token, token, line, line, line, line, line)
        + (agent,) * 19
    )
    return jax.shard_map(
        shards,
        mesh=mesh,
        in_specs=placed,
        out_specs=(
            P("seed", "dp", None),
            P("seed", "dp"),
            P("seed", "dp", None),
            P("seed", "dp"),
            P("seed", None, "dp"),
            P("seed", None),
            P("seed", None, "dp", None),
            P("seed", None, "dp"),
            P("seed", None, "dp", None),
            P("seed", None, "dp"),
            P("seed", None, "dp"),
            P("seed", None),
            P("seed"),
            P("seed", "dp"),
            P(),
        ),
        check_vma=False,
    )
```

```python
import functools
import math

import jax
import jax.numpy as jnp
from jax import lax
from jax.experimental import pallas as pl
from jax.experimental.pallas import tpu as pltpu
from jax.sharding import PartitionSpec as P

F32 = jnp.float32
BF16 = jnp.bfloat16
GAMMA = 0.99
STD_LO = -5.0
STD_HI = 2.0
ENTROPY_AIM = -6.0
SOFT_TEMP = 0.1
BETA = 0.4
PRIO_EXP = 0.6
PRIO_EPS = 0.001
HALF_LOG_TAU = 0.5 * math.log(2.0 * math.pi)
LOG_TWO = math.log(2.0)

LANES = 128
OBS = 17
ACT = 6
HID = 256
JOIN = 24
OUT_LANE = 48
HEAD_ROW = 3 * JOIN
REST_ROW = HEAD_ROW + 16
BIAS_ROW = REST_ROW + 8
SMALL = BIAS_ROW + 16
HEAD = 16
CRITIC_BLOCKS, CRITIC_STREAMS, CRITIC_LAG = 4, 4, 2000
ACTOR_BLOCKS, ACTOR_STREAMS = 8, 2
CRITIC_LIMIT = 56 * 1024 * 1024
ACTOR_LIMIT = 36 * 1024 * 1024
FINISH_LIMIT = 8 * 1024 * 1024


def dot(left, right):
    return jnp.dot(left, right, preferred_element_type=F32)


def dot_t(left, right):
    return lax.dot_general(left, right, (((1,), (1,)), ((), ())), preferred_element_type=F32)


def split(value):
    high = value.astype(BF16)
    low = (value - high.astype(F32)).astype(BF16)
    return high, low


def split_wide(value):
    high = value.astype(BF16).astype(F32)
    return high, value - high


def dot3(weight, value):
    high, low = value
    return dot(weight[0], high) + dot(weight[0], low) + dot(weight[1], high)


def dot3_few(weight, value):
    rows = weight[0].shape[0]
    both = dot(jnp.concatenate(weight, axis=0), value[0])
    return both[:rows] + both[rows:] + dot(weight[0], value[1])


def dot3_t(left, right):
    return dot_t(left[0], right[0]) + dot_t(left[0], right[1]) + dot_t(left[1], right[0])


def wide(column, blocks):
    return jnp.concatenate([column] * blocks, axis=1)


def stack_join(value):
    high, low = split_wide(value)
    return jnp.concatenate([high, low, high], axis=0).astype(BF16)


def stack_weight(value):
    high, low = split_wide(value)
    return jnp.transpose(jnp.concatenate([high, high, low], axis=0)).astype(BF16)


def activate(half):
    return half * (1.0 + jnp.tanh(half))


def activate_slope(half):
    bent = jnp.tanh(half)
    rise = 1.0 + bent
    hidden = half * rise
    return hidden, rise + hidden * (1.0 - bent)


def interleave(tasks):
    free = {"mxu": 0, "vpu": 0}
    times = {}
    queue = []

    def advance(task, now):
        generator, known = task
        seen = set(known)
        asked = next(generator, None)
        for name in known:
            if name not in seen:
                times[(id(known), name)] = now
        if asked is not None:
            queue.append((now, task, asked))

    for task in tasks:
        advance(task, task[1]["begin"])
    while queue:
        best = None
        for place, (ready, task, (unit, cost)) in enumerate(queue):
            if unit is None:
                if cost not in task[1]:
                    continue
                start = max(ready, times[(id(task[1]), cost)])
            else:
                start = max(ready, free[unit])
            if best is None or start < best[0]:
                best = (start, place)
        start, place = best
        ready, task, (unit, cost) = queue.pop(place)
        if unit is None:
            advance(task, start)
        else:
            cost = cost * 3 // 2 if unit == "vpu" else cost
            free[unit] = start + cost
            advance(task, start + cost)


def soft_min(first, second):
    return jnp.minimum(first, second) - SOFT_TEMP * jnp.log(
        1.0 + jnp.exp(-jnp.abs(first - second) / SOFT_TEMP)
    )


def squash(head, noise):
    means, bend = head[:8], jnp.tanh(head[8:])
    log_std = STD_LO + 0.5 * (STD_HI - STD_LO) * (bend + 1.0)
    spread = jnp.exp(log_std) * noise
    pre = means + spread
    action = jnp.tanh(pre)
    size = jnp.abs(pre)
    log_jac = 2.0 * (LOG_TWO - size - jnp.log(1.0 + jnp.exp(-2.0 * size)))
    row = lax.broadcasted_iota(jnp.int32, pre.shape, 0)
    inside = (row >= 1) & (row <= ACT)
    terms = jnp.where(inside, -0.5 * noise * noise - log_std - HALF_LOG_TAU - log_jac, 0.0)
    return action, jnp.sum(terms, axis=0, keepdims=True), spread, bend


def load_rows(ref, count, block):
    blocks = ref.shape[0] // count
    return ref[pl.ds(block, count, stride=blocks), :]


def load_chunk(ref, count, first, blocks):
    return jnp.concatenate([load_rows(ref, count, first + g) for g in range(blocks)], axis=1)


def load_row(ref, first, blocks):
    return jnp.concatenate([ref[pl.ds(first + g, 1), :] for g in range(blocks)], axis=1)


def fill_join(join, obs_ref, act_ref, first):
    blocks = join.shape[1] // LANES
    join[0:OBS, :] = load_chunk(obs_ref, OBS, first, blocks)
    if act_ref is not None:
        join[OBS : OBS + ACT, :] = load_chunk(act_ref, ACT, first, blocks)
    join[JOIN - 1 : JOIN, :] = jnp.ones((1, join.shape[1]), F32)


def with_action(join, action):
    row = lax.broadcasted_iota(jnp.int32, action.shape, 0)
    inside = (row >= 1) & (row <= ACT)
    return jnp.concatenate([join[:16], jnp.where(inside, action, join[16:])], axis=0)


def fill_first(ref, row, weight_ref, bias_row, index):
    rows = weight_ref.shape[0]
    ref[row : row + rows, :] = weight_ref[:, index, :]
    ref[row + JOIN - 1 : row + JOIN, :] = bias_row


def store_split(ref, index, value):
    high, low = split(value)
    ref[index, 0] = high
    ref[index, 1] = low


def pair(ref, index):
    return ref[index, 0], ref[index, 1]


def columns(rows):
    turned = jnp.transpose(rows)
    return [jnp.broadcast_to(turned[:, k : k + 1], (HID, LANES)) for k in range(rows.shape[0])]


def back_weights(weight, scale):
    both = jnp.concatenate([scale, scale], axis=1)
    return jnp.transpose(0.25 * both * weight)


def head_bias(bias_ref):
    row = lax.broadcasted_iota(jnp.int32, (HEAD, LANES), 0)
    out = jnp.zeros((HEAD, LANES), F32)
    for k in range(ACT):
        out = jnp.where(row == 1 + k, bias_ref[0, k], out)
        out = jnp.where(row == 9 + k, bias_ref[0, ACT + k], out)
    return out


def fold(value):
    total = value[:, :LANES]
    for g in range(1, value.shape[1] // LANES):
        total = total + value[:, g * LANES : (g + 1) * LANES]
    return total


def valid_lanes(first, count, width):
    lane = lax.broadcasted_iota(jnp.int32, (1, width), 1)
    return lane + first * LANES < count


def spread_row(value):
    return jnp.broadcast_to(value, (1, LANES))


def critic_kernel(
    peers,
    count_ref,
    temper_ref,
    actor_b3,
    critic_b3,
    target_b3,
    states,
    actions,
    rewards,
    next_states,
    dones,
    noise_next,
    probs,
    owners,
    slots,
    actor_w1,
    actor_b1,
    actor_w2,
    actor_b2,
    actor_w3,
    critic_w1,
    critic_b1,
    critic_w2,
    critic_b2,
    critic_w3,
    target_w1,
    target_b1,
    target_w2,
    target_b2,
    target_w3,
    send,
    small,
    one,
    two,
    back,
    head,
    bias_two,
    last,
    wide_bias,
    join,
    acc_two,
    acc_one,
    acc_side,
    acc_table,
    acc_row,
    turn,
):
    count = jnp.max(count_ref[...].astype(F32)).astype(jnp.int32)
    alpha = jnp.exp(temper_ref[...])
    share = HID // peers
    blocks = CRITIC_BLOCKS
    width = blocks * LANES
    depth = acc_table.shape[0] // peers
    small[...] = jnp.zeros_like(small)
    fill_first(small, 0, actor_w1, actor_b1[...], 0)
    for k in range(2):
        fill_first(small, (1 + k) * JOIN, critic_w1, critic_b1[k : k + 1, :], k)
        fill_first(turn, k * JOIN, target_w1, target_b1[k : k + 1, :], k)
    small[HEAD_ROW + 1 : HEAD_ROW + 1 + ACT, :] = actor_w3[0:ACT, 0, :]
    small[HEAD_ROW + 9 : HEAD_ROW + 9 + ACT, :] = actor_w3[ACT : 2 * ACT, 0, :]
    small[REST_ROW : REST_ROW + 1, :] = 0.5 * actor_b2[...]
    small[REST_ROW + 1 : REST_ROW + 3, :] = 0.5 * critic_b2[...]
    small[REST_ROW + 3 : REST_ROW + 5, :] = critic_w3[...]
    turn[2 * JOIN : 2 * JOIN + 2, :] = 0.5 * target_b2[...]
    turn[2 * JOIN + 2 : 2 * JOIN + 4, :] = target_w3[...]
    turn[2 * JOIN + 4 : 2 * JOIN + 8, :] = jnp.zeros((4, HID), F32)
    one[0] = stack_weight(0.5 * small[0:JOIN, :])
    store_split(two, 0, 0.5 * actor_w2[...])
    given = columns(small[REST_ROW : REST_ROW + 8, :])
    aims = columns(turn[2 * JOIN : 2 * JOIN + 8, :])
    bias_two[0] = given[0]
    for k in range(2):
        one[1 + k] = stack_weight(0.5 * turn[k * JOIN : (k + 1) * JOIN, :])
        one[3 + k] = stack_weight(0.5 * small[(1 + k) * JOIN : (2 + k) * JOIN, :])
        store_split(two, 1 + k, 0.5 * target_w2[k])
        store_split(two, 3 + k, 0.5 * critic_w2[k])
        bias_two[1 + k] = aims[k]
        bias_two[3 + k] = given[1 + k]
        last[k] = aims[2 + k]
        last[2 + k] = given[3 + k]
        store_split(back, k, back_weights(critic_w2[k], last[2 + k]))
    store_split(head, 0, small[HEAD_ROW : HEAD_ROW + HEAD, :])
    wide_bias[...] = head_bias(actor_b3)
    small[BIAS_ROW : BIAS_ROW + HEAD, 0:LANES] = wide_bias[...]
    for k in range(2):
        small[BIAS_ROW + k : BIAS_ROW + k + 1, LANES:] = jnp.full((1, LANES), critic_b3[0, k])
    acc_two[...] = jnp.zeros_like(acc_two)
    acc_one[...] = jnp.zeros_like(acc_one)
    acc_side[...] = jnp.zeros_like(acc_side)
    acc_table[...] = jnp.zeros_like(acc_table)
    acc_row[...] = jnp.zeros_like(acc_row)

    def next_action(first, known, lane):
        yield "mxu", 64
        fill_join(join.at[lane], next_states, None, first)
        join[lane, OBS : OBS + ACT, :] = jnp.zeros((ACT, width), F32)
        nexts = join[lane]
        half = dot(one[0], stack_join(nexts))
        yield "vpu", 110
        hidden = split(activate(half))
        yield "mxu", 192
        half = dot3(pair(two, 0), hidden)
        yield "vpu", 130
        hidden = split(activate(half + wide(bias_two[0], blocks)))
        yield "mxu", 128
        out = dot3_few(pair(head, 0), hidden)
        yield "vpu", 100
        join[lane, OBS : OBS + ACT, :] = load_chunk(noise_next, ACT, first, blocks)
        action, known["logp"], _, _ = squash(out + wide(wide_bias[...], blocks), join[lane, 16:24, :])
        known["given_next"] = stack_join(with_action(nexts, action))

    def target_value(first, known, k):
        yield None, "given_next"
        yield "mxu", 64
        half = dot(one[1 + k], known["given_next"])
        yield "vpu", 110
        hidden = split(activate(half))
        yield "mxu", 192
        half = dot3(pair(two, 1 + k), hidden)
        yield "vpu", 120
        hidden = activate(half + wide(bias_two[1 + k], blocks))
        total = jnp.sum(hidden * wide(last[k], blocks), axis=0, keepdims=True)
        known["next", k] = total + target_b3[0, k]

    def target_row(first, known):
        yield None, "logp"
        yield None, ("next", 0)
        yield None, ("next", 1)
        yield "vpu", 40
        keep = GAMMA * (1.0 - load_row(dones, first, blocks).astype(F32))
        worth = soft_min(known["next", 0], known["next", 1]) - alpha * known["logp"]
        known["target"] = load_row(rewards, first, blocks) + keep * worth
        known["valid"] = valid_lanes(first, count, width)
        coef = jnp.exp(-BETA * jnp.log(load_row(probs, first, blocks)))
        known["coef"] = jnp.where(known["valid"], coef, 0.0)

    def given_now(first, known, lane):
        yield "vpu", 20
        fill_join(join.at[lane], states, actions, first)
        known["given"] = stack_join(join[lane])

    def critic(first, known, k):
        yield None, "given"
        given = known["given"]
        yield "mxu", 64
        half = dot(one[3 + k], given)
        yield "vpu", 160
        hidden, slope_one = activate_slope(half)
        hidden_one = split(hidden)
        yield "mxu", 192
        half = dot3(pair(two, 3 + k), hidden_one)
        yield "vpu", 170
        hidden, slope_two = activate_slope(half + wide(bias_two[3 + k], blocks))
        value = jnp.sum(hidden * wide(last[2 + k], blocks), axis=0, keepdims=True) + critic_b3[0, k]
        yield None, "target"
        yield "vpu", 160
        error = value - known["target"]
        known["error", k] = error
        scaled = known["coef"] * error
        grad = scaled * slope_two
        acc_side[k] += fold(grad)
        acc_side[2 + k] += fold(scaled * hidden)
        acc_row[k : k + 1, :] += scaled
        grad_two = split(grad)
        yield "mxu", 192
        half = dot3(pair(back, k), grad_two)
        yield "vpu", 90
        grad_one = split(half * slope_one)
        yield "mxu", 192
        acc_two[k] += dot3_t(grad_two, hidden_one)
        yield "mxu", 128
        acc_one[k] += dot_t(given[:48], grad_one[0]) + dot_t(given[:48], grad_one[1])

    def priorities(first, known):
        yield None, ("error", 0)
        yield None, ("error", 1)
        yield "vpu", 120
        delta = 0.5 * (known["error", 0] + known["error", 1])
        priority = jnp.exp(PRIO_EXP * jnp.log(jnp.abs(delta) + PRIO_EPS))
        priority = jnp.where(known["valid"], priority, 0.0)
        acc_row[2:3, :] = jnp.maximum(acc_row[2:3, :], priority)
        slot = load_row(slots, first, blocks)
        place = load_row(owners, first, blocks) * depth + lax.shift_right_logical(slot, 7)
        lane = slot & (LANES - 1)
        rows = acc_table.shape[0]
        row_hit = lax.broadcasted_iota(jnp.int32, (rows, width), 0) == place
        lane_hit = lax.broadcasted_iota(jnp.int32, (LANES, width), 0) == lane
        high, low = split_wide(priority)
        picked = jnp.concatenate(
            [jnp.where(lane_hit, high, 0.0), jnp.where(lane_hit, low, 0.0)], axis=0
        ).astype(BF16)
        hits = jnp.where(row_hit, 1.0, 0.0).astype(BF16)
        yield "mxu", 64
        acc_table[...] += dot_t(hits, picked)

    def step(index, carry):
        tasks = []
        for lane in range(CRITIC_STREAMS):
            first = (index * CRITIC_STREAMS + lane) * blocks
            known = {"begin": CRITIC_LAG * (2 * lane // CRITIC_STREAMS)}
            tasks.append((next_action(first, known, 2 * lane), known))
            tasks.append((given_now(first, known, 2 * lane + 1), known))
            for k in range(2):
                tasks.append((critic(first, known, k), known))
            for k in range(2):
                tasks.append((target_value(first, known, k), known))
            tasks.append((target_row(first, known), known))
            tasks.append((priorities(first, known), known))
        interleave(tasks)
        return carry

    span = CRITIC_STREAMS * width
    lax.fori_loop(0, (count + span - 1) // span, step, 0)

    for k in range(2):
        acc_side[k] = 0.5 * last[2 + k] * acc_side[k]
    side = [jnp.sum(acc_side[k], axis=1, keepdims=True) for k in range(4)]
    small = [jnp.transpose(acc_one[k][:JOIN] + acc_one[k][JOIN:]) for k in range(2)]
    joined = jnp.concatenate(small + side + [jnp.zeros((HID, LANES - 52), F32)], axis=1)
    acc_side[0] = joined
    lane = lax.broadcasted_iota(jnp.int32, probs.shape, 1)
    row = lax.broadcasted_iota(jnp.int32, probs.shape, 0)
    least = jnp.min(jnp.where(row * LANES + lane < count, probs[...], 1.0), keepdims=True)
    best = jnp.max(acc_row[2:3, :], keepdims=True)
    sums = jnp.concatenate(
        [
            jnp.full((1, LANES), count.astype(F32)),
            spread_row(least),
            spread_row(jnp.sum(acc_row[0:1, :], keepdims=True)),
            spread_row(jnp.sum(acc_row[1:2, :], keepdims=True)),
            spread_row(best),
            jnp.zeros((3, LANES), F32),
        ],
        axis=0,
    )
    table = acc_table[:, :LANES] + acc_table[:, LANES:]
    for p in range(peers):
        mine = slice(p * share, (p + 1) * share)
        at = 0
        for k in range(2):
            for t in range(2):
                block = acc_two[k, mine, t * LANES : (t + 1) * LANES]
                send[p, at : at + share, :] = 0.5 * last[2 + k, mine, :] * block
                at += share
        send[p, at : at + share, :] = acc_side[0, mine, :]
        at += share
        send[p, at : at + depth, :] = table[p * depth : (p + 1) * depth]
        at += depth
        send[p, at : at + 8, :] = sums


def actor_kernel(
    peers,
    core_ref,
    count_ref,
    temper_ref,
    states,
    noise_now,
    small,
    actor_w2,
    critic_w2,
    keep,
    give,
    one,
    two,
    back,
    head,
    head_back,
    entry,
    bias_two,
    last,
    wide_bias,
    join,
    acc_two,
    acc_one,
    acc_head,
    acc_side,
    acc_out,
    acc_row,
):
    count = jnp.max(count_ref[...].astype(F32)).astype(jnp.int32)
    alpha = jnp.exp(temper_ref[...])
    share = HID // peers
    blocks = ACTOR_BLOCKS
    width = blocks * LANES
    given = columns(small[REST_ROW : REST_ROW + 8, :])
    final = small[HEAD_ROW : HEAD_ROW + HEAD, :]
    store_split(two, 0, 0.5 * actor_w2[...])
    store_split(back, 0, jnp.transpose(0.5 * actor_w2[...]))
    bias_two[0] = given[0]
    one[0] = stack_weight(0.5 * small[0:JOIN, :])
    for k in range(2):
        first = (1 + k) * JOIN
        one[1 + k] = stack_weight(0.5 * small[first : first + JOIN, :])
        store_split(entry, k, small[first + 8 : first + 24, :])
        store_split(two, 1 + k, 0.5 * critic_w2[k])
        bias_two[1 + k] = given[1 + k]
        last[k] = given[3 + k]
        store_split(back, 1 + k, back_weights(critic_w2[k], last[k]))
    store_split(head, 0, final)
    head_back[...] = stack_weight(0.5 * final)
    wide_bias[...] = small[BIAS_ROW : BIAS_ROW + HEAD, 0:LANES]
    critic_b3 = [small[BIAS_ROW + k : BIAS_ROW + k + 1, LANES : LANES + 1] for k in range(2)]
    acc_two[...] = jnp.zeros_like(acc_two)
    acc_one[...] = jnp.zeros_like(acc_one)
    acc_head[...] = jnp.zeros_like(acc_head)
    acc_side[...] = jnp.zeros_like(acc_side)
    acc_out[...] = jnp.zeros_like(acc_out)
    acc_row[...] = jnp.zeros_like(acc_row)

    row = lax.broadcasted_iota(jnp.int32, (8, width), 0)
    inside = (row >= 1) & (row <= ACT)

    def forward(first, known, lane):
        yield "mxu", 64
        valid = valid_lanes(first, count, width)
        known["mask"] = jnp.where(valid, 1.0, 0.0)
        fill_join(join.at[lane], states, noise_now, first)
        noise = join[lane, 16:24, :]
        tail = jnp.where(inside, 0.0, noise)
        given = stack_join(jnp.concatenate([join[lane, 0:16, :], tail], axis=0))
        half = dot(one[0], given)
        yield "vpu", 160
        hidden, slope_one = activate_slope(half)
        hidden_one = split(hidden)
        yield "mxu", 192
        half = dot3(pair(two, 0), hidden_one)
        yield "vpu", 170
        hidden, slope_two = activate_slope(half + wide(bias_two[0], blocks))
        hidden_two = split(hidden)
        yield "mxu", 128
        out = dot3_few(pair(head, 0), hidden_two)
        yield "vpu", 100
        action, logp, spread, bend = squash(out + wide(wide_bias[...], blocks), noise)
        acc_row[0:1, :] += known["mask"] * (logp + ENTROPY_AIM)
        known["fresh"] = stack_join(with_action(join[lane], action))
        yield None, "push"
        yield "vpu", 60
        push = known["push"]
        pull = alpha * known["mask"]
        grad_pre = jnp.where(inside, 2.0 * pull * action + push * (1.0 - action * action), 0.0)
        grad_std = jnp.where(inside, grad_pre * spread - pull, 0.0)
        grad_bend = 0.5 * (STD_HI - STD_LO) * grad_std * (1.0 - bend * bend)
        grad_out = jnp.concatenate([grad_pre, grad_bend], axis=0)
        acc_out[...] += fold(grad_out)
        outs = stack_join(grad_out)
        yield "mxu", 64
        half = dot(head_back[...], outs)
        yield "vpu", 100
        grad = half * slope_two
        acc_side[...] += fold(grad)
        grad_two = split(grad)
        yield "mxu", 192
        half = dot3(pair(back, 0), grad_two)
        yield "vpu", 90
        grad_one = split(half * slope_one)
        yield "mxu", 128
        acc_head[...] += dot_t(hidden_two[0], outs[:32]) + dot_t(hidden_two[1], outs[:32])
        yield "mxu", 192
        acc_two[...] += dot3_t(grad_two, hidden_one)
        yield "mxu", 128
        acc_one[...] += dot_t(grad_one[0], given[:48]) + dot_t(grad_one[1], given[:48])

    def critic(first, known, k):
        yield None, "fresh"
        yield "mxu", 64
        half = dot(one[1 + k], known["fresh"])
        yield "vpu", 160
        hidden, slope_one = activate_slope(half)
        hidden_one = split(hidden)
        yield "mxu", 192
        half = dot3(pair(two, 1 + k), hidden_one)
        yield "vpu", 220
        hidden, slope_two = activate_slope(half + wide(bias_two[1 + k], blocks))
        value = jnp.sum(hidden * wide(last[k], blocks), axis=0, keepdims=True) + critic_b3[k]
        known["value", k] = value
        grad_two = split(slope_two)
        yield "mxu", 192
        half = dot3(pair(back, 1 + k), grad_two)
        yield "vpu", 90
        grad_one = split(half * slope_one)
        yield "mxu", 128
        known["pull", k] = dot3_few(pair(entry, k), grad_one)[8:]

    def mix(first, known):
        for k in range(2):
            yield None, ("value", k)
            yield None, ("pull", k)
        yield "vpu", 10
        gap = (known["value", 1] - known["value", 0]) / SOFT_TEMP
        lean = 0.5 * jnp.tanh(0.5 * gap)
        parts = (0.5 + lean) * known["pull", 0] + (0.5 - lean) * known["pull", 1]
        known["push"] = -known["mask"] * parts

    def step(index, carry):
        tasks = []
        for lane in range(ACTOR_STREAMS):
            first = (index * ACTOR_STREAMS + lane) * blocks
            known = {"begin": 0}
            tasks.append((forward(first, known, lane), known))
            for k in range(2):
                tasks.append((critic(first, known, k), known))
            tasks.append((mix(first, known), known))
        interleave(tasks)
        return carry

    span = ACTOR_STREAMS * width
    lax.fori_loop(0, (count + span - 1) // span, step, 0)

    acc_out[...] = jnp.broadcast_to(jnp.sum(acc_out[...], axis=1, keepdims=True), (HEAD, LANES))
    joined = jnp.concatenate(
        [
            acc_one[:, :JOIN] + acc_one[:, JOIN:],
            acc_head[:, :HEAD] + acc_head[:, HEAD:],
            jnp.sum(acc_side[...], axis=1, keepdims=True),
            jnp.broadcast_to(-jnp.sum(acc_row[0:1, :], keepdims=True), (HID, 1)),
            jnp.zeros((HID, OUT_LANE - JOIN - HEAD - 2), F32),
            jnp.broadcast_to(jnp.transpose(acc_out[...])[0:1, :], (HID, HEAD)),
            jnp.zeros((HID, LANES - OUT_LANE - HEAD), F32),
        ],
        axis=1,
    )
    acc_side[...] = joined
    core = core_ref[0]
    for side, part in ((keep, core), (give, 1 - core)):
        for q in range(peers // 2):
            mine = pl.ds(pl.multiple_of((2 * q + part) * share, 8), share)
            side[q, 0:share, :] = acc_two[mine, 0:LANES]
            side[q, share : 2 * share, :] = acc_two[mine, LANES : 2 * LANES]
            side[q, 2 * share : 3 * share, :] = acc_side[mine, :]


def finish_kernel(critic_in, old, *refs):
    actor_in, best_in, outs = refs[:2], refs[2:4], refs[4:]
    a_one, a_bias_one, a_two, a_bias_two, a_three, a_bias_three = outs[:6]
    c_one, c_bias_one, c_two, c_bias_two, c_three, c_bias_three, g_alpha, new, best = outs[6:]
    peers = critic_in.shape[0]
    share = HID // peers
    depth = old.shape[0]

    def actor_total(start, size):
        value = actor_in[0][start : start + size, :]
        for ref in actor_in[1:]:
            value = value + ref[start : start + size, :]
        return value

    def total(ref, start, size):
        value = ref[0, start : start + size, :]
        for p in range(1, peers):
            value = value + ref[p, start : start + size, :]
        return value

    at = 5 * share
    table = total(critic_in, at, depth)
    new[...] = jnp.where(table > 0.0, table, old[...])
    at += depth
    sums = total(critic_in, at, 8)
    least = critic_in[0, at + 1 : at + 2, :]
    for p in range(1, peers):
        least = jnp.minimum(least, critic_in[p, at + 1 : at + 2, :])
    actor_scale = 1.0 / sums[0:1, :]
    critic_scale = actor_scale * jnp.exp(BETA * jnp.log(least))
    for k in range(2):
        for t in range(2):
            c_two[k, :, t * LANES : (t + 1) * LANES] = critic_scale * total(
                critic_in, (2 * k + t) * share, share
            )
    small = jnp.transpose(critic_scale * total(critic_in, 4 * share, share))
    for k in range(2):
        for j in range(JOIN - 1):
            c_one[j, k : k + 1, :] = small[k * JOIN + j : k * JOIN + j + 1, :]
        c_bias_one[k : k + 1, :] = small[k * JOIN + JOIN - 1 : k * JOIN + JOIN, :]
        c_bias_two[k : k + 1, :] = small[48 + k : 49 + k, :]
        c_three[k : k + 1, :] = small[50 + k : 51 + k, :]
    lane = lax.broadcasted_iota(jnp.int32, (1, LANES), 1)
    both = jnp.where(lane == 0, sums[2:3, :], sums[3:4, :])
    c_bias_three[...] = (critic_scale * both)[:, 0:2]
    for t in range(2):
        a_two[:, t * LANES : (t + 1) * LANES] = actor_scale * actor_total(t * share, share)
    flat = actor_scale * actor_total(2 * share, share)
    small = jnp.transpose(flat)
    for j in range(OBS):
        a_one[j] = small[j : j + 1, :]
    a_bias_one[...] = small[JOIN - 1 : JOIN, :]
    for j in range(ACT):
        a_three[j] = small[JOIN + 1 + j : JOIN + 2 + j, :]
        a_three[ACT + j] = small[JOIN + 9 + j : JOIN + 10 + j, :]
    a_bias_two[...] = small[JOIN + HEAD : JOIN + HEAD + 1, :]
    g_alpha[...] = flat[0:1, JOIN + HEAD + 1 : JOIN + HEAD + 2]
    a_bias_three[:, 0:ACT] = flat[0:1, OUT_LANE + 1 : OUT_LANE + 1 + ACT]
    a_bias_three[:, ACT : 2 * ACT] = flat[0:1, OUT_LANE + 9 : OUT_LANE + 9 + ACT]
    largest = best_in[0][...]
    for ref in best_in[1:]:
        largest = jnp.maximum(largest, ref[...])
    best[...] = largest[:, 0:1]


SMEM = pl.BlockSpec(memory_space=pltpu.SMEM)
VMEM = pl.BlockSpec(memory_space=pltpu.VMEM)


def shards(
    states,
    actions,
    rewards,
    next_states,
    dones,
    noise_now,
    noise_next,
    probs,
    valid_counts,
    owners,
    slots,
    old_priorities,
    actor_w1,
    actor_b1,
    actor_w2,
    actor_b2,
    actor_w3,
    actor_b3,
    critic_w1,
    critic_b1,
    critic_w2,
    critic_b2,
    critic_w3,
    critic_b3,
    target_w1,
    target_b1,
    target_w2,
    target_b2,
    target_w3,
    target_b3,
    log_alpha,
):
    peers = lax.axis_size("dp")
    me = lax.axis_index("dp")
    share = HID // peers

    def rows(value):
        return value.reshape(-1, LANES)

    states, actions, next_states = rows(states), rows(actions), rows(next_states)
    noise_now, noise_next = rows(noise_now), rows(noise_next)
    rewards, dones, probs = rows(rewards), rows(dones), rows(probs)
    owners, slots, old = rows(owners), rows(slots), rows(old_priorities)
    depth = old.shape[0]
    actor_one = jnp.transpose(actor_w1, (2, 0, 1))
    actor_three = jnp.transpose(actor_w3, (1, 0, 2))
    critic_one = jnp.transpose(critic_w1[0], (2, 0, 1))
    target_one = jnp.transpose(target_w1[0], (2, 0, 1))
    critic_rows = 5 * share + depth + 8
    actor_rows = 3 * share
    critic_send, small = pl.pallas_call(
        functools.partial(critic_kernel, peers),
        out_shape=(
            jax.ShapeDtypeStruct((peers, critic_rows, LANES), F32),
            jax.ShapeDtypeStruct((SMALL, HID), F32),
        ),
        in_specs=[VMEM] * 2 + [SMEM] * 3 + [VMEM] * 24,
        out_specs=(VMEM, VMEM),
        scratch_shapes=[
            pltpu.VMEM((5, HID, 3 * JOIN), BF16),
            pltpu.VMEM((5, 2, HID, HID), BF16),
            pltpu.VMEM((2, 2, HID, HID), BF16),
            pltpu.VMEM((1, 2, HEAD, HID), BF16),
            pltpu.VMEM((5, HID, LANES), F32),
            pltpu.VMEM((4, HID, LANES), F32),
            pltpu.VMEM((HEAD, LANES), F32),
            pltpu.VMEM((2 * CRITIC_STREAMS, JOIN, CRITIC_BLOCKS * LANES), F32),
            pltpu.VMEM((2, HID, HID), F32),
            pltpu.VMEM((2, 2 * JOIN, HID), F32),
            pltpu.VMEM((4, HID, LANES), F32),
            pltpu.VMEM((peers * depth, 2 * LANES), F32),
            pltpu.VMEM((8, CRITIC_BLOCKS * LANES), F32),
            pltpu.VMEM((2 * JOIN + 8, HID), F32),
        ],
        compiler_params=pltpu.CompilerParams(vmem_limit_bytes=CRITIC_LIMIT),
        cost_estimate=pl.CostEstimate(flops=20 * 10**9, bytes_accessed=4 * 10**6, transcendentals=10**7),
        name="critic",
    )(
        valid_counts,
        log_alpha.reshape(1, 1),
        actor_b3,
        critic_b3,
        target_b3,
        states,
        actions,
        rewards,
        next_states,
        dones,
        noise_next,
        probs,
        owners,
        slots,
        actor_one,
        actor_b1,
        actor_w2[0],
        actor_b2,
        actor_three,
        critic_one,
        critic_b1[0],
        critic_w2[0],
        critic_b2[0],
        critic_w3[0],
        target_one,
        target_b1[0],
        target_w2[0],
        target_b2[0],
        target_w3[0],
    )
    critic_in = lax.all_to_all(critic_send, "dp", split_axis=0, concat_axis=0, tiled=True)
    kept, given = pl.pallas_call(
        functools.partial(actor_kernel, peers),
        out_shape=(jax.ShapeDtypeStruct((peers // 2, actor_rows, LANES), F32),) * 2,
        in_specs=[SMEM] + [VMEM] * 7,
        out_specs=(VMEM, VMEM),
        scratch_shapes=[
            pltpu.VMEM((3, HID, 3 * JOIN), BF16),
            pltpu.VMEM((3, 2, HID, HID), BF16),
            pltpu.VMEM((3, 2, HID, HID), BF16),
            pltpu.VMEM((1, 2, HEAD, HID), BF16),
            pltpu.VMEM((HID, 3 * HEAD), BF16),
            pltpu.VMEM((2, 2, 16, HID), BF16),
            pltpu.VMEM((3, HID, LANES), F32),
            pltpu.VMEM((2, HID, LANES), F32),
            pltpu.VMEM((HEAD, LANES), F32),
            pltpu.VMEM((ACTOR_STREAMS, JOIN, ACTOR_BLOCKS * LANES), F32),
            pltpu.VMEM((HID, HID), F32),
            pltpu.VMEM((HID, 2 * JOIN), F32),
            pltpu.VMEM((HID, 2 * HEAD), F32),
            pltpu.VMEM((HID, LANES), F32),
            pltpu.VMEM((HEAD, LANES), F32),
            pltpu.VMEM((8, ACTOR_BLOCKS * LANES), F32),
        ],
        compiler_params=pltpu.CompilerParams(vmem_limit_bytes=ACTOR_LIMIT),
        cost_estimate=pl.CostEstimate(flops=20 * 10**9, bytes_accessed=4 * 10**6, transcendentals=10**7),
        name="actor",
    )(
        (me % 2).reshape(1),
        valid_counts,
        log_alpha.reshape(1, 1),
        states,
        noise_now,
        small,
        actor_w2[0],
        critic_w2[0],
    )
    at = 5 * share + depth + 4
    best = jnp.max(critic_in[:, at : at + 1, :], axis=0)
    best_in = best
    agents = lax.axis_size("seed")
    spans = (agents - 1).bit_length()
    bits = (peers - 1).bit_length()
    actor_in = lax.ppermute(given, "dp", [(k, k ^ 1) for k in range(peers)])
    for bit in range(1, max(bits, 1 + spans)):
        if bit < bits:
            both = (kept + actor_in).reshape(-1, 2, actor_rows, LANES)
            mine = (me >> bit) & 1
            kept = lax.dynamic_index_in_dim(both, mine, 1, False)
            given = lax.dynamic_index_in_dim(both, 1 - mine, 1, False)
            actor_in = lax.ppermute(given, "dp", [(k, k ^ (1 << bit)) for k in range(peers)])
        if bit <= spans:
            best = jnp.maximum(best, best_in)
            best_in = lax.ppermute(best, "seed", [(k, k ^ (1 << (bit - 1))) for k in range(agents)])
        actor_in, best_in = lax.optimization_barrier((actor_in, best_in))
    actor_parts, bests = (kept[0], actor_in[0]), (best, best_in)
    shape = jax.ShapeDtypeStruct
    outs = pl.pallas_call(
        finish_kernel,
        out_shape=(
            shape((OBS, 1, share), F32),
            shape((1, share), F32),
            shape((share, HID), F32),
            shape((1, share), F32),
            shape((2 * ACT, 1, share), F32),
            shape((1, 2 * ACT), F32),
            shape((JOIN - 1, 2, share), F32),
            shape((2, share), F32),
            shape((2, share, HID), F32),
            shape((2, share), F32),
            shape((2, share), F32),
            shape((1, 2), F32),
            shape((1, 1), F32),
            shape((depth, LANES), F32),
            shape((1, 1), F32),
        ),
        in_specs=[VMEM] * 6,
        out_specs=(VMEM,) * 15,
        compiler_params=pltpu.CompilerParams(vmem_limit_bytes=FINISH_LIMIT),
        name="finish",
    )(critic_in, old, *actor_parts, *bests)
    return (
        jnp.transpose(outs[0], (1, 2, 0)),
        outs[1],
        outs[2][None],
        outs[3],
        jnp.transpose(outs[4], (1, 0, 2)),
        outs[5],
        jnp.transpose(outs[6], (1, 2, 0))[None],
        outs[7][None],
        outs[8][None],
        outs[9][None],
        outs[10][None],
        outs[11],
        outs[12].reshape(1),
        outs[13].reshape(1, -1),
        outs[14].reshape(()),
    )


def solution(mesh):
    token = P("seed", None, "dp")
    line = P("seed", "dp")
    agent = P("seed")
    placed = (
        (token, token, line, token, line, token, token, line, line, line, line, line)
        + (agent,) * 19
    )
    return jax.shard_map(
        shards,
        mesh=mesh,
        in_specs=placed,
        out_specs=(
            P("seed", "dp", None),
            P("seed", "dp"),
            P("seed", "dp", None),
            P("seed", "dp"),
            P("seed", None, "dp"),
            P("seed", None),
            P("seed", None, "dp", None),
            P("seed", None, "dp"),
            P("seed", None, "dp", None),
            P("seed", None, "dp"),
            P("seed", None, "dp"),
            P("seed", None),
            P("seed"),
            P("seed", "dp"),
            P(),
        ),
        check_vma=False,
    )
```

```python
import functools
import math

import jax
import jax.numpy as jnp
from jax import lax
from jax.experimental import pallas as pl
from jax.experimental.pallas import tpu as pltpu
from jax.sharding import PartitionSpec as P

F32 = jnp.float32
BF16 = jnp.bfloat16
GAMMA = 0.99
STD_LO = -5.0
STD_HI = 2.0
ENTROPY_AIM = -6.0
SOFT_TEMP = 0.1
BETA = 0.4
PRIO_EXP = 0.6
PRIO_EPS = 0.001
HALF_LOG_TAU = 0.5 * math.log(2.0 * math.pi)
LOG_TWO = math.log(2.0)

LANES = 128
OBS = 17
ACT = 6
HID = 256
JOIN = 24
OUT_LANE = 48
HEAD_ROW = 3 * JOIN
REST_ROW = HEAD_ROW + 16
BIAS_ROW = REST_ROW + 8
SMALL = BIAS_ROW + 16
HEAD = 16
CRITIC_BLOCKS, CRITIC_STREAMS, CRITIC_LAG = 4, 4, 2000
ACTOR_BLOCKS, ACTOR_STREAMS = 8, 2
SOURCES = 29
CRITIC_LIMIT = 56 * 1024 * 1024
ACTOR_LIMIT = 36 * 1024 * 1024
FINISH_LIMIT = 8 * 1024 * 1024


def dot(left, right):
    return jnp.dot(left, right, preferred_element_type=F32)


def dot_t(left, right):
    return lax.dot_general(left, right, (((1,), (1,)), ((), ())), preferred_element_type=F32)


def split(value):
    high = value.astype(BF16)
    low = (value - high.astype(F32)).astype(BF16)
    return high, low


def split_wide(value):
    high = value.astype(BF16).astype(F32)
    return high, value - high


def dot3(weight, value):
    high, low = value
    return dot(weight[0], high) + dot(weight[0], low) + dot(weight[1], high)


def dot3_joint(weight, value):
    rows = weight[0].shape[0]
    both = dot(jnp.concatenate(weight, axis=0), value[0])
    return both[:rows] + both[rows:] + dot(weight[0], value[1])


def dot3_t(left, right):
    return dot_t(left[0], right[0]) + dot_t(left[0], right[1]) + dot_t(left[1], right[0])


def wide(column, blocks):
    return jnp.concatenate([column] * blocks, axis=1)


def stack_join(value):
    high, low = split_wide(value)
    return jnp.concatenate([high, low, high], axis=0).astype(BF16)


def stack_weight(value):
    high, low = split_wide(value)
    return jnp.transpose(jnp.concatenate([high, high, low], axis=0)).astype(BF16)


def activate(half):
    return half * (1.0 + jnp.tanh(half))


def activate_slope(half):
    bent = jnp.tanh(half)
    rise = 1.0 + bent
    hidden = half * rise
    return hidden, rise + hidden * (1.0 - bent)


def interleave(tasks):
    free = {"mxu": 0, "vpu": 0}
    times = {}
    queue = []

    def advance(task, now):
        generator, known = task
        seen = set(known)
        asked = next(generator, None)
        for name in known:
            if name not in seen:
                times[(id(known), name)] = now
        if asked is not None:
            queue.append((now, task, asked))

    for task in tasks:
        advance(task, task[1]["begin"])
    while queue:
        best = None
        for place, (ready, task, (unit, cost)) in enumerate(queue):
            if unit is None:
                if cost not in task[1]:
                    continue
                start = max(ready, times[(id(task[1]), cost)])
            else:
                start = max(ready, free[unit])
            if best is None or start < best[0]:
                best = (start, place)
        start, place = best
        ready, task, (unit, cost) = queue.pop(place)
        if unit is None:
            advance(task, start)
        else:
            cost = cost * 2 if unit == "vpu" else cost
            free[unit] = start + cost
            advance(task, start + cost)


def soft_min(first, second):
    return jnp.minimum(first, second) - SOFT_TEMP * jnp.log(
        1.0 + jnp.exp(-jnp.abs(first - second) / SOFT_TEMP)
    )


def squash(head, noise):
    means, bend = head[:8], jnp.tanh(head[8:])
    log_std = STD_LO + 0.5 * (STD_HI - STD_LO) * (bend + 1.0)
    spread = jnp.exp(log_std) * noise
    pre = means + spread
    action = jnp.tanh(pre)
    size = jnp.abs(pre)
    log_jac = 2.0 * (LOG_TWO - size - jnp.log(1.0 + jnp.exp(-2.0 * size)))
    row = lax.broadcasted_iota(jnp.int32, pre.shape, 0)
    inside = (row >= 1) & (row <= ACT)
    terms = jnp.where(inside, -0.5 * noise * noise - log_std - HALF_LOG_TAU - log_jac, 0.0)
    return action, jnp.sum(terms, axis=0, keepdims=True), spread, bend


def load_rows(ref, count, block):
    blocks = ref.shape[0] // count
    return ref[pl.ds(block, count, stride=blocks), :]


def load_chunk(ref, count, first, blocks):
    return jnp.concatenate([load_rows(ref, count, first + g) for g in range(blocks)], axis=1)


def load_row(ref, first, blocks):
    return jnp.concatenate([ref[pl.ds(first + g, 1), :] for g in range(blocks)], axis=1)


def fill_join(join, obs_ref, act_ref, first):
    blocks = join.shape[1] // LANES
    join[0:OBS, :] = load_chunk(obs_ref, OBS, first, blocks)
    if act_ref is not None:
        join[OBS : OBS + ACT, :] = load_chunk(act_ref, ACT, first, blocks)
    join[JOIN - 1 : JOIN, :] = jnp.ones((1, join.shape[1]), F32)


def with_action(join, action):
    row = lax.broadcasted_iota(jnp.int32, action.shape, 0)
    inside = (row >= 1) & (row <= ACT)
    return jnp.concatenate([join[:16], jnp.where(inside, action, join[16:])], axis=0)


def fill_first(ref, row, weight_ref, bias_row, index):
    rows = weight_ref.shape[0]
    ref[row : row + rows, :] = weight_ref[:, index, :]
    ref[row + JOIN - 1 : row + JOIN, :] = bias_row


def store_split(ref, index, value):
    high, low = split(value)
    ref[index, 0] = high
    ref[index, 1] = low


def pair(ref, index):
    return ref[index, 0], ref[index, 1]


def columns(rows):
    turned = jnp.transpose(rows)
    return [jnp.broadcast_to(turned[:, k : k + 1], (HID, LANES)) for k in range(rows.shape[0])]


def back_weights(weight, scale):
    both = jnp.concatenate([scale, scale], axis=1)
    return jnp.transpose(0.25 * both * weight)


def head_bias(bias_ref):
    row = lax.broadcasted_iota(jnp.int32, (HEAD, LANES), 0)
    out = jnp.zeros((HEAD, LANES), F32)
    for k in range(ACT):
        out = jnp.where(row == 1 + k, bias_ref[0, k], out)
        out = jnp.where(row == 9 + k, bias_ref[0, ACT + k], out)
    return out


def fold(value):
    total = value[:, :LANES]
    for g in range(1, value.shape[1] // LANES):
        total = total + value[:, g * LANES : (g + 1) * LANES]
    return total


def valid_lanes(first, count, width):
    lane = lax.broadcasted_iota(jnp.int32, (1, width), 1)
    return lane + first * LANES < count


def spread_row(value):
    return jnp.broadcast_to(value, (1, LANES))


def critic_kernel(peers, *refs):
    sources, refs = refs[:SOURCES], refs[SOURCES:]
    (send, small), refs = refs[:2], refs[2:]
    places, refs = refs[:SOURCES], refs[SOURCES:]
    one, two, back, head, bias_two, last, wide_bias, join = refs[:8]
    acc_two, acc_one, acc_side, acc_table, acc_row, turn, arrived = refs[8:]
    copies = [
        pltpu.make_async_copy(source, place, arrived.at[k])
        for k, (source, place) in enumerate(zip(sources, places))
    ]
    for copy in copies:
        copy.start()
    count_ref, temper_ref, actor_b3, critic_b3, target_b3 = places[:5]
    actor_w1, actor_b1, actor_b2, actor_w3 = places[5:9]
    critic_w1, critic_b1, critic_b2, critic_w3 = places[9:13]
    target_w1, target_b1, target_b2, target_w3 = places[13:17]
    actor_w2, target_w2, critic_w2 = places[17:20]
    states, actions, rewards, next_states, dones, noise_next, probs, owners, slots = places[20:]
    acc_two[...] = jnp.zeros_like(acc_two)
    acc_one[...] = jnp.zeros_like(acc_one)
    acc_side[...] = jnp.zeros_like(acc_side)
    acc_table[...] = jnp.zeros_like(acc_table)
    acc_row[...] = jnp.zeros_like(acc_row)
    small[...] = jnp.zeros_like(small)
    for copy in copies[:17]:
        copy.wait()
    count = count_ref[0, 0]
    alpha = jnp.exp(temper_ref[0, 0])
    share = HID // peers
    blocks = CRITIC_BLOCKS
    width = blocks * LANES
    depth = acc_table.shape[0] // peers
    fill_first(small, 0, actor_w1, actor_b1[...], 0)
    for k in range(2):
        fill_first(small, (1 + k) * JOIN, critic_w1, critic_b1[k : k + 1, :], k)
        fill_first(turn, k * JOIN, target_w1, target_b1[k : k + 1, :], k)
    small[HEAD_ROW + 1 : HEAD_ROW + 1 + ACT, :] = actor_w3[0:ACT, 0, :]
    small[HEAD_ROW + 9 : HEAD_ROW + 9 + ACT, :] = actor_w3[ACT : 2 * ACT, 0, :]
    small[REST_ROW : REST_ROW + 1, :] = 0.5 * actor_b2[...]
    small[REST_ROW + 1 : REST_ROW + 3, :] = 0.5 * critic_b2[...]
    small[REST_ROW + 3 : REST_ROW + 5, :] = critic_w3[...]
    turn[2 * JOIN : 2 * JOIN + 2, :] = 0.5 * target_b2[...]
    turn[2 * JOIN + 2 : 2 * JOIN + 4, :] = target_w3[...]
    turn[2 * JOIN + 4 : 2 * JOIN + 8, :] = jnp.zeros((4, HID), F32)
    wide_bias[...] = head_bias(actor_b3)
    small[BIAS_ROW : BIAS_ROW + HEAD, 0:LANES] = wide_bias[...]
    for k in range(2):
        small[BIAS_ROW + k : BIAS_ROW + k + 1, LANES:] = jnp.full((1, LANES), critic_b3[0, k])
    store_split(head, 0, small[HEAD_ROW : HEAD_ROW + HEAD, :])
    one[0] = stack_weight(0.5 * small[0:JOIN, :])
    given = columns(small[REST_ROW : REST_ROW + 8, :])
    aims = columns(turn[2 * JOIN : 2 * JOIN + 8, :])
    bias_two[0] = given[0]
    for k in range(2):
        one[1 + k] = stack_weight(0.5 * turn[k * JOIN : (k + 1) * JOIN, :])
        one[3 + k] = stack_weight(0.5 * small[(1 + k) * JOIN : (2 + k) * JOIN, :])
        bias_two[1 + k] = aims[k]
        bias_two[3 + k] = given[1 + k]
        last[k] = aims[2 + k]
        last[2 + k] = given[3 + k]
    for copy in copies[17:20]:
        copy.wait()
    store_split(two, 0, 0.5 * actor_w2[...])
    for k in range(2):
        store_split(two, 1 + k, 0.5 * target_w2[k])
        store_split(two, 3 + k, 0.5 * critic_w2[k])
        store_split(back, k, back_weights(critic_w2[k], last[2 + k]))
    for copy in copies[20:]:
        copy.wait()

    def next_action(first, known, lane):
        yield "mxu", 64
        fill_join(join.at[lane], next_states, None, first)
        join[lane, OBS : OBS + ACT, :] = jnp.zeros((ACT, width), F32)
        nexts = join[lane]
        half = dot(one[0], stack_join(nexts))
        yield "vpu", 110
        hidden = split(activate(half))
        yield "mxu", 192
        half = dot3(pair(two, 0), hidden)
        yield "vpu", 130
        hidden = split(activate(half + wide(bias_two[0], blocks)))
        yield "mxu", 128
        out = dot3_joint(pair(head, 0), hidden)
        yield "vpu", 100
        join[lane, OBS : OBS + ACT, :] = load_chunk(noise_next, ACT, first, blocks)
        action, known["logp"], _, _ = squash(out + wide(wide_bias[...], blocks), join[lane, 16:24, :])
        known["given_next"] = stack_join(with_action(nexts, action))

    def target_value(first, known, k):
        yield None, "given_next"
        yield "mxu", 64
        half = dot(one[1 + k], known["given_next"])
        yield "vpu", 110
        hidden = split(activate(half))
        yield "mxu", 192
        half = dot3(pair(two, 1 + k), hidden)
        yield "vpu", 120
        hidden = activate(half + wide(bias_two[1 + k], blocks))
        total = jnp.sum(hidden * wide(last[k], blocks), axis=0, keepdims=True)
        known["next", k] = total + target_b3[0, k]

    def target_row(first, known):
        yield None, "logp"
        yield None, ("next", 0)
        yield None, ("next", 1)
        yield "vpu", 40
        keep = GAMMA * (1.0 - load_row(dones, first, blocks).astype(F32))
        worth = soft_min(known["next", 0], known["next", 1]) - alpha * known["logp"]
        known["target"] = load_row(rewards, first, blocks) + keep * worth
        known["valid"] = valid_lanes(first, count, width)
        coef = jnp.exp(-BETA * jnp.log(load_row(probs, first, blocks)))
        known["coef"] = jnp.where(known["valid"], coef, 0.0)

    def given_now(first, known, lane):
        yield "vpu", 20
        fill_join(join.at[lane], states, actions, first)
        known["given"] = stack_join(join[lane])

    def critic(first, known, k):
        yield None, "given"
        given = known["given"]
        yield "mxu", 64
        half = dot(one[3 + k], given)
        yield "vpu", 160
        hidden, slope_one = activate_slope(half)
        hidden_one = split(hidden)
        yield "mxu", 192
        half = dot3(pair(two, 3 + k), hidden_one)
        yield "vpu", 170
        hidden, slope_two = activate_slope(half + wide(bias_two[3 + k], blocks))
        value = jnp.sum(hidden * wide(last[2 + k], blocks), axis=0, keepdims=True) + critic_b3[0, k]
        yield None, "target"
        yield "vpu", 160
        error = value - known["target"]
        known["error", k] = error
        scaled = known["coef"] * error
        grad = scaled * slope_two
        acc_side[k] += fold(grad)
        acc_side[2 + k] += fold(scaled * hidden)
        acc_row[k : k + 1, :] += scaled
        grad_two = split(grad)
        yield "mxu", 192
        half = dot3(pair(back, k), grad_two)
        yield "vpu", 90
        grad_one = split(half * slope_one)
        yield "mxu", 192
        acc_two[k] += dot3_t(grad_two, hidden_one)
        yield "mxu", 128
        acc_one[k] += dot_t(given[:48], grad_one[0]) + dot_t(given[:48], grad_one[1])

    def priorities(first, known):
        yield None, ("error", 0)
        yield None, ("error", 1)
        yield "vpu", 120
        delta = 0.5 * (known["error", 0] + known["error", 1])
        priority = jnp.exp(PRIO_EXP * jnp.log(jnp.abs(delta) + PRIO_EPS))
        priority = jnp.where(known["valid"], priority, 0.0)
        acc_row[2:3, :] = jnp.maximum(acc_row[2:3, :], priority)
        slot = load_row(slots, first, blocks)
        place = load_row(owners, first, blocks) * depth + lax.shift_right_logical(slot, 7)
        lane = slot & (LANES - 1)
        rows = acc_table.shape[0]
        row_hit = lax.broadcasted_iota(jnp.int32, (rows, width), 0) == place
        lane_hit = lax.broadcasted_iota(jnp.int32, (LANES, width), 0) == lane
        high, low = split_wide(priority)
        picked = jnp.concatenate(
            [jnp.where(lane_hit, high, 0.0), jnp.where(lane_hit, low, 0.0)], axis=0
        ).astype(BF16)
        hits = jnp.where(row_hit, 1.0, 0.0).astype(BF16)
        yield "mxu", 64
        acc_table[...] += dot_t(hits, picked)

    def step(index, carry):
        tasks = []
        for lane in range(CRITIC_STREAMS):
            first = (index * CRITIC_STREAMS + lane) * blocks
            known = {"begin": CRITIC_LAG * (2 * lane // CRITIC_STREAMS)}
            tasks.append((next_action(first, known, 2 * lane), known))
            tasks.append((given_now(first, known, 2 * lane + 1), known))
            for k in range(2):
                tasks.append((critic(first, known, k), known))
            for k in range(2):
                tasks.append((target_value(first, known, k), known))
            tasks.append((target_row(first, known), known))
            tasks.append((priorities(first, known), known))
        interleave(tasks)
        return carry

    span = CRITIC_STREAMS * width
    lax.fori_loop(0, (count + span - 1) // span, step, 0)

    for k in range(2):
        acc_side[k] = 0.5 * last[2 + k] * acc_side[k]
    side = [jnp.sum(acc_side[k], axis=1, keepdims=True) for k in range(4)]
    small = [jnp.transpose(acc_one[k][:JOIN] + acc_one[k][JOIN:]) for k in range(2)]
    joined = jnp.concatenate(small + side + [jnp.zeros((HID, LANES - 52), F32)], axis=1)
    acc_side[0] = joined
    lane = lax.broadcasted_iota(jnp.int32, probs.shape, 1)
    row = lax.broadcasted_iota(jnp.int32, probs.shape, 0)
    least = jnp.min(jnp.where(row * LANES + lane < count, probs[...], 1.0), keepdims=True)
    best = jnp.max(acc_row[2:3, :], keepdims=True)
    sums = jnp.concatenate(
        [
            jnp.full((1, LANES), count.astype(F32)),
            spread_row(least),
            spread_row(jnp.sum(acc_row[0:1, :], keepdims=True)),
            spread_row(jnp.sum(acc_row[1:2, :], keepdims=True)),
            spread_row(best),
            jnp.zeros((3, LANES), F32),
        ],
        axis=0,
    )
    table = acc_table[:, :LANES] + acc_table[:, LANES:]
    for p in range(peers):
        mine = slice(p * share, (p + 1) * share)
        at = 0
        for k in range(2):
            for t in range(2):
                block = acc_two[k, mine, t * LANES : (t + 1) * LANES]
                send[p, at : at + share, :] = 0.5 * last[2 + k, mine, :] * block
                at += share
        send[p, at : at + share, :] = acc_side[0, mine, :]
        at += share
        send[p, at : at + depth, :] = table[p * depth : (p + 1) * depth]
        at += depth
        send[p, at : at + 8, :] = sums


def actor_kernel(
    peers,
    core_ref,
    count_ref,
    temper_ref,
    states,
    noise_now,
    small,
    actor_w2,
    critic_w2,
    keep,
    give,
    one,
    two,
    back,
    head,
    head_back,
    entry,
    bias_two,
    last,
    wide_bias,
    join,
    acc_two,
    acc_one,
    acc_head,
    acc_side,
    acc_out,
    acc_row,
):
    count = jnp.max(count_ref[...].astype(F32)).astype(jnp.int32)
    alpha = jnp.exp(temper_ref[...])
    share = HID // peers
    blocks = ACTOR_BLOCKS
    width = blocks * LANES
    given = columns(small[REST_ROW : REST_ROW + 8, :])
    final = small[HEAD_ROW : HEAD_ROW + HEAD, :]
    store_split(two, 0, 0.5 * actor_w2[...])
    store_split(back, 0, jnp.transpose(0.5 * actor_w2[...]))
    bias_two[0] = given[0]
    one[0] = stack_weight(0.5 * small[0:JOIN, :])
    for k in range(2):
        first = (1 + k) * JOIN
        one[1 + k] = stack_weight(0.5 * small[first : first + JOIN, :])
        store_split(entry, k, small[first + 8 : first + 24, :])
        store_split(two, 1 + k, 0.5 * critic_w2[k])
        bias_two[1 + k] = given[1 + k]
        last[k] = given[3 + k]
        store_split(back, 1 + k, back_weights(critic_w2[k], last[k]))
    store_split(head, 0, final)
    head_back[...] = stack_weight(0.5 * final)
    wide_bias[...] = small[BIAS_ROW : BIAS_ROW + HEAD, 0:LANES]
    critic_b3 = [small[BIAS_ROW + k : BIAS_ROW + k + 1, LANES : LANES + 1] for k in range(2)]
    acc_two[...] = jnp.zeros_like(acc_two)
    acc_one[...] = jnp.zeros_like(acc_one)
    acc_head[...] = jnp.zeros_like(acc_head)
    acc_side[...] = jnp.zeros_like(acc_side)
    acc_out[...] = jnp.zeros_like(acc_out)
    acc_row[...] = jnp.zeros_like(acc_row)

    row = lax.broadcasted_iota(jnp.int32, (8, width), 0)
    inside = (row >= 1) & (row <= ACT)

    def forward(first, known, lane):
        yield "mxu", 64
        valid = valid_lanes(first, count, width)
        known["mask"] = jnp.where(valid, 1.0, 0.0)
        fill_join(join.at[lane], states, noise_now, first)
        noise = join[lane, 16:24, :]
        tail = jnp.where(inside, 0.0, noise)
        given = stack_join(jnp.concatenate([join[lane, 0:16, :], tail], axis=0))
        half = dot(one[0], given)
        yield "vpu", 160
        hidden, slope_one = activate_slope(half)
        hidden_one = split(hidden)
        yield "mxu", 192
        half = dot3_joint(pair(two, 0), hidden_one)
        yield "vpu", 170
        hidden, slope_two = activate_slope(half + wide(bias_two[0], blocks))
        hidden_two = split(hidden)
        yield "mxu", 128
        out = dot3_joint(pair(head, 0), hidden_two)
        yield "vpu", 100
        action, logp, spread, bend = squash(out + wide(wide_bias[...], blocks), noise)
        acc_row[0:1, :] += known["mask"] * (logp + ENTROPY_AIM)
        known["fresh"] = stack_join(with_action(join[lane], action))
        yield None, "push"
        yield "vpu", 60
        push = known["push"]
        pull = alpha * known["mask"]
        grad_pre = jnp.where(inside, 2.0 * pull * action + push * (1.0 - action * action), 0.0)
        grad_std = jnp.where(inside, grad_pre * spread - pull, 0.0)
        grad_bend = 0.5 * (STD_HI - STD_LO) * grad_std * (1.0 - bend * bend)
        grad_out = jnp.concatenate([grad_pre, grad_bend], axis=0)
        acc_out[...] += fold(grad_out)
        outs = stack_join(grad_out)
        yield "mxu", 64
        half = dot(head_back[...], outs)
        yield "vpu", 100
        grad = half * slope_two
        acc_side[...] += fold(grad)
        grad_two = split(grad)
        yield "mxu", 192
        half = dot3_joint(pair(back, 0), grad_two)
        yield "vpu", 90
        grad_one = split(half * slope_one)
        yield "mxu", 128
        acc_head[...] += dot_t(hidden_two[0], outs[:32]) + dot_t(hidden_two[1], outs[:32])
        yield "mxu", 192
        acc_two[...] += dot3_t(grad_two, hidden_one)
        yield "mxu", 128
        acc_one[...] += dot_t(grad_one[0], given[:48]) + dot_t(grad_one[1], given[:48])

    def critic(first, known, k):
        yield None, "fresh"
        yield "mxu", 64
        half = dot(one[1 + k], known["fresh"])
        yield "vpu", 160
        hidden, slope_one = activate_slope(half)
        hidden_one = split(hidden)
        yield "mxu", 192
        half = dot3_joint(pair(two, 1 + k), hidden_one)
        yield "vpu", 220
        hidden, slope_two = activate_slope(half + wide(bias_two[1 + k], blocks))
        value = jnp.sum(hidden * wide(last[k], blocks), axis=0, keepdims=True) + critic_b3[k]
        known["value", k] = value
        grad_two = split(slope_two)
        yield "mxu", 192
        half = dot3_joint(pair(back, 1 + k), grad_two)
        yield "vpu", 90
        grad_one = split(half * slope_one)
        yield "mxu", 128
        known["pull", k] = dot3_joint(pair(entry, k), grad_one)[8:]

    def mix(first, known):
        for k in range(2):
            yield None, ("value", k)
            yield None, ("pull", k)
        yield "vpu", 10
        gap = (known["value", 1] - known["value", 0]) / SOFT_TEMP
        lean = 0.5 * jnp.tanh(0.5 * gap)
        parts = (0.5 + lean) * known["pull", 0] + (0.5 - lean) * known["pull", 1]
        known["push"] = -known["mask"] * parts

    def step(index, carry):
        tasks = []
        for lane in range(ACTOR_STREAMS):
            first = (index * ACTOR_STREAMS + lane) * blocks
            known = {"begin": 0}
            tasks.append((forward(first, known, lane), known))
            for k in range(2):
                tasks.append((critic(first, known, k), known))
            tasks.append((mix(first, known), known))
        interleave(tasks)
        return carry

    span = ACTOR_STREAMS * width
    lax.fori_loop(0, (count + span - 1) // span, step, 0)

    acc_out[...] = jnp.broadcast_to(jnp.sum(acc_out[...], axis=1, keepdims=True), (HEAD, LANES))
    joined = jnp.concatenate(
        [
            acc_one[:, :JOIN] + acc_one[:, JOIN:],
            acc_head[:, :HEAD] + acc_head[:, HEAD:],
            jnp.sum(acc_side[...], axis=1, keepdims=True),
            jnp.broadcast_to(-jnp.sum(acc_row[0:1, :], keepdims=True), (HID, 1)),
            jnp.zeros((HID, OUT_LANE - JOIN - HEAD - 2), F32),
            jnp.broadcast_to(jnp.transpose(acc_out[...])[0:1, :], (HID, HEAD)),
            jnp.zeros((HID, LANES - OUT_LANE - HEAD), F32),
        ],
        axis=1,
    )
    acc_side[...] = joined
    core = core_ref[0]
    for side, part in ((keep, core), (give, 1 - core)):
        for q in range(peers // 2):
            mine = pl.ds(pl.multiple_of((2 * q + part) * share, 8), share)
            side[q, 0:share, :] = acc_two[mine, 0:LANES]
            side[q, share : 2 * share, :] = acc_two[mine, LANES : 2 * LANES]
            side[q, 2 * share : 3 * share, :] = acc_side[mine, :]


def finish_kernel(critic_in, old, *refs):
    actor_in, best_in, outs = refs[:2], refs[2:4], refs[4:]
    a_one, a_bias_one, a_two, a_bias_two, a_three, a_bias_three = outs[:6]
    c_one, c_bias_one, c_two, c_bias_two, c_three, c_bias_three, g_alpha, new, best = outs[6:]
    peers = critic_in.shape[0]
    share = HID // peers
    depth = old.shape[0]

    def actor_total(start, size):
        value = actor_in[0][start : start + size, :]
        for ref in actor_in[1:]:
            value = value + ref[start : start + size, :]
        return value

    def total(ref, start, size):
        value = ref[0, start : start + size, :]
        for p in range(1, peers):
            value = value + ref[p, start : start + size, :]
        return value

    at = 5 * share
    table = total(critic_in, at, depth)
    new[...] = jnp.where(table > 0.0, table, old[...])
    at += depth
    sums = total(critic_in, at, 8)
    least = critic_in[0, at + 1 : at + 2, :]
    for p in range(1, peers):
        least = jnp.minimum(least, critic_in[p, at + 1 : at + 2, :])
    actor_scale = 1.0 / sums[0:1, :]
    critic_scale = actor_scale * jnp.exp(BETA * jnp.log(least))
    for k in range(2):
        for t in range(2):
            c_two[k, :, t * LANES : (t + 1) * LANES] = critic_scale * total(
                critic_in, (2 * k + t) * share, share
            )
    small = jnp.transpose(critic_scale * total(critic_in, 4 * share, share))
    for k in range(2):
        for j in range(JOIN - 1):
            c_one[j, k : k + 1, :] = small[k * JOIN + j : k * JOIN + j + 1, :]
        c_bias_one[k : k + 1, :] = small[k * JOIN + JOIN - 1 : k * JOIN + JOIN, :]
        c_bias_two[k : k + 1, :] = small[48 + k : 49 + k, :]
        c_three[k : k + 1, :] = small[50 + k : 51 + k, :]
    lane = lax.broadcasted_iota(jnp.int32, (1, LANES), 1)
    both = jnp.where(lane == 0, sums[2:3, :], sums[3:4, :])
    c_bias_three[...] = (critic_scale * both)[:, 0:2]
    for t in range(2):
        a_two[:, t * LANES : (t + 1) * LANES] = actor_scale * actor_total(t * share, share)
    flat = actor_scale * actor_total(2 * share, share)
    small = jnp.transpose(flat)
    for j in range(OBS):
        a_one[j] = small[j : j + 1, :]
    a_bias_one[...] = small[JOIN - 1 : JOIN, :]
    for j in range(ACT):
        a_three[j] = small[JOIN + 1 + j : JOIN + 2 + j, :]
        a_three[ACT + j] = small[JOIN + 9 + j : JOIN + 10 + j, :]
    a_bias_two[...] = small[JOIN + HEAD : JOIN + HEAD + 1, :]
    g_alpha[...] = flat[0:1, JOIN + HEAD + 1 : JOIN + HEAD + 2]
    a_bias_three[:, 0:ACT] = flat[0:1, OUT_LANE + 1 : OUT_LANE + 1 + ACT]
    a_bias_three[:, ACT : 2 * ACT] = flat[0:1, OUT_LANE + 9 : OUT_LANE + 9 + ACT]
    largest = best_in[0][...]
    for ref in best_in[1:]:
        largest = jnp.maximum(largest, ref[...])
    best[...] = largest[:, 0:1]


SMEM = pl.BlockSpec(memory_space=pltpu.SMEM)
HBM = pl.BlockSpec(memory_space=pltpu.HBM)
VMEM = pl.BlockSpec(memory_space=pltpu.VMEM)


def shards(
    states,
    actions,
    rewards,
    next_states,
    dones,
    noise_now,
    noise_next,
    probs,
    valid_counts,
    owners,
    slots,
    old_priorities,
    actor_w1,
    actor_b1,
    actor_w2,
    actor_b2,
    actor_w3,
    actor_b3,
    critic_w1,
    critic_b1,
    critic_w2,
    critic_b2,
    critic_w3,
    critic_b3,
    target_w1,
    target_b1,
    target_w2,
    target_b2,
    target_w3,
    target_b3,
    log_alpha,
):
    peers = lax.axis_size("dp")
    me = lax.axis_index("dp")
    share = HID // peers

    def rows(value):
        return value.reshape(-1, LANES)

    states, actions, next_states = rows(states), rows(actions), rows(next_states)
    noise_now, noise_next = rows(noise_now), rows(noise_next)
    rewards, dones, probs = rows(rewards), rows(dones), rows(probs)
    owners, slots, old = rows(owners), rows(slots), rows(old_priorities)
    depth = old.shape[0]
    actor_one = jnp.transpose(actor_w1, (2, 0, 1))
    actor_three = jnp.transpose(actor_w3, (1, 0, 2))
    critic_one = jnp.transpose(critic_w1[0], (2, 0, 1))
    target_one = jnp.transpose(target_w1[0], (2, 0, 1))
    critic_rows = 5 * share + depth + 8
    actor_rows = 3 * share
    sources = (
        valid_counts,
        log_alpha.reshape(1, 1),
        actor_b3,
        critic_b3,
        target_b3,
        actor_one,
        actor_b1,
        actor_b2,
        actor_three,
        critic_one,
        critic_b1[0],
        critic_b2[0],
        critic_w3[0],
        target_one,
        target_b1[0],
        target_b2[0],
        target_w3[0],
        actor_w2[0],
        target_w2[0],
        critic_w2[0],
        states,
        actions,
        rewards,
        next_states,
        dones,
        noise_next,
        probs,
        owners,
        slots,
    )
    critic_send, small = pl.pallas_call(
        functools.partial(critic_kernel, peers),
        out_shape=(
            jax.ShapeDtypeStruct((peers, critic_rows, LANES), F32),
            jax.ShapeDtypeStruct((SMALL, HID), F32),
        ),
        in_specs=[HBM] * SOURCES,
        out_specs=(VMEM, VMEM),
        scratch_shapes=[
            (pltpu.SMEM if k < 5 else pltpu.VMEM)(source.shape, source.dtype)
            for k, source in enumerate(sources)
        ]
        + [
            pltpu.VMEM((5, HID, 3 * JOIN), BF16),
            pltpu.VMEM((5, 2, HID, HID), BF16),
            pltpu.VMEM((2, 2, HID, HID), BF16),
            pltpu.VMEM((1, 2, HEAD, HID), BF16),
            pltpu.VMEM((5, HID, LANES), F32),
            pltpu.VMEM((4, HID, LANES), F32),
            pltpu.VMEM((HEAD, LANES), F32),
            pltpu.VMEM((2 * CRITIC_STREAMS, JOIN, CRITIC_BLOCKS * LANES), F32),
            pltpu.VMEM((2, HID, HID), F32),
            pltpu.VMEM((2, 2 * JOIN, HID), F32),
            pltpu.VMEM((4, HID, LANES), F32),
            pltpu.VMEM((peers * depth, 2 * LANES), F32),
            pltpu.VMEM((8, CRITIC_BLOCKS * LANES), F32),
            pltpu.VMEM((2 * JOIN + 8, HID), F32),
            pltpu.SemaphoreType.DMA((SOURCES,)),
        ],
        compiler_params=pltpu.CompilerParams(vmem_limit_bytes=CRITIC_LIMIT),
        cost_estimate=pl.CostEstimate(flops=20 * 10**9, bytes_accessed=4 * 10**6, transcendentals=10**7),
        name="critic",
    )(*sources)
    critic_in = lax.all_to_all(critic_send, "dp", split_axis=0, concat_axis=0, tiled=True)
    kept, given = pl.pallas_call(
        functools.partial(actor_kernel, peers),
        out_shape=(jax.ShapeDtypeStruct((peers // 2, actor_rows, LANES), F32),) * 2,
        in_specs=[SMEM] + [VMEM] * 7,
        out_specs=(VMEM, VMEM),
        scratch_shapes=[
            pltpu.VMEM((3, HID, 3 * JOIN), BF16),
            pltpu.VMEM((3, 2, HID, HID), BF16),
            pltpu.VMEM((3, 2, HID, HID), BF16),
            pltpu.VMEM((1, 2, HEAD, HID), BF16),
            pltpu.VMEM((HID, 3 * HEAD), BF16),
            pltpu.VMEM((2, 2, 16, HID), BF16),
            pltpu.VMEM((3, HID, LANES), F32),
            pltpu.VMEM((2, HID, LANES), F32),
            pltpu.VMEM((HEAD, LANES), F32),
            pltpu.VMEM((ACTOR_STREAMS, JOIN, ACTOR_BLOCKS * LANES), F32),
            pltpu.VMEM((HID, HID), F32),
            pltpu.VMEM((HID, 2 * JOIN), F32),
            pltpu.VMEM((HID, 2 * HEAD), F32),
            pltpu.VMEM((HID, LANES), F32),
            pltpu.VMEM((HEAD, LANES), F32),
            pltpu.VMEM((8, ACTOR_BLOCKS * LANES), F32),
        ],
        compiler_params=pltpu.CompilerParams(vmem_limit_bytes=ACTOR_LIMIT),
        cost_estimate=pl.CostEstimate(flops=20 * 10**9, bytes_accessed=4 * 10**6, transcendentals=10**7),
        name="actor",
    )(
        (me % 2).reshape(1),
        valid_counts,
        log_alpha.reshape(1, 1),
        states,
        noise_now,
        small,
        actor_w2[0],
        critic_w2[0],
    )
    at = 5 * share + depth + 4
    best = jnp.max(critic_in[:, at : at + 1, :], axis=0)
    best_in = best
    agents = lax.axis_size("seed")
    spans = (agents - 1).bit_length()
    bits = (peers - 1).bit_length()
    actor_in = lax.ppermute(given, "dp", [(k, k ^ 1) for k in range(peers)])
    for bit in range(1, max(bits, 1 + spans)):
        if bit < bits:
            both = (kept + actor_in).reshape(-1, 2, actor_rows, LANES)
            mine = (me >> bit) & 1
            kept = lax.dynamic_index_in_dim(both, mine, 1, False)
            given = lax.dynamic_index_in_dim(both, 1 - mine, 1, False)
            actor_in = lax.ppermute(given, "dp", [(k, k ^ (1 << bit)) for k in range(peers)])
        if bit <= spans:
            best = jnp.maximum(best, best_in)
            best_in = lax.ppermute(best, "seed", [(k, k ^ (1 << (bit - 1))) for k in range(agents)])
        actor_in, best_in = lax.optimization_barrier((actor_in, best_in))
    actor_parts, bests = (kept[0], actor_in[0]), (best, best_in)
    shape = jax.ShapeDtypeStruct
    outs = pl.pallas_call(
        finish_kernel,
        out_shape=(
            shape((OBS, 1, share), F32),
            shape((1, share), F32),
            shape((share, HID), F32),
            shape((1, share), F32),
            shape((2 * ACT, 1, share), F32),
            shape((1, 2 * ACT), F32),
            shape((JOIN - 1, 2, share), F32),
            shape((2, share), F32),
            shape((2, share, HID), F32),
            shape((2, share), F32),
            shape((2, share), F32),
            shape((1, 2), F32),
            shape((1, 1), F32),
            shape((depth, LANES), F32),
            shape((1, 1), F32),
        ),
        in_specs=[VMEM] * 6,
        out_specs=(VMEM,) * 15,
        compiler_params=pltpu.CompilerParams(vmem_limit_bytes=FINISH_LIMIT),
        name="finish",
    )(critic_in, old, *actor_parts, *bests)
    return (
        jnp.transpose(outs[0], (1, 2, 0)),
        outs[1],
        outs[2][None],
        outs[3],
        jnp.transpose(outs[4], (1, 0, 2)),
        outs[5],
        jnp.transpose(outs[6], (1, 2, 0))[None],
        outs[7][None],
        outs[8][None],
        outs[9][None],
        outs[10][None],
        outs[11],
        outs[12].reshape(1),
        outs[13].reshape(1, -1),
        outs[14].reshape(()),
    )


def solution(mesh):
    token = P("seed", None, "dp")
    line = P("seed", "dp")
    agent = P("seed")
    placed = (
        (token, token, line, token, line, token, token, line, line, line, line, line)
        + (agent,) * 19
    )
    return jax.shard_map(
        shards,
        mesh=mesh,
        in_specs=placed,
        out_specs=(
            P("seed", "dp", None),
            P("seed", "dp"),
            P("seed", "dp", None),
            P("seed", "dp"),
            P("seed", None, "dp"),
            P("seed", None),
            P("seed", None, "dp", None),
            P("seed", None, "dp"),
            P("seed", None, "dp", None),
            P("seed", None, "dp"),
            P("seed", None, "dp"),
            P("seed", None),
            P("seed"),
            P("seed", "dp"),
            P(),
        ),
        check_vma=False,
    )
```

```python
import functools
import math

import jax
import jax.numpy as jnp
from jax import lax
from jax.experimental import pallas as pl
from jax.experimental.pallas import tpu as pltpu
from jax.sharding import PartitionSpec as P

F32 = jnp.float32
BF16 = jnp.bfloat16
GAMMA = 0.99
STD_LO = -5.0
STD_HI = 2.0
ENTROPY_AIM = -6.0
SOFT_TEMP = 0.1
BETA = 0.4
PRIO_EXP = 0.6
PRIO_EPS = 0.001
HALF_LOG_TAU = 0.5 * math.log(2.0 * math.pi)
LOG_TWO = math.log(2.0)

LANES = 128
OBS = 17
ACT = 6
HID = 256
JOIN = 24
OUT_LANE = 48
HEAD_ROW = 3 * JOIN
REST_ROW = HEAD_ROW + 16
BIAS_ROW = REST_ROW + 8
SMALL = BIAS_ROW + 16
HEAD = 16
CRITIC_BLOCKS, CRITIC_STREAMS, CRITIC_LAG = 4, 4, 2000
ACTOR_BLOCKS, ACTOR_STREAMS = 8, 2
SOURCES = 29
CRITIC_LIMIT = 56 * 1024 * 1024
ACTOR_LIMIT = 36 * 1024 * 1024
FINISH_LIMIT = 8 * 1024 * 1024


def dot(left, right):
    return jnp.dot(left, right, preferred_element_type=F32)


def dot_t(left, right):
    return lax.dot_general(left, right, (((1,), (1,)), ((), ())), preferred_element_type=F32)


def split(value):
    high = value.astype(BF16)
    low = (value - high.astype(F32)).astype(BF16)
    return high, low


def split_wide(value):
    high = value.astype(BF16).astype(F32)
    return high, value - high


def dot3(weight, value):
    high, low = value
    return dot(weight[0], high) + dot(weight[0], low) + dot(weight[1], high)


def dot3_joint(weight, value):
    rows = weight[0].shape[0]
    both = dot(jnp.concatenate(weight, axis=0), value[0])
    return both[:rows] + both[rows:] + dot(weight[0], value[1])


def dot3_t(left, right):
    return dot_t(left[0], right[0]) + dot_t(left[0], right[1]) + dot_t(left[1], right[0])


def store_three(ref, value):
    rows = value.shape[0]
    for k, part in enumerate(split_three(value)):
        ref[k * rows : (k + 1) * rows, :] = part.astype(BF16)


def split_rest(value):
    high, low = split(value)
    rest = (value - high.astype(F32) - low.astype(F32)).astype(BF16)
    return high, low, rest


def dot6(weight, value):
    rows = weight.shape[0] // 3
    first = dot(weight, value[0])
    second = dot(weight[: 2 * rows], value[1])
    third = first[2 * rows :] + second[rows:] + dot(weight[:rows], value[2])
    return first[:rows] + ((first[rows : 2 * rows] + second[:rows]) + third)


def wide(column, blocks):
    return jnp.concatenate([column] * blocks, axis=1)


def stack_join(value):
    high, low = split_wide(value)
    return jnp.concatenate([high, low, high], axis=0).astype(BF16)


def split_three(value):
    high, rest = split_wide(value)
    middle, low = split_wide(rest)
    return high, middle, low


def stack_join_three(value):
    high, middle, low = split_three(value)
    return jnp.concatenate([high, middle, low, high, middle, high], axis=0).astype(BF16)


def stack_weight_three(value):
    high, middle, low = split_three(value)
    return jnp.transpose(jnp.concatenate([high, high, high, middle, middle, low], axis=0)).astype(BF16)


def stack_weight(value):
    high, low = split_wide(value)
    return jnp.transpose(jnp.concatenate([high, high, low], axis=0)).astype(BF16)


def activate(half):
    return half * (1.0 + jnp.tanh(half))


def activate_slope(half):
    bent = jnp.tanh(half)
    rise = 1.0 + bent
    hidden = half * rise
    return hidden, rise + hidden * (1.0 - bent)


def interleave(tasks):
    free = {"mxu": 0, "vpu": 0}
    times = {}
    queue = []

    def advance(task, now):
        generator, known = task
        seen = set(known)
        asked = next(generator, None)
        for name in known:
            if name not in seen:
                times[(id(known), name)] = now
        if asked is not None:
            queue.append((now, task, asked))

    for task in tasks:
        advance(task, task[1]["begin"])
    while queue:
        best = None
        for place, (ready, task, (unit, cost)) in enumerate(queue):
            if unit is None:
                if cost not in task[1]:
                    continue
                start = max(ready, times[(id(task[1]), cost)])
            else:
                start = max(ready, free[unit])
            if best is None or start < best[0]:
                best = (start, place)
        start, place = best
        ready, task, (unit, cost) = queue.pop(place)
        if unit is None:
            advance(task, start)
        else:
            cost = cost * 2 if unit == "vpu" else cost
            free[unit] = start + cost
            advance(task, start + cost)


def soft_min(first, second):
    return jnp.minimum(first, second) - SOFT_TEMP * jnp.log(
        1.0 + jnp.exp(-jnp.abs(first - second) / SOFT_TEMP)
    )


def squash(head, noise):
    means, bend = head[:8], jnp.tanh(head[8:])
    log_std = STD_LO + 0.5 * (STD_HI - STD_LO) * (bend + 1.0)
    spread = jnp.exp(log_std) * noise
    pre = means + spread
    action = jnp.tanh(pre)
    size = jnp.abs(pre)
    log_jac = 2.0 * (LOG_TWO - size - jnp.log(1.0 + jnp.exp(-2.0 * size)))
    row = lax.broadcasted_iota(jnp.int32, pre.shape, 0)
    inside = (row >= 1) & (row <= ACT)
    terms = jnp.where(inside, -0.5 * noise * noise - log_std - HALF_LOG_TAU - log_jac, 0.0)
    return action, jnp.sum(terms, axis=0, keepdims=True), spread, bend


def load_rows(ref, count, block):
    blocks = ref.shape[0] // count
    return ref[pl.ds(block, count, stride=blocks), :]


def load_chunk(ref, count, first, blocks):
    return jnp.concatenate([load_rows(ref, count, first + g) for g in range(blocks)], axis=1)


def load_row(ref, first, blocks):
    return jnp.concatenate([ref[pl.ds(first + g, 1), :] for g in range(blocks)], axis=1)


def fill_join(join, obs_ref, act_ref, first):
    blocks = join.shape[1] // LANES
    join[0:OBS, :] = load_chunk(obs_ref, OBS, first, blocks)
    if act_ref is not None:
        join[OBS : OBS + ACT, :] = load_chunk(act_ref, ACT, first, blocks)
    join[JOIN - 1 : JOIN, :] = jnp.ones((1, join.shape[1]), F32)


def with_action(join, action):
    row = lax.broadcasted_iota(jnp.int32, action.shape, 0)
    inside = (row >= 1) & (row <= ACT)
    return jnp.concatenate([join[:16], jnp.where(inside, action, join[16:])], axis=0)


def fill_first(ref, row, weight_ref, bias_row, index):
    rows = weight_ref.shape[0]
    ref[row : row + rows, :] = weight_ref[:, index, :]
    ref[row + JOIN - 1 : row + JOIN, :] = bias_row


def store_split(ref, index, value):
    high, low = split(value)
    ref[index, 0] = high
    ref[index, 1] = low


def pair(ref, index):
    return ref[index, 0], ref[index, 1]


def columns(rows):
    turned = jnp.transpose(rows)
    return [jnp.broadcast_to(turned[:, k : k + 1], (HID, LANES)) for k in range(rows.shape[0])]


def back_weights(weight, scale):
    both = jnp.concatenate([scale, scale], axis=1)
    return jnp.transpose(0.25 * both * weight)


def head_bias(bias_ref):
    row = lax.broadcasted_iota(jnp.int32, (HEAD, LANES), 0)
    out = jnp.zeros((HEAD, LANES), F32)
    for k in range(ACT):
        out = jnp.where(row == 1 + k, bias_ref[0, k], out)
        out = jnp.where(row == 9 + k, bias_ref[0, ACT + k], out)
    return out


def fold(value):
    total = value[:, :LANES]
    for g in range(1, value.shape[1] // LANES):
        total = total + value[:, g * LANES : (g + 1) * LANES]
    return total


def valid_lanes(first, count, width):
    lane = lax.broadcasted_iota(jnp.int32, (1, width), 1)
    return lane + first * LANES < count


def spread_row(value):
    return jnp.broadcast_to(value, (1, LANES))


def critic_kernel(peers, *refs):
    sources, refs = refs[:SOURCES], refs[SOURCES:]
    (send, small), refs = refs[:2], refs[2:]
    places, refs = refs[:SOURCES], refs[SOURCES:]
    one, two, back, head, bias_two, last, wide_bias, join = refs[:8]
    acc_two, acc_one, acc_side, acc_table, acc_row, turn, arrived = refs[8:]
    copies = [
        pltpu.make_async_copy(source, place, arrived.at[k])
        for k, (source, place) in enumerate(zip(sources, places))
    ]
    for copy in copies:
        copy.start()
    count_ref, temper_ref, actor_b3, critic_b3, target_b3 = places[:5]
    actor_w1, actor_b1, actor_b2, actor_w3 = places[5:9]
    critic_w1, critic_b1, critic_b2, critic_w3 = places[9:13]
    target_w1, target_b1, target_b2, target_w3 = places[13:17]
    actor_w2, target_w2, critic_w2 = places[17:20]
    states, actions, rewards, next_states, dones, noise_next, probs, owners, slots = places[20:]
    acc_two[...] = jnp.zeros_like(acc_two)
    acc_one[...] = jnp.zeros_like(acc_one)
    acc_side[...] = jnp.zeros_like(acc_side)
    acc_table[...] = jnp.zeros_like(acc_table)
    acc_row[...] = jnp.zeros_like(acc_row)
    small[...] = jnp.zeros_like(small)
    for copy in copies[:17]:
        copy.wait()
    count = count_ref[0, 0]
    alpha = jnp.exp(temper_ref[0, 0])
    share = HID // peers
    blocks = CRITIC_BLOCKS
    width = blocks * LANES
    depth = acc_table.shape[0] // peers
    fill_first(small, 0, actor_w1, actor_b1[...], 0)
    for k in range(2):
        fill_first(small, (1 + k) * JOIN, critic_w1, critic_b1[k : k + 1, :], k)
        fill_first(turn, k * JOIN, target_w1, target_b1[k : k + 1, :], k)
    small[HEAD_ROW + 1 : HEAD_ROW + 1 + ACT, :] = actor_w3[0:ACT, 0, :]
    small[HEAD_ROW + 9 : HEAD_ROW + 9 + ACT, :] = actor_w3[ACT : 2 * ACT, 0, :]
    small[REST_ROW : REST_ROW + 1, :] = 0.5 * actor_b2[...]
    small[REST_ROW + 1 : REST_ROW + 3, :] = 0.5 * critic_b2[...]
    small[REST_ROW + 3 : REST_ROW + 5, :] = critic_w3[...]
    turn[2 * JOIN : 2 * JOIN + 2, :] = 0.5 * target_b2[...]
    turn[2 * JOIN + 2 : 2 * JOIN + 4, :] = target_w3[...]
    turn[2 * JOIN + 4 : 2 * JOIN + 8, :] = jnp.zeros((4, HID), F32)
    wide_bias[...] = head_bias(actor_b3)
    small[BIAS_ROW : BIAS_ROW + HEAD, 0:LANES] = wide_bias[...]
    for k in range(2):
        small[BIAS_ROW + k : BIAS_ROW + k + 1, LANES:] = jnp.full((1, LANES), critic_b3[0, k])
    store_split(head, 0, small[HEAD_ROW : HEAD_ROW + HEAD, :])
    one[0] = stack_weight(0.5 * small[0:JOIN, :])
    given = columns(small[REST_ROW : REST_ROW + 8, :])
    aims = columns(turn[2 * JOIN : 2 * JOIN + 8, :])
    bias_two[0] = given[0]
    for k in range(2):
        one[1 + k] = stack_weight(0.5 * turn[k * JOIN : (k + 1) * JOIN, :])
        one[3 + k] = stack_weight(0.5 * small[(1 + k) * JOIN : (2 + k) * JOIN, :])
        bias_two[1 + k] = aims[k]
        bias_two[3 + k] = given[1 + k]
        last[k] = aims[2 + k]
        last[2 + k] = given[3 + k]
    for copy in copies[17:20]:
        copy.wait()
    store_split(two, 0, 0.5 * actor_w2[...])
    for k in range(2):
        store_split(two, 1 + k, 0.5 * target_w2[k])
        store_split(two, 3 + k, 0.5 * critic_w2[k])
        store_split(back, k, back_weights(critic_w2[k], last[2 + k]))
    for copy in copies[20:]:
        copy.wait()

    def next_action(first, known, lane):
        yield "mxu", 64
        fill_join(join.at[lane], next_states, None, first)
        join[lane, OBS : OBS + ACT, :] = jnp.zeros((ACT, width), F32)
        nexts = join[lane]
        half = dot(one[0], stack_join(nexts))
        yield "vpu", 110
        hidden = split(activate(half))
        yield "mxu", 192
        half = dot3(pair(two, 0), hidden)
        yield "vpu", 130
        hidden = split(activate(half + wide(bias_two[0], blocks)))
        yield "mxu", 128
        out = dot3_joint(pair(head, 0), hidden)
        yield "vpu", 100
        join[lane, OBS : OBS + ACT, :] = load_chunk(noise_next, ACT, first, blocks)
        action, known["logp"], _, _ = squash(out + wide(wide_bias[...], blocks), join[lane, 16:24, :])
        known["given_next"] = stack_join(with_action(nexts, action))

    def target_value(first, known, k):
        yield None, "given_next"
        yield "mxu", 64
        half = dot(one[1 + k], known["given_next"])
        yield "vpu", 110
        hidden = split(activate(half))
        yield "mxu", 192
        half = dot3(pair(two, 1 + k), hidden)
        yield "vpu", 120
        hidden = activate(half + wide(bias_two[1 + k], blocks))
        total = jnp.sum(hidden * wide(last[k], blocks), axis=0, keepdims=True)
        known["next", k] = total + target_b3[0, k]

    def target_row(first, known):
        yield None, "logp"
        yield None, ("next", 0)
        yield None, ("next", 1)
        yield "vpu", 40
        keep = GAMMA * (1.0 - load_row(dones, first, blocks).astype(F32))
        worth = soft_min(known["next", 0], known["next", 1]) - alpha * known["logp"]
        known["target"] = load_row(rewards, first, blocks) + keep * worth
        known["valid"] = valid_lanes(first, count, width)
        coef = jnp.exp(-BETA * jnp.log(load_row(probs, first, blocks)))
        known["coef"] = jnp.where(known["valid"], coef, 0.0)

    def given_now(first, known, lane):
        yield "vpu", 20
        fill_join(join.at[lane], states, actions, first)
        known["given"] = stack_join(join[lane])

    def critic(first, known, k):
        yield None, "given"
        given = known["given"]
        yield "mxu", 64
        half = dot(one[3 + k], given)
        yield "vpu", 160
        hidden, slope_one = activate_slope(half)
        hidden_one = split(hidden)
        yield "mxu", 192
        half = dot3(pair(two, 3 + k), hidden_one)
        yield "vpu", 170
        hidden, slope_two = activate_slope(half + wide(bias_two[3 + k], blocks))
        value = jnp.sum(hidden * wide(last[2 + k], blocks), axis=0, keepdims=True) + critic_b3[0, k]
        yield None, "target"
        yield "vpu", 160
        error = value - known["target"]
        known["error", k] = error
        scaled = known["coef"] * error
        grad = scaled * slope_two
        acc_side[k] += fold(grad)
        acc_side[2 + k] += fold(scaled * hidden)
        acc_row[k : k + 1, :] += scaled
        grad_two = split(grad)
        yield "mxu", 192
        half = dot3(pair(back, k), grad_two)
        yield "vpu", 90
        grad_one = split(half * slope_one)
        yield "mxu", 192
        acc_two[k] += dot3_t(grad_two, hidden_one)
        yield "mxu", 128
        acc_one[k] += dot_t(given[:48], grad_one[0]) + dot_t(given[:48], grad_one[1])

    def priorities(first, known):
        yield None, ("error", 0)
        yield None, ("error", 1)
        yield "vpu", 120
        delta = 0.5 * (known["error", 0] + known["error", 1])
        priority = jnp.exp(PRIO_EXP * jnp.log(jnp.abs(delta) + PRIO_EPS))
        priority = jnp.where(known["valid"], priority, 0.0)
        acc_row[2:3, :] = jnp.maximum(acc_row[2:3, :], priority)
        slot = load_row(slots, first, blocks)
        place = load_row(owners, first, blocks) * depth + lax.shift_right_logical(slot, 7)
        lane = slot & (LANES - 1)
        rows = acc_table.shape[0]
        row_hit = lax.broadcasted_iota(jnp.int32, (rows, width), 0) == place
        lane_hit = lax.broadcasted_iota(jnp.int32, (LANES, width), 0) == lane
        high, low = split_wide(priority)
        picked = jnp.concatenate(
            [jnp.where(lane_hit, high, 0.0), jnp.where(lane_hit, low, 0.0)], axis=0
        ).astype(BF16)
        hits = jnp.where(row_hit, 1.0, 0.0).astype(BF16)
        yield "mxu", 64
        acc_table[...] += dot_t(hits, picked)

    def step(index, carry):
        tasks = []
        for lane in range(CRITIC_STREAMS):
            first = (index * CRITIC_STREAMS + lane) * blocks
            known = {"begin": CRITIC_LAG * (2 * lane // CRITIC_STREAMS)}
            tasks.append((next_action(first, known, 2 * lane), known))
            tasks.append((given_now(first, known, 2 * lane + 1), known))
            for k in range(2):
                tasks.append((critic(first, known, k), known))
            for k in range(2):
                tasks.append((target_value(first, known, k), known))
            tasks.append((target_row(first, known), known))
            tasks.append((priorities(first, known), known))
        interleave(tasks)
        return carry

    span = CRITIC_STREAMS * width
    lax.fori_loop(0, (count + span - 1) // span, step, 0)

    for k in range(2):
        acc_side[k] = 0.5 * last[2 + k] * acc_side[k]
    side = [jnp.sum(acc_side[k], axis=1, keepdims=True) for k in range(4)]
    small = [jnp.transpose(acc_one[k][:JOIN] + acc_one[k][JOIN:]) for k in range(2)]
    joined = jnp.concatenate(small + side + [jnp.zeros((HID, LANES - 52), F32)], axis=1)
    acc_side[0] = joined
    lane = lax.broadcasted_iota(jnp.int32, probs.shape, 1)
    row = lax.broadcasted_iota(jnp.int32, probs.shape, 0)
    least = jnp.min(jnp.where(row * LANES + lane < count, probs[...], 1.0), keepdims=True)
    best = jnp.max(acc_row[2:3, :], keepdims=True)
    sums = jnp.concatenate(
        [
            jnp.full((1, LANES), count.astype(F32)),
            spread_row(least),
            spread_row(jnp.sum(acc_row[0:1, :], keepdims=True)),
            spread_row(jnp.sum(acc_row[1:2, :], keepdims=True)),
            spread_row(best),
            jnp.zeros((3, LANES), F32),
        ],
        axis=0,
    )
    table = acc_table[:, :LANES] + acc_table[:, LANES:]
    for p in range(peers):
        mine = slice(p * share, (p + 1) * share)
        at = 0
        for k in range(2):
            for t in range(2):
                block = acc_two[k, mine, t * LANES : (t + 1) * LANES]
                send[p, at : at + share, :] = 0.5 * last[2 + k, mine, :] * block
                at += share
        send[p, at : at + share, :] = acc_side[0, mine, :]
        at += share
        send[p, at : at + depth, :] = table[p * depth : (p + 1) * depth]
        at += depth
        send[p, at : at + 8, :] = sums


def halvings(peers):
    bits = list(range(1, (peers - 1).bit_length()))
    turn = len(bits) // 2
    return bits, bits[turn:] + bits[:turn]


def actor_kernel(
    peers,
    core_ref,
    count_ref,
    temper_ref,
    states,
    noise_now,
    small,
    actor_w2,
    critic_w2,
    keep,
    give,
    one,
    two,
    back,
    head_back,
    entry,
    bias_two,
    last,
    wide_bias,
    join,
    acc_two,
    acc_one,
    acc_head,
    acc_side,
    acc_out,
    acc_row,
    actor_first,
    actor_second,
    actor_head,
):
    count = jnp.max(count_ref[...].astype(F32)).astype(jnp.int32)
    alpha = jnp.exp(temper_ref[...])
    share = HID // peers
    blocks = ACTOR_BLOCKS
    width = blocks * LANES
    given = columns(small[REST_ROW : REST_ROW + 8, :])
    final = small[HEAD_ROW : HEAD_ROW + HEAD, :]
    store_three(actor_second, 0.5 * actor_w2[...])
    store_split(back, 0, jnp.transpose(0.5 * actor_w2[...]))
    bias_two[0] = given[0]
    actor_first[...] = stack_weight_three(0.5 * small[0:JOIN, :])
    for k in range(2):
        first = (1 + k) * JOIN
        one[1 + k] = stack_weight(0.5 * small[first : first + JOIN, :])
        store_split(entry, k, small[first + 8 : first + 24, :])
        store_split(two, 1 + k, 0.5 * critic_w2[k])
        bias_two[1 + k] = given[1 + k]
        last[k] = given[3 + k]
        store_split(back, 1 + k, back_weights(critic_w2[k], last[k]))
    store_three(actor_head, final)
    head_back[...] = stack_weight(0.5 * final)
    wide_bias[...] = small[BIAS_ROW : BIAS_ROW + HEAD, 0:LANES]
    critic_b3 = [small[BIAS_ROW + k : BIAS_ROW + k + 1, LANES : LANES + 1] for k in range(2)]
    acc_two[...] = jnp.zeros_like(acc_two)
    acc_one[...] = jnp.zeros_like(acc_one)
    acc_head[...] = jnp.zeros_like(acc_head)
    acc_side[...] = jnp.zeros_like(acc_side)
    acc_out[...] = jnp.zeros_like(acc_out)
    acc_row[...] = jnp.zeros_like(acc_row)

    row = lax.broadcasted_iota(jnp.int32, (8, width), 0)
    inside = (row >= 1) & (row <= ACT)

    def forward(first, known, lane):
        yield "mxu", 64
        valid = valid_lanes(first, count, width)
        known["mask"] = jnp.where(valid, 1.0, 0.0)
        fill_join(join.at[lane], states, noise_now, first)
        noise = join[lane, 16:24, :]
        tail = jnp.where(inside, 0.0, noise)
        given = stack_join_three(jnp.concatenate([join[lane, 0:16, :], tail], axis=0))
        half = dot(actor_first[...], given)
        yield "vpu", 160
        hidden, slope_one = activate_slope(half)
        hidden_one = split_rest(hidden)
        yield "mxu", 384
        half = dot6(actor_second[...], hidden_one)
        yield "vpu", 170
        hidden, slope_two = activate_slope(half + wide(bias_two[0], blocks))
        hidden_two = split_rest(hidden)
        yield "mxu", 192
        out = dot6(actor_head[...], hidden_two)
        yield "vpu", 100
        action, logp, spread, bend = squash(out + wide(wide_bias[...], blocks), noise)
        acc_row[0:1, :] += known["mask"] * (logp + ENTROPY_AIM)
        known["fresh"] = stack_join(with_action(join[lane], action))
        yield None, "push"
        yield "vpu", 60
        push = known["push"]
        pull = alpha * known["mask"]
        grad_pre = jnp.where(inside, 2.0 * pull * action + push * (1.0 - action * action), 0.0)
        grad_std = jnp.where(inside, grad_pre * spread - pull, 0.0)
        grad_bend = 0.5 * (STD_HI - STD_LO) * grad_std * (1.0 - bend * bend)
        grad_out = jnp.concatenate([grad_pre, grad_bend], axis=0)
        acc_out[...] += fold(grad_out)
        outs = stack_join(grad_out)
        yield "mxu", 64
        half = dot(head_back[...], outs)
        yield "vpu", 100
        grad = half * slope_two
        acc_side[...] += fold(grad)
        grad_two = split(grad)
        yield "mxu", 192
        half = dot3_joint(pair(back, 0), grad_two)
        yield "vpu", 90
        grad_one = split(half * slope_one)
        yield "mxu", 128
        acc_head[...] += dot_t(hidden_two[0], outs[:32]) + dot_t(hidden_two[1], outs[:32])
        yield "mxu", 192
        acc_two[...] += dot3_t(grad_two, hidden_one)
        yield "mxu", 128
        acc_one[...] += dot_t(grad_one[0], given[:48]) + dot_t(grad_one[1], given[:48])

    def critic(first, known, k):
        yield None, "fresh"
        yield "mxu", 64
        half = dot(one[1 + k], known["fresh"])
        yield "vpu", 160
        hidden, slope_one = activate_slope(half)
        hidden_one = split(hidden)
        yield "mxu", 192
        half = dot3_joint(pair(two, 1 + k), hidden_one)
        yield "vpu", 220
        hidden, slope_two = activate_slope(half + wide(bias_two[1 + k], blocks))
        value = jnp.sum(hidden * wide(last[k], blocks), axis=0, keepdims=True) + critic_b3[k]
        known["value", k] = value
        grad_two = split(slope_two)
        yield "mxu", 192
        half = dot3_joint(pair(back, 1 + k), grad_two)
        yield "vpu", 90
        grad_one = split(half * slope_one)
        yield "mxu", 128
        known["pull", k] = dot3_joint(pair(entry, k), grad_one)[8:]

    def mix(first, known):
        for k in range(2):
            yield None, ("value", k)
            yield None, ("pull", k)
        yield "vpu", 10
        gap = (known["value", 1] - known["value", 0]) / SOFT_TEMP
        lean = 0.5 * jnp.tanh(0.5 * gap)
        parts = (0.5 + lean) * known["pull", 0] + (0.5 - lean) * known["pull", 1]
        known["push"] = -known["mask"] * parts

    def step(index, carry):
        tasks = []
        for lane in range(ACTOR_STREAMS):
            first = (index * ACTOR_STREAMS + lane) * blocks
            known = {"begin": 0}
            tasks.append((forward(first, known, lane), known))
            for k in range(2):
                tasks.append((critic(first, known, k), known))
            tasks.append((mix(first, known), known))
        interleave(tasks)
        return carry

    span = ACTOR_STREAMS * width
    lax.fori_loop(0, (count + span - 1) // span, step, 0)

    acc_out[...] = jnp.broadcast_to(jnp.sum(acc_out[...], axis=1, keepdims=True), (HEAD, LANES))
    joined = jnp.concatenate(
        [
            acc_one[:, :JOIN] + acc_one[:, JOIN:],
            acc_head[:, :HEAD] + acc_head[:, HEAD:],
            jnp.sum(acc_side[...], axis=1, keepdims=True),
            jnp.broadcast_to(-jnp.sum(acc_row[0:1, :], keepdims=True), (HID, 1)),
            jnp.zeros((HID, OUT_LANE - JOIN - HEAD - 2), F32),
            jnp.broadcast_to(jnp.transpose(acc_out[...])[0:1, :], (HID, HEAD)),
            jnp.zeros((HID, LANES - OUT_LANE - HEAD), F32),
        ],
        axis=1,
    )
    acc_side[...] = joined
    core = core_ref[0]
    orders = halvings(peers)
    for side, part in ((keep, core), (give, 1 - core)):
        for q in range(peers // 2):
            chips = [sum(((q >> j) & 1) << (bit - 1) for j, bit in enumerate(order)) for order in orders]
            chip = chips[0] + part * (chips[1] - chips[0])
            mine = pl.ds(pl.multiple_of((2 * chip + part) * share, 8), share)
            side[q, 0:share, :] = acc_two[mine, 0:LANES]
            side[q, share : 2 * share, :] = acc_two[mine, LANES : 2 * LANES]
            side[q, 2 * share : 3 * share, :] = acc_side[mine, :]


def finish_kernel(critic_in, old, *refs):
    actor_in, best_in, outs = refs[:2], refs[2:4], refs[4:]
    a_one, a_bias_one, a_two, a_bias_two, a_three, a_bias_three = outs[:6]
    c_one, c_bias_one, c_two, c_bias_two, c_three, c_bias_three, g_alpha, new, best = outs[6:]
    peers = critic_in.shape[0]
    share = HID // peers
    depth = old.shape[0]

    def actor_total(start, size):
        value = actor_in[0][start : start + size, :]
        for ref in actor_in[1:]:
            value = value + ref[start : start + size, :]
        return value

    def total(ref, start, size):
        value = ref[0, start : start + size, :]
        for p in range(1, peers):
            value = value + ref[p, start : start + size, :]
        return value

    at = 5 * share
    table = total(critic_in, at, depth)
    new[...] = jnp.where(table > 0.0, table, old[...])
    at += depth
    sums = total(critic_in, at, 8)
    least = critic_in[0, at + 1 : at + 2, :]
    for p in range(1, peers):
        least = jnp.minimum(least, critic_in[p, at + 1 : at + 2, :])
    actor_scale = 1.0 / sums[0:1, :]
    critic_scale = actor_scale * jnp.exp(BETA * jnp.log(least))
    for k in range(2):
        for t in range(2):
            c_two[k, :, t * LANES : (t + 1) * LANES] = critic_scale * total(
                critic_in, (2 * k + t) * share, share
            )
    small = jnp.transpose(critic_scale * total(critic_in, 4 * share, share))
    for k in range(2):
        for j in range(JOIN - 1):
            c_one[j, k : k + 1, :] = small[k * JOIN + j : k * JOIN + j + 1, :]
        c_bias_one[k : k + 1, :] = small[k * JOIN + JOIN - 1 : k * JOIN + JOIN, :]
        c_bias_two[k : k + 1, :] = small[48 + k : 49 + k, :]
        c_three[k : k + 1, :] = small[50 + k : 51 + k, :]
    lane = lax.broadcasted_iota(jnp.int32, (1, LANES), 1)
    both = jnp.where(lane == 0, sums[2:3, :], sums[3:4, :])
    c_bias_three[...] = (critic_scale * both)[:, 0:2]
    for t in range(2):
        a_two[:, t * LANES : (t + 1) * LANES] = actor_scale * actor_total(t * share, share)
    flat = actor_scale * actor_total(2 * share, share)
    small = jnp.transpose(flat)
    for j in range(OBS):
        a_one[j] = small[j : j + 1, :]
    a_bias_one[...] = small[JOIN - 1 : JOIN, :]
    for j in range(ACT):
        a_three[j] = small[JOIN + 1 + j : JOIN + 2 + j, :]
        a_three[ACT + j] = small[JOIN + 9 + j : JOIN + 10 + j, :]
    a_bias_two[...] = small[JOIN + HEAD : JOIN + HEAD + 1, :]
    g_alpha[...] = flat[0:1, JOIN + HEAD + 1 : JOIN + HEAD + 2]
    a_bias_three[:, 0:ACT] = flat[0:1, OUT_LANE + 1 : OUT_LANE + 1 + ACT]
    a_bias_three[:, ACT : 2 * ACT] = flat[0:1, OUT_LANE + 9 : OUT_LANE + 9 + ACT]
    largest = best_in[0][...]
    for ref in best_in[1:]:
        largest = jnp.maximum(largest, ref[...])
    best[...] = largest[:, 0:1]


SMEM = pl.BlockSpec(memory_space=pltpu.SMEM)
HBM = pl.BlockSpec(memory_space=pltpu.HBM)
VMEM = pl.BlockSpec(memory_space=pltpu.VMEM)


def shards(
    states,
    actions,
    rewards,
    next_states,
    dones,
    noise_now,
    noise_next,
    probs,
    valid_counts,
    owners,
    slots,
    old_priorities,
    actor_w1,
    actor_b1,
    actor_w2,
    actor_b2,
    actor_w3,
    actor_b3,
    critic_w1,
    critic_b1,
    critic_w2,
    critic_b2,
    critic_w3,
    critic_b3,
    target_w1,
    target_b1,
    target_w2,
    target_b2,
    target_w3,
    target_b3,
    log_alpha,
):
    peers = lax.axis_size("dp")
    me = lax.axis_index("dp")
    share = HID // peers

    def rows(value):
        return value.reshape(-1, LANES)

    states, actions, next_states = rows(states), rows(actions), rows(next_states)
    noise_now, noise_next = rows(noise_now), rows(noise_next)
    rewards, dones, probs = rows(rewards), rows(dones), rows(probs)
    owners, slots, old = rows(owners), rows(slots), rows(old_priorities)
    depth = old.shape[0]
    actor_one = jnp.transpose(actor_w1, (2, 0, 1))
    actor_three = jnp.transpose(actor_w3, (1, 0, 2))
    critic_one = jnp.transpose(critic_w1[0], (2, 0, 1))
    target_one = jnp.transpose(target_w1[0], (2, 0, 1))
    critic_rows = 5 * share + depth + 8
    actor_rows = 3 * share
    sources = (
        valid_counts,
        log_alpha.reshape(1, 1),
        actor_b3,
        critic_b3,
        target_b3,
        actor_one,
        actor_b1,
        actor_b2,
        actor_three,
        critic_one,
        critic_b1[0],
        critic_b2[0],
        critic_w3[0],
        target_one,
        target_b1[0],
        target_b2[0],
        target_w3[0],
        actor_w2[0],
        target_w2[0],
        critic_w2[0],
        states,
        actions,
        rewards,
        next_states,
        dones,
        noise_next,
        probs,
        owners,
        slots,
    )
    critic_send, small = pl.pallas_call(
        functools.partial(critic_kernel, peers),
        out_shape=(
            jax.ShapeDtypeStruct((peers, critic_rows, LANES), F32),
            jax.ShapeDtypeStruct((SMALL, HID), F32),
        ),
        in_specs=[HBM] * SOURCES,
        out_specs=(VMEM, VMEM),
        scratch_shapes=[
            (pltpu.SMEM if k < 5 else pltpu.VMEM)(source.shape, source.dtype)
            for k, source in enumerate(sources)
        ]
        + [
            pltpu.VMEM((5, HID, 3 * JOIN), BF16),
            pltpu.VMEM((5, 2, HID, HID), BF16),
            pltpu.VMEM((2, 2, HID, HID), BF16),
            pltpu.VMEM((1, 2, HEAD, HID), BF16),
            pltpu.VMEM((5, HID, LANES), F32),
            pltpu.VMEM((4, HID, LANES), F32),
            pltpu.VMEM((HEAD, LANES), F32),
            pltpu.VMEM((2 * CRITIC_STREAMS, JOIN, CRITIC_BLOCKS * LANES), F32),
            pltpu.VMEM((2, HID, HID), F32),
            pltpu.VMEM((2, 2 * JOIN, HID), F32),
            pltpu.VMEM((4, HID, LANES), F32),
            pltpu.VMEM((peers * depth, 2 * LANES), F32),
            pltpu.VMEM((8, CRITIC_BLOCKS * LANES), F32),
            pltpu.VMEM((2 * JOIN + 8, HID), F32),
            pltpu.SemaphoreType.DMA((SOURCES,)),
        ],
        compiler_params=pltpu.CompilerParams(vmem_limit_bytes=CRITIC_LIMIT),
        cost_estimate=pl.CostEstimate(flops=20 * 10**9, bytes_accessed=4 * 10**6, transcendentals=10**7),
        name="critic",
    )(*sources)
    critic_in = lax.all_to_all(critic_send, "dp", split_axis=0, concat_axis=0, tiled=True)
    kept, given = pl.pallas_call(
        functools.partial(actor_kernel, peers),
        out_shape=(jax.ShapeDtypeStruct((peers // 2, actor_rows, LANES), F32),) * 2,
        in_specs=[SMEM] + [VMEM] * 7,
        out_specs=(VMEM, VMEM),
        scratch_shapes=[
            pltpu.VMEM((3, HID, 3 * JOIN), BF16),
            pltpu.VMEM((3, 2, HID, HID), BF16),
            pltpu.VMEM((3, 2, HID, HID), BF16),
            pltpu.VMEM((HID, 3 * HEAD), BF16),
            pltpu.VMEM((2, 2, 16, HID), BF16),
            pltpu.VMEM((3, HID, LANES), F32),
            pltpu.VMEM((2, HID, LANES), F32),
            pltpu.VMEM((HEAD, LANES), F32),
            pltpu.VMEM((ACTOR_STREAMS, JOIN, ACTOR_BLOCKS * LANES), F32),
            pltpu.VMEM((HID, HID), F32),
            pltpu.VMEM((HID, 2 * JOIN), F32),
            pltpu.VMEM((HID, 2 * HEAD), F32),
            pltpu.VMEM((HID, LANES), F32),
            pltpu.VMEM((HEAD, LANES), F32),
            pltpu.VMEM((8, ACTOR_BLOCKS * LANES), F32),
            pltpu.VMEM((HID, 6 * JOIN), BF16),
            pltpu.VMEM((3 * HID, HID), BF16),
            pltpu.VMEM((3 * HEAD, HID), BF16),
        ],
        compiler_params=pltpu.CompilerParams(vmem_limit_bytes=ACTOR_LIMIT),
        cost_estimate=pl.CostEstimate(flops=20 * 10**9, bytes_accessed=4 * 10**6, transcendentals=10**7),
        name="actor",
    )(
        (me % 2).reshape(1),
        valid_counts,
        log_alpha.reshape(1, 1),
        states,
        noise_now,
        small,
        actor_w2[0],
        critic_w2[0],
    )
    at = 5 * share + depth + 4
    best = jnp.max(critic_in[:, at : at + 1, :], axis=0)
    best_in = best
    agents = lax.axis_size("seed")
    spans = (agents - 1).bit_length()
    orders = halvings(peers)
    actor_in = lax.ppermute(given, "dp", [(k, k ^ 1) for k in range(peers)])
    for step in range(max(len(orders[0]), spans)):
        if step < len(orders[0]):
            both = (kept + actor_in).reshape(-1, 2, actor_rows, LANES)
            first, second = orders[0][step], orders[1][step]
            mine = jnp.where(me % 2 == 0, me >> first, me >> second) & 1
            kept = lax.dynamic_index_in_dim(both, mine, 1, False)
            given = lax.dynamic_index_in_dim(both, 1 - mine, 1, False)
            pairs = [(k, k ^ (1 << (second if k % 2 else first))) for k in range(peers)]
            actor_in = lax.ppermute(given, "dp", pairs)
        if step < spans:
            best = jnp.maximum(best, best_in)
            far = 1 << (spans - 1 - step)
            best_in = lax.ppermute(best, "seed", [(k, k ^ far) for k in range(agents)])
        actor_in, best_in = lax.optimization_barrier((actor_in, best_in))
    actor_parts, bests = (kept[0], actor_in[0]), (best, best_in)
    shape = jax.ShapeDtypeStruct
    outs = pl.pallas_call(
        finish_kernel,
        out_shape=(
            shape((OBS, 1, share), F32),
            shape((1, share), F32),
            shape((share, HID), F32),
            shape((1, share), F32),
            shape((2 * ACT, 1, share), F32),
            shape((1, 2 * ACT), F32),
            shape((JOIN - 1, 2, share), F32),
            shape((2, share), F32),
            shape((2, share, HID), F32),
            shape((2, share), F32),
            shape((2, share), F32),
            shape((1, 2), F32),
            shape((1, 1), F32),
            shape((depth, LANES), F32),
            shape((1, 1), F32),
        ),
        in_specs=[VMEM] * 6,
        out_specs=(VMEM,) * 15,
        compiler_params=pltpu.CompilerParams(vmem_limit_bytes=FINISH_LIMIT),
        name="finish",
    )(critic_in, old, *actor_parts, *bests)
    return (
        jnp.transpose(outs[0], (1, 2, 0)),
        outs[1],
        outs[2][None],
        outs[3],
        jnp.transpose(outs[4], (1, 0, 2)),
        outs[5],
        jnp.transpose(outs[6], (1, 2, 0))[None],
        outs[7][None],
        outs[8][None],
        outs[9][None],
        outs[10][None],
        outs[11],
        outs[12].reshape(1),
        outs[13].reshape(1, -1),
        outs[14].reshape(()),
    )


def solution(mesh):
    token = P("seed", None, "dp")
    line = P("seed", "dp")
    agent = P("seed")
    placed = (
        (token, token, line, token, line, token, token, line, line, line, line, line)
        + (agent,) * 19
    )
    return jax.shard_map(
        shards,
        mesh=mesh,
        in_specs=placed,
        out_specs=(
            P("seed", "dp", None),
            P("seed", "dp"),
            P("seed", "dp", None),
            P("seed", "dp"),
            P("seed", None, "dp"),
            P("seed", None),
            P("seed", None, "dp", None),
            P("seed", None, "dp"),
            P("seed", None, "dp", None),
            P("seed", None, "dp"),
            P("seed", None, "dp"),
            P("seed", None),
            P("seed"),
            P("seed", "dp"),
            P(),
        ),
        check_vma=False,
    )
```

```python
import functools
import math

import jax
import jax.numpy as jnp
from jax import lax
from jax.experimental import pallas as pl
from jax.experimental.pallas import tpu as pltpu
from jax.sharding import PartitionSpec as P

F32 = jnp.float32
BF16 = jnp.bfloat16
GAMMA = 0.99
STD_LO = -5.0
STD_HI = 2.0
ENTROPY_AIM = -6.0
SOFT_TEMP = 0.1
BETA = 0.4
PRIO_EXP = 0.6
PRIO_EPS = 0.001
HALF_LOG_TAU = 0.5 * math.log(2.0 * math.pi)
LOG_TWO = math.log(2.0)

LANES = 128
OBS = 17
ACT = 6
HID = 256
JOIN = 24
OUT_LANE = 48
HEAD_ROW = 3 * JOIN
REST_ROW = HEAD_ROW + 16
BIAS_ROW = REST_ROW + 8
SMALL = BIAS_ROW + 16
HEAD = 16
CRITIC_BLOCKS, CRITIC_STREAMS, CRITIC_LAG = 4, 4, 2600
ACTOR_BLOCKS, ACTOR_STREAMS = 8, 2
SOURCES = 29
CRITIC_LIMIT = 56 * 1024 * 1024
ACTOR_LIMIT = 36 * 1024 * 1024
FINISH_LIMIT = 8 * 1024 * 1024


def dot(left, right):
    return jnp.dot(left, right, preferred_element_type=F32)


def dot_t(left, right):
    return lax.dot_general(left, right, (((1,), (1,)), ((), ())), preferred_element_type=F32)


def split(value):
    high = value.astype(BF16)
    low = (value - high.astype(F32)).astype(BF16)
    return high, low


def split_wide(value):
    high = value.astype(BF16).astype(F32)
    return high, value - high


def dot3(weight, value):
    high, low = value
    return dot(weight[0], high) + dot(weight[0], low) + dot(weight[1], high)


def dot3_joint(weight, value):
    rows = weight[0].shape[0]
    both = dot(jnp.concatenate(weight, axis=0), value[0])
    return both[:rows] + both[rows:] + dot(weight[0], value[1])


def dot3_t(left, right):
    return dot_t(left[0], right[0]) + dot_t(left[0], right[1]) + dot_t(left[1], right[0])


def store_three(ref, value):
    rows = value.shape[0]
    for k, part in enumerate(split_three(value)):
        ref[k * rows : (k + 1) * rows, :] = part.astype(BF16)


def split_rest(value):
    high, low = split(value)
    rest = (value - high.astype(F32) - low.astype(F32)).astype(BF16)
    return high, low, rest


def dot6(weight, value):
    rows = weight.shape[0] // 3
    first = dot(weight, value[0])
    second = dot(weight[: 2 * rows], value[1])
    third = first[2 * rows :] + second[rows:] + dot(weight[:rows], value[2])
    return first[:rows] + ((first[rows : 2 * rows] + second[:rows]) + third)


def sum_parts(value):
    rows = value.shape[0] // 2
    return value[:rows] + value[rows:]


def wide(column, blocks):
    return jnp.concatenate([column] * blocks, axis=1)


def stack_join(value):
    high, low = split_wide(value)
    return jnp.concatenate([high, low, high], axis=0).astype(BF16)


def split_three(value):
    high, rest = split_wide(value)
    middle, low = split_wide(rest)
    return high, middle, low


def stack_join_three(value):
    high, middle, low = split_three(value)
    return jnp.concatenate([high, middle, low, high, middle, high], axis=0).astype(BF16)


def stack_weight_three(value):
    high, middle, low = split_three(value)
    return jnp.transpose(jnp.concatenate([high, high, high, middle, middle, low], axis=0)).astype(BF16)


def stack_weight(value):
    high, low = split_wide(value)
    return jnp.transpose(jnp.concatenate([high, high, low], axis=0)).astype(BF16)


def activate(half):
    return half * (1.0 + jnp.tanh(half))


def activate_slope(half):
    bent = jnp.tanh(half)
    rise = 1.0 + bent
    hidden = half * rise
    return hidden, rise + hidden * (1.0 - bent)


def interleave(tasks):
    free = {"mxu": 0, "vpu": 0}
    times = {}
    queue = []

    def advance(task, now):
        generator, known = task
        seen = set(known)
        asked = next(generator, None)
        for name in known:
            if name not in seen:
                times[(id(known), name)] = now
        if asked is not None:
            queue.append((now, task, asked))

    for task in tasks:
        advance(task, task[1]["begin"])
    while queue:
        best = None
        for place, (ready, task, (unit, cost)) in enumerate(queue):
            if unit is None:
                if cost not in task[1]:
                    continue
                start = max(ready, times[(id(task[1]), cost)])
            else:
                start = max(ready, free[unit])
            if best is None or start < best[0]:
                best = (start, place)
        start, place = best
        ready, task, (unit, cost) = queue.pop(place)
        if unit is None:
            advance(task, start)
        else:
            cost = cost * 2 if unit == "vpu" else cost
            free[unit] = start + cost
            advance(task, start + cost)


def soft_min(first, second):
    return jnp.minimum(first, second) - SOFT_TEMP * jnp.log(
        1.0 + jnp.exp(-jnp.abs(first - second) / SOFT_TEMP)
    )


def squash(head, noise):
    means, bend = head[:8], jnp.tanh(head[8:])
    log_std = STD_LO + 0.5 * (STD_HI - STD_LO) * (bend + 1.0)
    spread = jnp.exp(log_std) * noise
    pre = means + spread
    action = jnp.tanh(pre)
    size = jnp.abs(pre)
    log_jac = 2.0 * (LOG_TWO - size - jnp.log(1.0 + jnp.exp(-2.0 * size)))
    row = lax.broadcasted_iota(jnp.int32, pre.shape, 0)
    inside = (row >= 1) & (row <= ACT)
    terms = jnp.where(inside, -0.5 * noise * noise - log_std - HALF_LOG_TAU - log_jac, 0.0)
    return action, jnp.sum(terms, axis=0, keepdims=True), spread, bend


def load_rows(ref, count, block):
    blocks = ref.shape[0] // count
    return ref[pl.ds(block, count, stride=blocks), :]


def load_chunk(ref, count, first, blocks):
    return jnp.concatenate([load_rows(ref, count, first + g) for g in range(blocks)], axis=1)


def load_row(ref, first, blocks):
    return jnp.concatenate([ref[pl.ds(first + g, 1), :] for g in range(blocks)], axis=1)


def fill_join(join, obs_ref, act_ref, first):
    blocks = join.shape[1] // LANES
    join[0:OBS, :] = load_chunk(obs_ref, OBS, first, blocks)
    if act_ref is not None:
        join[OBS : OBS + ACT, :] = load_chunk(act_ref, ACT, first, blocks)
    join[JOIN - 1 : JOIN, :] = jnp.ones((1, join.shape[1]), F32)


def with_action(join, action):
    row = lax.broadcasted_iota(jnp.int32, action.shape, 0)
    inside = (row >= 1) & (row <= ACT)
    return jnp.concatenate([join[:16], jnp.where(inside, action, join[16:])], axis=0)


def fill_first(ref, row, weight_ref, bias_row, index):
    rows = weight_ref.shape[0]
    ref[row : row + rows, :] = weight_ref[:, index, :]
    ref[row + JOIN - 1 : row + JOIN, :] = bias_row


def store_split(ref, index, value):
    high, low = split(value)
    ref[index, 0] = high
    ref[index, 1] = low


def pair(ref, index):
    return ref[index, 0], ref[index, 1]


def columns(rows):
    turned = jnp.transpose(rows)
    return [jnp.broadcast_to(turned[:, k : k + 1], (HID, LANES)) for k in range(rows.shape[0])]


def back_weights(weight, scale):
    both = jnp.concatenate([scale, scale], axis=1)
    return jnp.transpose(0.25 * both * weight)


def head_bias(bias_ref):
    row = lax.broadcasted_iota(jnp.int32, (HEAD, LANES), 0)
    out = jnp.zeros((HEAD, LANES), F32)
    for k in range(ACT):
        out = jnp.where(row == 1 + k, bias_ref[0, k], out)
        out = jnp.where(row == 9 + k, bias_ref[0, ACT + k], out)
    return out


def fold(value):
    total = value[:, :LANES]
    for g in range(1, value.shape[1] // LANES):
        total = total + value[:, g * LANES : (g + 1) * LANES]
    return total


def valid_lanes(first, count, width):
    lane = lax.broadcasted_iota(jnp.int32, (1, width), 1)
    return lane + first * LANES < count


def spread_row(value):
    return jnp.broadcast_to(value, (1, LANES))


def critic_kernel(peers, *refs):
    sources, refs = refs[:SOURCES], refs[SOURCES:]
    (send, small), refs = refs[:2], refs[2:]
    places, refs = refs[:SOURCES], refs[SOURCES:]
    one, two, back, head, bias_two, last, wide_bias, join = refs[:8]
    acc_two, acc_one, acc_side, acc_table, acc_row, turn, arrived = refs[8:]
    copies = [
        pltpu.make_async_copy(source, place, arrived.at[k])
        for k, (source, place) in enumerate(zip(sources, places))
    ]
    for copy in copies:
        copy.start()
    count_ref, temper_ref, actor_b3, critic_b3, target_b3 = places[:5]
    actor_w1, actor_b1, actor_b2, actor_w3 = places[5:9]
    critic_w1, critic_b1, critic_b2, critic_w3 = places[9:13]
    target_w1, target_b1, target_b2, target_w3 = places[13:17]
    actor_w2, target_w2, critic_w2 = places[17:20]
    states, actions, rewards, next_states, dones, noise_next, probs, owners, slots = places[20:]
    acc_two[...] = jnp.zeros_like(acc_two)
    acc_one[...] = jnp.zeros_like(acc_one)
    acc_side[...] = jnp.zeros_like(acc_side)
    acc_table[...] = jnp.zeros_like(acc_table)
    acc_row[...] = jnp.zeros_like(acc_row)
    small[...] = jnp.zeros_like(small)
    for copy in copies[:17]:
        copy.wait()
    count = count_ref[0, 0]
    alpha = jnp.exp(temper_ref[0, 0])
    share = HID // peers
    blocks = CRITIC_BLOCKS
    width = blocks * LANES
    depth = acc_table.shape[0] // peers
    fill_first(small, 0, actor_w1, actor_b1[...], 0)
    for k in range(2):
        fill_first(small, (1 + k) * JOIN, critic_w1, critic_b1[k : k + 1, :], k)
        fill_first(turn, k * JOIN, target_w1, target_b1[k : k + 1, :], k)
    small[HEAD_ROW + 1 : HEAD_ROW + 1 + ACT, :] = actor_w3[0:ACT, 0, :]
    small[HEAD_ROW + 9 : HEAD_ROW + 9 + ACT, :] = actor_w3[ACT : 2 * ACT, 0, :]
    small[REST_ROW : REST_ROW + 1, :] = 0.5 * actor_b2[...]
    small[REST_ROW + 1 : REST_ROW + 3, :] = 0.5 * critic_b2[...]
    small[REST_ROW + 3 : REST_ROW + 5, :] = critic_w3[...]
    turn[2 * JOIN : 2 * JOIN + 2, :] = 0.5 * target_b2[...]
    turn[2 * JOIN + 2 : 2 * JOIN + 4, :] = target_w3[...]
    turn[2 * JOIN + 4 : 2 * JOIN + 8, :] = jnp.zeros((4, HID), F32)
    wide_bias[...] = head_bias(actor_b3)
    small[BIAS_ROW : BIAS_ROW + HEAD, 0:LANES] = wide_bias[...]
    for k in range(2):
        small[BIAS_ROW + k : BIAS_ROW + k + 1, LANES:] = jnp.full((1, LANES), critic_b3[0, k])
    store_split(head, 0, small[HEAD_ROW : HEAD_ROW + HEAD, :])
    one[0] = stack_weight(0.5 * small[0:JOIN, :])
    given = columns(small[REST_ROW : REST_ROW + 8, :])
    aims = columns(turn[2 * JOIN : 2 * JOIN + 8, :])
    bias_two[0] = given[0]
    for k in range(2):
        one[1 + k] = stack_weight(0.5 * turn[k * JOIN : (k + 1) * JOIN, :])
        one[3 + k] = stack_weight(0.5 * small[(1 + k) * JOIN : (2 + k) * JOIN, :])
        bias_two[1 + k] = aims[k]
        bias_two[3 + k] = given[1 + k]
        last[k] = aims[2 + k]
        last[2 + k] = given[3 + k]
    for copy in copies[17:20]:
        copy.wait()
    store_split(two, 0, 0.5 * actor_w2[...])
    for k in range(2):
        store_split(two, 1 + k, 0.5 * target_w2[k])
        store_split(two, 3 + k, 0.5 * critic_w2[k])
        store_split(back, k, back_weights(critic_w2[k], last[2 + k]))
    for copy in copies[20:]:
        copy.wait()

    def next_action(first, known, lane):
        yield "mxu", 64
        fill_join(join.at[lane], next_states, None, first)
        join[lane, OBS : OBS + ACT, :] = jnp.zeros((ACT, width), F32)
        nexts = join[lane]
        half = dot(one[0], stack_join(nexts))
        yield "vpu", 110
        hidden = split(activate(half))
        yield "mxu", 192
        half = dot3(pair(two, 0), hidden)
        yield "vpu", 130
        hidden = split(activate(half + wide(bias_two[0], blocks)))
        yield "mxu", 128
        out = dot3_joint(pair(head, 0), hidden)
        yield "vpu", 100
        join[lane, OBS : OBS + ACT, :] = load_chunk(noise_next, ACT, first, blocks)
        action, known["logp"], _, _ = squash(out + wide(wide_bias[...], blocks), join[lane, 16:24, :])
        known["given_next"] = stack_join(with_action(nexts, action))

    def target_value(first, known, k):
        yield None, "given_next"
        yield "mxu", 64
        half = dot(one[1 + k], known["given_next"])
        yield "vpu", 110
        hidden = split(activate(half))
        yield "mxu", 192
        half = dot3(pair(two, 1 + k), hidden)
        yield "vpu", 120
        hidden = activate(half + wide(bias_two[1 + k], blocks))
        total = jnp.sum(hidden * wide(last[k], blocks), axis=0, keepdims=True)
        known["next", k] = total + target_b3[0, k]

    def target_row(first, known):
        yield None, "logp"
        yield None, ("next", 0)
        yield None, ("next", 1)
        yield "vpu", 40
        keep = GAMMA * (1.0 - load_row(dones, first, blocks).astype(F32))
        worth = soft_min(known["next", 0], known["next", 1]) - alpha * known["logp"]
        known["target"] = load_row(rewards, first, blocks) + keep * worth
        known["valid"] = valid_lanes(first, count, width)
        coef = jnp.exp(-BETA * jnp.log(load_row(probs, first, blocks)))
        known["coef"] = jnp.where(known["valid"], coef, 0.0)

    def given_now(first, known, lane):
        yield "vpu", 20
        fill_join(join.at[lane], states, actions, first)
        known["given"] = stack_join(join[lane])

    def critic(first, known, k):
        yield None, "given"
        given = known["given"]
        yield "mxu", 64
        half = dot(one[3 + k], given)
        yield "vpu", 160
        hidden, slope_one = activate_slope(half)
        hidden_one = split(hidden)
        yield "mxu", 192
        half = dot3(pair(two, 3 + k), hidden_one)
        yield "vpu", 170
        hidden, slope_two = activate_slope(half + wide(bias_two[3 + k], blocks))
        value = jnp.sum(hidden * wide(last[2 + k], blocks), axis=0, keepdims=True) + critic_b3[0, k]
        yield None, "target"
        yield "vpu", 160
        error = value - known["target"]
        known["error", k] = error
        scaled = known["coef"] * error
        grad = scaled * slope_two
        acc_side[k] += fold(grad)
        acc_side[2 + k] += fold(scaled * hidden)
        acc_row[k : k + 1, :] += scaled
        grad_two = split(grad)
        yield "mxu", 192
        half = dot3(pair(back, k), grad_two)
        yield "vpu", 90
        grad_one = split(half * slope_one)
        yield "mxu", 192
        acc_two[k] += dot3_t(grad_two, hidden_one)
        yield "mxu", 128
        acc_one[k] += dot_t(given[:48], grad_one[0]) + dot_t(given[:48], grad_one[1])

    def priorities(first, known):
        yield None, ("error", 0)
        yield None, ("error", 1)
        yield "vpu", 120
        delta = 0.5 * (known["error", 0] + known["error", 1])
        priority = jnp.exp(PRIO_EXP * jnp.log(jnp.abs(delta) + PRIO_EPS))
        priority = jnp.where(known["valid"], priority, 0.0)
        acc_row[2:3, :] = jnp.maximum(acc_row[2:3, :], priority)
        slot = load_row(slots, first, blocks)
        place = load_row(owners, first, blocks) * depth + lax.shift_right_logical(slot, 7)
        lane = slot & (LANES - 1)
        rows = acc_table.shape[0]
        row_hit = lax.broadcasted_iota(jnp.int32, (rows, width), 0) == place
        lane_hit = lax.broadcasted_iota(jnp.int32, (LANES, width), 0) == lane
        high, low = split_wide(priority)
        picked = jnp.concatenate(
            [jnp.where(lane_hit, high, 0.0), jnp.where(lane_hit, low, 0.0)], axis=0
        ).astype(BF16)
        hits = jnp.where(row_hit, 1.0, 0.0).astype(BF16)
        yield "mxu", 64
        acc_table[...] += dot_t(hits, picked)

    def step(index, carry):
        tasks = []
        for lane in range(CRITIC_STREAMS):
            first = (index * CRITIC_STREAMS + lane) * blocks
            known = {"begin": CRITIC_LAG * (2 * lane // CRITIC_STREAMS)}
            tasks.append((next_action(first, known, 2 * lane), known))
            tasks.append((given_now(first, known, 2 * lane + 1), known))
            for k in range(2):
                tasks.append((critic(first, known, k), known))
            for k in range(2):
                tasks.append((target_value(first, known, k), known))
            tasks.append((target_row(first, known), known))
            tasks.append((priorities(first, known), known))
        interleave(tasks)
        return carry

    span = CRITIC_STREAMS * width
    lax.fori_loop(0, (count + span - 1) // span, step, 0)

    for k in range(2):
        acc_side[k] = 0.5 * last[2 + k] * acc_side[k]
    side = [jnp.sum(acc_side[k], axis=1, keepdims=True) for k in range(4)]
    small = [jnp.transpose(acc_one[k][:JOIN] + acc_one[k][JOIN:]) for k in range(2)]
    joined = jnp.concatenate(small + side + [jnp.zeros((HID, LANES - 52), F32)], axis=1)
    acc_side[0] = joined
    lane = lax.broadcasted_iota(jnp.int32, probs.shape, 1)
    row = lax.broadcasted_iota(jnp.int32, probs.shape, 0)
    least = jnp.min(jnp.where(row * LANES + lane < count, probs[...], 1.0), keepdims=True)
    best = jnp.max(acc_row[2:3, :], keepdims=True)
    sums = jnp.concatenate(
        [
            jnp.full((1, LANES), count.astype(F32)),
            spread_row(least),
            spread_row(jnp.sum(acc_row[0:1, :], keepdims=True)),
            spread_row(jnp.sum(acc_row[1:2, :], keepdims=True)),
            spread_row(best),
            jnp.zeros((3, LANES), F32),
        ],
        axis=0,
    )
    table = acc_table[:, :LANES] + acc_table[:, LANES:]
    for p in range(peers):
        mine = slice(p * share, (p + 1) * share)
        at = 0
        for k in range(2):
            for t in range(2):
                block = acc_two[k, mine, t * LANES : (t + 1) * LANES]
                send[p, at : at + share, :] = 0.5 * last[2 + k, mine, :] * block
                at += share
        send[p, at : at + share, :] = acc_side[0, mine, :]
        at += share
        send[p, at : at + depth, :] = table[p * depth : (p + 1) * depth]
        at += depth
        send[p, at : at + 8, :] = sums


def halvings(peers):
    bits = list(range(1, (peers - 1).bit_length()))
    turn = len(bits) // 2
    return bits, bits[turn:] + bits[:turn]


def actor_kernel(
    peers,
    core_ref,
    count_ref,
    temper_ref,
    states,
    noise_now,
    small,
    actor_w2,
    critic_w2,
    keep,
    give,
    one,
    two,
    back,
    head_back,
    entry,
    bias_two,
    last,
    wide_bias,
    join,
    acc_two,
    acc_one,
    acc_head,
    acc_side,
    acc_out,
    acc_row,
    actor_first,
    actor_second,
    actor_head,
):
    count = jnp.max(count_ref[...].astype(F32)).astype(jnp.int32)
    alpha = jnp.exp(temper_ref[...])
    share = HID // peers
    blocks = ACTOR_BLOCKS
    width = blocks * LANES
    given = columns(small[REST_ROW : REST_ROW + 8, :])
    final = small[HEAD_ROW : HEAD_ROW + HEAD, :]
    store_three(actor_second, 0.5 * actor_w2[...])
    store_split(back, 0, jnp.transpose(0.5 * actor_w2[...]))
    bias_two[0] = given[0]
    actor_first[...] = stack_weight_three(0.5 * small[0:JOIN, :])
    for k in range(2):
        first = (1 + k) * JOIN
        one[1 + k] = stack_weight(0.5 * small[first : first + JOIN, :])
        store_split(entry, k, small[first + 8 : first + 24, :])
        store_split(two, 1 + k, 0.5 * critic_w2[k])
        bias_two[1 + k] = given[1 + k]
        last[k] = given[3 + k]
        store_split(back, 1 + k, back_weights(critic_w2[k], last[k]))
    store_three(actor_head, final)
    head_back[...] = stack_weight(0.5 * final)
    wide_bias[...] = small[BIAS_ROW : BIAS_ROW + HEAD, 0:LANES]
    critic_b3 = [small[BIAS_ROW + k : BIAS_ROW + k + 1, LANES : LANES + 1] for k in range(2)]
    acc_two[...] = jnp.zeros_like(acc_two)
    acc_one[...] = jnp.zeros_like(acc_one)
    acc_head[...] = jnp.zeros_like(acc_head)
    acc_side[...] = jnp.zeros_like(acc_side)
    acc_out[...] = jnp.zeros_like(acc_out)
    acc_row[...] = jnp.zeros_like(acc_row)

    row = lax.broadcasted_iota(jnp.int32, (8, width), 0)
    inside = (row >= 1) & (row <= ACT)

    def forward(first, known, lane):
        yield "mxu", 64
        valid = valid_lanes(first, count, width)
        known["mask"] = jnp.where(valid, 1.0, 0.0)
        fill_join(join.at[lane], states, noise_now, first)
        noise = join[lane, 16:24, :]
        tail = jnp.where(inside, 0.0, noise)
        given = stack_join_three(jnp.concatenate([join[lane, 0:16, :], tail], axis=0))
        half = dot(actor_first[...], given)
        yield "vpu", 160
        hidden, slope_one = activate_slope(half)
        hidden_one = split_rest(hidden)
        yield "mxu", 384
        half = dot6(actor_second[...], hidden_one)
        yield "vpu", 170
        hidden, slope_two = activate_slope(half + wide(bias_two[0], blocks))
        hidden_two = split_rest(hidden)
        yield "mxu", 192
        out = dot6(actor_head[...], hidden_two)
        yield "vpu", 100
        action, logp, spread, bend = squash(out + wide(wide_bias[...], blocks), noise)
        acc_row[0:1, :] += known["mask"] * (logp + ENTROPY_AIM)
        known["fresh"] = stack_join(with_action(join[lane], action))
        yield None, "push"
        yield "vpu", 60
        push = known["push"]
        pull = alpha * known["mask"]
        grad_pre = jnp.where(inside, 2.0 * pull * action + push * (1.0 - action * action), 0.0)
        grad_std = jnp.where(inside, grad_pre * spread - pull, 0.0)
        grad_bend = 0.5 * (STD_HI - STD_LO) * grad_std * (1.0 - bend * bend)
        grad_out = jnp.concatenate([grad_pre, grad_bend], axis=0)
        acc_out[...] += fold(grad_out)
        outs = stack_join(grad_out)
        yield "mxu", 64
        half = dot(head_back[...], outs)
        yield "vpu", 100
        grad = half * slope_two
        acc_side[...] += fold(grad)
        grad_two = split(grad)
        yield "mxu", 192
        half = dot3_joint(pair(back, 0), grad_two)
        yield "vpu", 90
        grad_one = split(half * slope_one)
        yield "mxu", 128
        acc_head[...] += sum_parts(dot_t(jnp.concatenate(hidden_two[:2], axis=0), outs[:32]))
        yield "mxu", 192
        acc_two[...] += dot3_t(grad_two, hidden_one)
        yield "mxu", 128
        acc_one[...] += sum_parts(dot_t(jnp.concatenate(grad_one, axis=0), given[:48]))

    def critic(first, known, k):
        yield None, "fresh"
        yield "mxu", 64
        half = dot(one[1 + k], known["fresh"])
        yield "vpu", 160
        hidden, slope_one = activate_slope(half)
        hidden_one = split(hidden)
        yield "mxu", 192
        half = dot3_joint(pair(two, 1 + k), hidden_one)
        yield "vpu", 220
        hidden, slope_two = activate_slope(half + wide(bias_two[1 + k], blocks))
        value = jnp.sum(hidden * wide(last[k], blocks), axis=0, keepdims=True) + critic_b3[k]
        known["value", k] = value
        grad_two = split(slope_two)
        yield "mxu", 192
        half = dot3_joint(pair(back, 1 + k), grad_two)
        yield "vpu", 90
        grad_one = split(half * slope_one)
        yield "mxu", 128
        known["pull", k] = dot3_joint(pair(entry, k), grad_one)[8:]

    def mix(first, known):
        for k in range(2):
            yield None, ("value", k)
            yield None, ("pull", k)
        yield "vpu", 10
        gap = (known["value", 1] - known["value", 0]) / SOFT_TEMP
        lean = 0.5 * jnp.tanh(0.5 * gap)
        parts = (0.5 + lean) * known["pull", 0] + (0.5 - lean) * known["pull", 1]
        known["push"] = -known["mask"] * parts

    def step(index, carry):
        tasks = []
        for lane in range(ACTOR_STREAMS):
            first = (index * ACTOR_STREAMS + lane) * blocks
            known = {"begin": 0}
            tasks.append((forward(first, known, lane), known))
            for k in range(2):
                tasks.append((critic(first, known, k), known))
            tasks.append((mix(first, known), known))
        interleave(tasks)
        return carry

    span = ACTOR_STREAMS * width
    lax.fori_loop(0, (count + span - 1) // span, step, 0)

    acc_out[...] = jnp.broadcast_to(jnp.sum(acc_out[...], axis=1, keepdims=True), (HEAD, LANES))
    joined = jnp.concatenate(
        [
            acc_one[:, :JOIN] + acc_one[:, JOIN:],
            acc_head[:, :HEAD] + acc_head[:, HEAD:],
            jnp.sum(acc_side[...], axis=1, keepdims=True),
            jnp.broadcast_to(-jnp.sum(acc_row[0:1, :], keepdims=True), (HID, 1)),
            jnp.zeros((HID, OUT_LANE - JOIN - HEAD - 2), F32),
            jnp.broadcast_to(jnp.transpose(acc_out[...])[0:1, :], (HID, HEAD)),
            jnp.zeros((HID, LANES - OUT_LANE - HEAD), F32),
        ],
        axis=1,
    )
    acc_side[...] = joined
    core = core_ref[0]
    orders = halvings(peers)
    for side, part in ((keep, core), (give, 1 - core)):
        for q in range(peers // 2):
            chips = [sum(((q >> j) & 1) << (bit - 1) for j, bit in enumerate(order)) for order in orders]
            chip = chips[0] + part * (chips[1] - chips[0])
            mine = pl.ds(pl.multiple_of((2 * chip + part) * share, 8), share)
            side[q, 0:share, :] = acc_two[mine, 0:LANES]
            side[q, share : 2 * share, :] = acc_two[mine, LANES : 2 * LANES]
            side[q, 2 * share : 3 * share, :] = acc_side[mine, :]


def finish_kernel(critic_in, old, *refs):
    actor_in, best_in, outs = refs[:2], refs[2:4], refs[4:]
    a_one, a_bias_one, a_two, a_bias_two, a_three, a_bias_three = outs[:6]
    c_one, c_bias_one, c_two, c_bias_two, c_three, c_bias_three, g_alpha, new, best = outs[6:]
    peers = critic_in.shape[0]
    share = HID // peers
    depth = old.shape[0]

    def actor_total(start, size):
        value = actor_in[0][start : start + size, :]
        for ref in actor_in[1:]:
            value = value + ref[start : start + size, :]
        return value

    def total(ref, start, size):
        value = ref[0, start : start + size, :]
        for p in range(1, peers):
            value = value + ref[p, start : start + size, :]
        return value

    at = 5 * share
    table = total(critic_in, at, depth)
    new[...] = jnp.where(table > 0.0, table, old[...])
    at += depth
    sums = total(critic_in, at, 8)
    least = critic_in[0, at + 1 : at + 2, :]
    for p in range(1, peers):
        least = jnp.minimum(least, critic_in[p, at + 1 : at + 2, :])
    actor_scale = 1.0 / sums[0:1, :]
    critic_scale = actor_scale * jnp.exp(BETA * jnp.log(least))
    for k in range(2):
        for t in range(2):
            c_two[k, :, t * LANES : (t + 1) * LANES] = critic_scale * total(
                critic_in, (2 * k + t) * share, share
            )
    small = jnp.transpose(critic_scale * total(critic_in, 4 * share, share))
    for k in range(2):
        for j in range(JOIN - 1):
            c_one[j, k : k + 1, :] = small[k * JOIN + j : k * JOIN + j + 1, :]
        c_bias_one[k : k + 1, :] = small[k * JOIN + JOIN - 1 : k * JOIN + JOIN, :]
        c_bias_two[k : k + 1, :] = small[48 + k : 49 + k, :]
        c_three[k : k + 1, :] = small[50 + k : 51 + k, :]
    lane = lax.broadcasted_iota(jnp.int32, (1, LANES), 1)
    both = jnp.where(lane == 0, sums[2:3, :], sums[3:4, :])
    c_bias_three[...] = (critic_scale * both)[:, 0:2]
    for t in range(2):
        a_two[:, t * LANES : (t + 1) * LANES] = actor_scale * actor_total(t * share, share)
    flat = actor_scale * actor_total(2 * share, share)
    small = jnp.transpose(flat)
    for j in range(OBS):
        a_one[j] = small[j : j + 1, :]
    a_bias_one[...] = small[JOIN - 1 : JOIN, :]
    for j in range(ACT):
        a_three[j] = small[JOIN + 1 + j : JOIN + 2 + j, :]
        a_three[ACT + j] = small[JOIN + 9 + j : JOIN + 10 + j, :]
    a_bias_two[...] = small[JOIN + HEAD : JOIN + HEAD + 1, :]
    g_alpha[...] = flat[0:1, JOIN + HEAD + 1 : JOIN + HEAD + 2]
    a_bias_three[:, 0:ACT] = flat[0:1, OUT_LANE + 1 : OUT_LANE + 1 + ACT]
    a_bias_three[:, ACT : 2 * ACT] = flat[0:1, OUT_LANE + 9 : OUT_LANE + 9 + ACT]
    largest = best_in[0][...]
    for ref in best_in[1:]:
        largest = jnp.maximum(largest, ref[...])
    best[...] = largest[:, 0:1]


SMEM = pl.BlockSpec(memory_space=pltpu.SMEM)
HBM = pl.BlockSpec(memory_space=pltpu.HBM)
VMEM = pl.BlockSpec(memory_space=pltpu.VMEM)


def shards(
    states,
    actions,
    rewards,
    next_states,
    dones,
    noise_now,
    noise_next,
    probs,
    valid_counts,
    owners,
    slots,
    old_priorities,
    actor_w1,
    actor_b1,
    actor_w2,
    actor_b2,
    actor_w3,
    actor_b3,
    critic_w1,
    critic_b1,
    critic_w2,
    critic_b2,
    critic_w3,
    critic_b3,
    target_w1,
    target_b1,
    target_w2,
    target_b2,
    target_w3,
    target_b3,
    log_alpha,
):
    peers = lax.axis_size("dp")
    me = lax.axis_index("dp")
    share = HID // peers

    def rows(value):
        return value.reshape(-1, LANES)

    states, actions, next_states = rows(states), rows(actions), rows(next_states)
    noise_now, noise_next = rows(noise_now), rows(noise_next)
    rewards, dones, probs = rows(rewards), rows(dones), rows(probs)
    owners, slots, old = rows(owners), rows(slots), rows(old_priorities)
    depth = old.shape[0]
    actor_one = jnp.transpose(actor_w1, (2, 0, 1))
    actor_three = jnp.transpose(actor_w3, (1, 0, 2))
    critic_one = jnp.transpose(critic_w1[0], (2, 0, 1))
    target_one = jnp.transpose(target_w1[0], (2, 0, 1))
    critic_rows = 5 * share + depth + 8
    actor_rows = 3 * share
    sources = (
        valid_counts,
        log_alpha.reshape(1, 1),
        actor_b3,
        critic_b3,
        target_b3,
        actor_one,
        actor_b1,
        actor_b2,
        actor_three,
        critic_one,
        critic_b1[0],
        critic_b2[0],
        critic_w3[0],
        target_one,
        target_b1[0],
        target_b2[0],
        target_w3[0],
        actor_w2[0],
        target_w2[0],
        critic_w2[0],
        states,
        actions,
        rewards,
        next_states,
        dones,
        noise_next,
        probs,
        owners,
        slots,
    )
    critic_send, small = pl.pallas_call(
        functools.partial(critic_kernel, peers),
        out_shape=(
            jax.ShapeDtypeStruct((peers, critic_rows, LANES), F32),
            jax.ShapeDtypeStruct((SMALL, HID), F32),
        ),
        in_specs=[HBM] * SOURCES,
        out_specs=(VMEM, VMEM),
        scratch_shapes=[
            (pltpu.SMEM if k < 5 else pltpu.VMEM)(source.shape, source.dtype)
            for k, source in enumerate(sources)
        ]
        + [
            pltpu.VMEM((5, HID, 3 * JOIN), BF16),
            pltpu.VMEM((5, 2, HID, HID), BF16),
            pltpu.VMEM((2, 2, HID, HID), BF16),
            pltpu.VMEM((1, 2, HEAD, HID), BF16),
            pltpu.VMEM((5, HID, LANES), F32),
            pltpu.VMEM((4, HID, LANES), F32),
            pltpu.VMEM((HEAD, LANES), F32),
            pltpu.VMEM((2 * CRITIC_STREAMS, JOIN, CRITIC_BLOCKS * LANES), F32),
            pltpu.VMEM((2, HID, HID), F32),
            pltpu.VMEM((2, 2 * JOIN, HID), F32),
            pltpu.VMEM((4, HID, LANES), F32),
            pltpu.VMEM((peers * depth, 2 * LANES), F32),
            pltpu.VMEM((8, CRITIC_BLOCKS * LANES), F32),
            pltpu.VMEM((2 * JOIN + 8, HID), F32),
            pltpu.SemaphoreType.DMA((SOURCES,)),
        ],
        compiler_params=pltpu.CompilerParams(vmem_limit_bytes=CRITIC_LIMIT),
        cost_estimate=pl.CostEstimate(flops=20 * 10**9, bytes_accessed=4 * 10**6, transcendentals=10**7),
        name="critic",
    )(*sources)
    critic_in = lax.all_to_all(critic_send, "dp", split_axis=0, concat_axis=0, tiled=True)
    kept, given = pl.pallas_call(
        functools.partial(actor_kernel, peers),
        out_shape=(jax.ShapeDtypeStruct((peers // 2, actor_rows, LANES), F32),) * 2,
        in_specs=[SMEM] + [VMEM] * 7,
        out_specs=(VMEM, VMEM),
        scratch_shapes=[
            pltpu.VMEM((3, HID, 3 * JOIN), BF16),
            pltpu.VMEM((3, 2, HID, HID), BF16),
            pltpu.VMEM((3, 2, HID, HID), BF16),
            pltpu.VMEM((HID, 3 * HEAD), BF16),
            pltpu.VMEM((2, 2, 16, HID), BF16),
            pltpu.VMEM((3, HID, LANES), F32),
            pltpu.VMEM((2, HID, LANES), F32),
            pltpu.VMEM((HEAD, LANES), F32),
            pltpu.VMEM((ACTOR_STREAMS, JOIN, ACTOR_BLOCKS * LANES), F32),
            pltpu.VMEM((HID, HID), F32),
            pltpu.VMEM((HID, 2 * JOIN), F32),
            pltpu.VMEM((HID, 2 * HEAD), F32),
            pltpu.VMEM((HID, LANES), F32),
            pltpu.VMEM((HEAD, LANES), F32),
            pltpu.VMEM((8, ACTOR_BLOCKS * LANES), F32),
            pltpu.VMEM((HID, 6 * JOIN), BF16),
            pltpu.VMEM((3 * HID, HID), BF16),
            pltpu.VMEM((3 * HEAD, HID), BF16),
        ],
        compiler_params=pltpu.CompilerParams(vmem_limit_bytes=ACTOR_LIMIT),
        cost_estimate=pl.CostEstimate(flops=20 * 10**9, bytes_accessed=4 * 10**6, transcendentals=10**7),
        name="actor",
    )(
        (me % 2).reshape(1),
        valid_counts,
        log_alpha.reshape(1, 1),
        states,
        noise_now,
        small,
        actor_w2[0],
        critic_w2[0],
    )
    at = 5 * share + depth + 4
    best = jnp.max(critic_in[:, at : at + 1, :], axis=0)
    best_in = best
    agents = lax.axis_size("seed")
    spans = (agents - 1).bit_length()
    orders = halvings(peers)
    actor_in = lax.ppermute(given, "dp", [(k, k ^ 1) for k in range(peers)])
    for step in range(max(len(orders[0]), spans)):
        if step < len(orders[0]):
            both = (kept + actor_in).reshape(-1, 2, actor_rows, LANES)
            first, second = orders[0][step], orders[1][step]
            mine = jnp.where(me % 2 == 0, me >> first, me >> second) & 1
            kept = lax.dynamic_index_in_dim(both, mine, 1, False)
            given = lax.dynamic_index_in_dim(both, 1 - mine, 1, False)
            pairs = [(k, k ^ (1 << (second if k % 2 else first))) for k in range(peers)]
            actor_in = lax.ppermute(given, "dp", pairs)
        if step < spans:
            best = jnp.maximum(best, best_in)
            far = 1 << (spans - 1 - step)
            best_in = lax.ppermute(best, "seed", [(k, k ^ far) for k in range(agents)])
        actor_in, best_in = lax.optimization_barrier((actor_in, best_in))
    actor_parts, bests = (kept[0], actor_in[0]), (best, best_in)
    shape = jax.ShapeDtypeStruct
    outs = pl.pallas_call(
        finish_kernel,
        out_shape=(
            shape((OBS, 1, share), F32),
            shape((1, share), F32),
            shape((share, HID), F32),
            shape((1, share), F32),
            shape((2 * ACT, 1, share), F32),
            shape((1, 2 * ACT), F32),
            shape((JOIN - 1, 2, share), F32),
            shape((2, share), F32),
            shape((2, share, HID), F32),
            shape((2, share), F32),
            shape((2, share), F32),
            shape((1, 2), F32),
            shape((1, 1), F32),
            shape((depth, LANES), F32),
            shape((1, 1), F32),
        ),
        in_specs=[VMEM] * 6,
        out_specs=(VMEM,) * 15,
        compiler_params=pltpu.CompilerParams(vmem_limit_bytes=FINISH_LIMIT),
        name="finish",
    )(critic_in, old, *actor_parts, *bests)
    return (
        jnp.transpose(outs[0], (1, 2, 0)),
        outs[1],
        outs[2][None],
        outs[3],
        jnp.transpose(outs[4], (1, 0, 2)),
        outs[5],
        jnp.transpose(outs[6], (1, 2, 0))[None],
        outs[7][None],
        outs[8][None],
        outs[9][None],
        outs[10][None],
        outs[11],
        outs[12].reshape(1),
        outs[13].reshape(1, -1),
        outs[14].reshape(()),
    )


def solution(mesh):
    token = P("seed", None, "dp")
    line = P("seed", "dp")
    agent = P("seed")
    placed = (
        (token, token, line, token, line, token, token, line, line, line, line, line)
        + (agent,) * 19
    )
    return jax.shard_map(
        shards,
        mesh=mesh,
        in_specs=placed,
        out_specs=(
            P("seed", "dp", None),
            P("seed", "dp"),
            P("seed", "dp", None),
            P("seed", "dp"),
            P("seed", None, "dp"),
            P("seed", None),
            P("seed", None, "dp", None),
            P("seed", None, "dp"),
            P("seed", None, "dp", None),
            P("seed", None, "dp"),
            P("seed", None, "dp"),
            P("seed", None),
            P("seed"),
            P("seed", "dp"),
            P(),
        ),
        check_vma=False,
    )
```
